256 devices in a mesh: fsdp: 16 (over y, z_lo), expert: 16 (over z_hi, x, core).
Axes of the slice: x: 4, y: 4, z: 8 (z_hi: 2, z_lo: 4; z = z_hi * 4 + z_lo), core: 2. Of those that a mesh axis runs over, the one named last changes fastest.
Arguments:
- tokens: bfloat16 [16, 2048, 2048], P('fsdp', 'expert'), may hold values from -6 to 6
- doc_ids: int32 [16, 2048], P('fsdp'), may hold values from 0 to 7, never falling along the last dimension, each value on 1 to 512 neighbouring positions
- route_ids: int32 [16, 2048, 10], P('fsdp', 'expert'), may hold values from 0 to 15, all different within a row; in each aligned block of 128 rows (0 to 127, 128 to 255, ..., all dimensions but the last counted through in order) at most 88 rows name the same one
- norm_gain: bfloat16 [2048], replicated, may hold values from 0.25 to 1.75
- proj_weight: bfloat16 [2048, 16, 512], P('fsdp', 'expert'), may hold values from -0.125 to 0.125
- gating_weight: bfloat16 [2048, 2, 16], P('fsdp', None, 'expert'), may hold values from -0.125 to 0.125
- block_scale: bfloat16 [16, 16, 4], P('fsdp', 'expert'), may hold values from 0.5 to 2
- conv_weight: bfloat16 [16, 4, 384], P('expert'), may hold values from -3 to 3
- decay_rate: float32 [16], P('expert'), may hold values from 0.005 to 0.1
- head_gain: bfloat16 [128], replicated, may hold values from 0.25 to 1.75
- out_weight: bfloat16 [16, 128, 2048], P('expert', None, 'fsdp'), may hold values from -0.125 to 0.125
- moe_gain: bfloat16 [2048], replicated, may hold values from 0.25 to 1.75
- router_weight: bfloat16 [2048, 16], replicated, may hold values from -0.125 to 0.125
- expert_in: bfloat16 [16, 2048, 1024], P('expert'), may hold values from -0.125 to 0.125
- expert_out: bfloat16 [16, 512, 2048], P('expert'), may hold values from -0.25 to 0.25
Outputs:
- mixed_out: bfloat16 [16, 2048, 2048], P('fsdp', 'expert')
The draws below stay inside these ranges and needn't reach their ends.
Inputs may be any that keep to these rules, and one draw needn't show every extreme that they name: `route_ids`: each token names 10 different experts. Among the 128 tokens of one device (aligned blocks of 128 token rows in order) no expert is named by more than 88 tokens, and in every draw some expert is named by exactly 88. `doc_ids`: along each sequence the ids never fall; a document spans 1 to 512 positions and one spans exactly 512.
All inputs are finite; a program needn't handle non-finite values.
Results may differ from the reference program's by a relative error of at most 0.015.
Values may be sent and summed in bfloat16 or wider, within the bound.
A program may use at most 128 MiB of HBM per device.

```python
import math
import jax
import jax.numpy as jnp
import numpy as np
from jax import lax

D = 2048
FF = 512
HD = 128
QB = 128
KW = 4
TOK_DEV = 128
EXPERTS = 16
TOP = 10
HEADS = 16
SEQ = 2048
BATCH = 16
CAP = 88
N_EXPERT = 16


def levels(key, dims, shards, smallest, high):
    factor_of = 1.0
    for position, parts in shards:
        steps = jax.random.uniform(jax.random.fold_in(jax.random.fold_in(key, 6), position), (parts,), jnp.float32, smallest / len(shards), high / len(shards))
        factor_of = factor_of * jnp.repeat(jnp.exp(steps), dims[position] // parts).reshape((-1,) + (1,) * (len(dims) - 1 - position))
    return factor_of


def profile(number_of, total, reach, lean):
    weights = [(1 << 20) // math.isqrt(rank ** lean) + 1 for rank in range(2, number_of + 1)]
    surplus, counts = total - reach - (number_of - 1), [1] * (number_of - 1)
    while surplus > 0:
        candidates = [i for i in range(number_of - 1) if counts[i] < reach]
        pool, budget = sum([weights[i] for i in candidates]), surplus
        for i in candidates:
            addition = min(reach - counts[i], max(1, budget * weights[i] // pool), surplus)
            counts[i] = counts[i] + addition
            surplus = surplus - addition
    return np.array([reach] + counts)


def ragged(key, count, total, limit, lean):
    if count == 2:
        one = jax.random.randint(key, (), max(1, total - limit), min(limit, total - 1) + 1)
        return jnp.stack([one, total - one])
    lengths = jnp.asarray(profile(count, total, limit, lean), jnp.int32)
    couples = (count - 1) // 2
    giver, sink = lengths[1:1 + 2 * couples:2], lengths[2:2 + 2 * couples:2]
    slack = jnp.minimum(giver - 1, limit - sink)
    moved = jax.random.randint(jax.random.fold_in(key, 1), (couples,), 0, 1 << 20) % (slack + 1)
    lengths = lengths.at[1:1 + 2 * couples:2].set(giver - moved).at[2:2 + 2 * couples:2].set(sink + moved)
    return lengths[jax.random.permutation(jax.random.fold_in(key, 2), count)]


def deal_out(key, own, number, rows, count, top, reach, lean):
    order = jax.random.permutation(key, count)
    heavy_load, common = portions_of(count, rows * top, reach, lean, True), portions_of(count, rows * top, reach, lean, False)
    places = jnp.arange(count)

    def named(lengths, turn):
        used = int((lengths > 0).sum())
        fixed = max(1, used // 4)
        passed = fixed + (places - fixed + turn * (used - fixed)) % max(1, count - fixed)
        return jnp.zeros((count,), jnp.int32).at[order[jnp.where(places < fixed, places, passed)]].set(jnp.asarray(lengths, jnp.int32))

    lengths = jnp.where(number % 4 == 0, named(heavy_load, number // 4), named(common, number - number // 4 - 1))
    mixed = jax.random.permutation(jax.random.fold_in(own, 3), count)
    source_of, receiver = mixed[0:count // 2 * 2:2], mixed[1:count // 2 * 2:2]
    margin = jnp.minimum(lengths[source_of] - 1, reach - lengths[receiver]) // 2
    margin = jnp.where((source_of == order[0]) | (receiver == order[0]) | (lengths[receiver] == 0), 0, jnp.maximum(margin, 0))
    passed = jax.random.randint(jax.random.fold_in(own, 4), (count // 2,), 0, 1 << 20) % (margin + 1)
    lengths = lengths.at[source_of].add(-passed).at[receiver].add(passed)
    members = jnp.searchsorted(jnp.cumsum(lengths), jnp.arange(rows * top), side="right").astype(jnp.int32)
    table = members.reshape(top, rows).T
    table = table[jax.random.permutation(jax.random.fold_in(own, 1), rows)]
    turn = jax.random.randint(jax.random.fold_in(own, 2), (rows, 1), 0, top)
    return jnp.take_along_axis(table, (jnp.arange(top)[None, :] + turn) % top, axis=1)


def portions_of(number_of, total, limit, lean, full):
    loads = [(1 << 20) // math.isqrt(rank ** lean) + 1 for rank in range(1, number_of + 1)]
    largest = limit if full else min(limit, max(-(-total // number_of), total * loads[0] // sum(loads)))
    least = 1 if total - largest >= number_of - 1 else 0
    given, spare = [largest] + [least] * (number_of - 1), total - largest - least * (number_of - 1)
    while spare > 0:
        free = [i for i in range(1, number_of) if given[i] < largest] or [i for i in range(1, number_of) if given[i] < limit]
        pool, left = sum([loads[i] for i in free]), spare
        for i in free:
            more = min(limit - given[i], max(1, left * loads[i] // pool), spare)
            given[i] = given[i] + more
            spare = spare - more
    return np.array(given)


def noise(stream_key, shape, width, reach, shards=(), held_as=jnp.bfloat16):
    entries = width * jax.random.normal(stream_key, shape, jnp.float32)
    if shards:
        entries = entries * levels(stream_key, shape, shards, -0.22, 0.18)
    return jnp.clip(entries, -reach, reach).astype(held_as)


def setup_inputs(seed: int = 0) -> dict:
    key_of = jax.random.split(jax.random.key(seed), 16)
    tokens = noise(key_of[0], (BATCH, SEQ, D), 1.0, 6.0, ((0, 16), (1, 16)))
    doc_ids = jax.vmap(lambda own: jnp.searchsorted(jnp.cumsum(ragged(own, 8, SEQ, SEQ // 4, 1)), jnp.arange(SEQ), side="right"))(jax.random.split(key_of[1], BATCH)).reshape((BATCH, SEQ)).astype(jnp.int32)
    route_ids_keys = jax.random.split(jax.random.fold_in(key_of[2], 1), BATCH * SEQ // TOK_DEV)
    route_ids_turns = jax.random.permutation(jax.random.fold_in(key_of[2], 3), BATCH * SEQ // TOK_DEV)
    route_ids = jax.vmap(lambda own, number: deal_out(jax.random.fold_in(key_of[2], 2), own, number, TOK_DEV, EXPERTS, TOP, CAP, 1))(route_ids_keys, route_ids_turns).reshape((BATCH, SEQ, TOP))
    norm_gain = jnp.clip(1.0 + 0.15 * jax.random.normal(key_of[3], (D,), jnp.float32), 0.25, 1.75).astype(jnp.bfloat16)
    proj_weight = noise(key_of[4], (D, HEADS, 4 * HD), D ** -0.5, 0.125, ((0, 16), (1, 16)))
    gating_weight = noise(key_of[5], (D, 2, HEADS), D ** -0.5, 0.125, ((0, 16), (2, 16)))
    block_scale = jnp.clip(jnp.exp(math.log(2.0) - 1.3862944 * jax.random.uniform(key_of[6], (D // QB, HEADS, 4), jnp.float32) ** levels(key_of[6], (D // QB, HEADS, 4), ((0, 16), (1, 16)), -0.2, 0.2)), 0.5, 2.0).astype(jnp.bfloat16)
    conv_weight = noise(key_of[7], (HEADS, KW, 3 * HD), KW ** -0.5, 3.0, ((0, 16),))
    decay_rate = jnp.clip(jnp.exp(math.log(0.1) - 2.9957323 * jax.random.uniform(key_of[8], (HEADS,), jnp.float32) ** levels(key_of[8], (HEADS,), ((0, 16),), -0.2, 0.2)), 0.005, 0.1)
    head_gain = jnp.clip(1.0 + 0.15 * jax.random.normal(key_of[9], (HD,), jnp.float32), 0.25, 1.75).astype(jnp.bfloat16)
    out_weight = noise(key_of[10], (HEADS, HD, D), (HEADS * HD) ** -0.5, 0.125, ((0, 16), (2, 16)))
    moe_gain = jnp.clip(1.0 + 0.15 * jax.random.normal(key_of[11], (D,), jnp.float32), 0.25, 1.75).astype(jnp.bfloat16)
    router_weight = noise(key_of[12], (D, EXPERTS), D ** -0.5, 0.125)
    expert_in = noise(key_of[13], (EXPERTS, D, 2 * FF), D ** -0.5, 0.125, ((0, 16),))
    expert_out = noise(key_of[14], (EXPERTS, FF, D), FF ** -0.5, 0.25, ((0, 16),))
    return dict(tokens=tokens, doc_ids=doc_ids, route_ids=route_ids, norm_gain=norm_gain, proj_weight=proj_weight, gating_weight=gating_weight, block_scale=block_scale, conv_weight=conv_weight, decay_rate=decay_rate, head_gain=head_gain, out_weight=out_weight, moe_gain=moe_gain, router_weight=router_weight, expert_in=expert_in, expert_out=expert_out)


def rms_scale(values, gain):
    mean_square = lax.optimization_barrier(jnp.mean(values * values, axis=-1, keepdims=True))
    return values * lax.rsqrt(mean_square + 1e-06) * gain.astype(jnp.float32)

def short_conv(channels, conv_weight, seq_docs):
    tap_count = conv_weight.shape[1]
    summed = channels * conv_weight[:, 0, :].astype(jnp.float32)
    for shift_by in range(1, tap_count):
        moved = jnp.concatenate([jnp.zeros((shift_by,) + channels.shape[1:], jnp.float32), channels[:-shift_by]], 0)
        moved_docs = jnp.concatenate([jnp.full((shift_by,), -1, jnp.int32), seq_docs[:-shift_by].astype(jnp.int32)], 0)
        keep_mask = (moved_docs == seq_docs.astype(jnp.int32)).astype(jnp.float32)[:, None, None]
        summed = summed + moved * keep_mask * conv_weight[:, shift_by, :].astype(jnp.float32)
    return jax.nn.silu(summed)

def prepare(projected, gate_inputs, seq_docs, conv_weight, decay_rate):
    seq_len, head_count = (projected.shape[0], projected.shape[1])
    widened = projected.astype(jnp.float32)
    mixed_in = widened[:, :, 0:3, :].reshape(seq_len, head_count, 3 * HD)
    activated = short_conv(mixed_in, conv_weight, seq_docs)
    queries = activated[..., :HD]
    key_vecs = activated[..., HD:2 * HD]
    value_vecs = activated[..., 2 * HD:]
    queries = queries * lax.rsqrt(lax.optimization_barrier(jnp.sum(queries * queries, axis=-1, keepdims=True)) + 1e-06) * HD ** (-0.5)
    key_vecs = key_vecs * lax.rsqrt(lax.optimization_barrier(jnp.sum(key_vecs * key_vecs, axis=-1, keepdims=True)) + 1e-06)
    beta_vals = jax.nn.sigmoid(gate_inputs[:, 0, :])
    log_gate = -decay_rate[None, :] * jax.nn.softplus(gate_inputs[:, 1, :])
    return (queries, key_vecs, value_vecs, beta_vals, log_gate, widened[:, :, 3, :])

def gated_output(recurrent, gate_branch, head_gain):
    return (rms_scale(recurrent, head_gain) * jax.nn.silu(gate_branch)).astype(jnp.bfloat16)

def recurrence(queries, key_vecs, value_vecs, beta_vals, gamma_vals):
    highest_precision = lax.Precision.HIGHEST
    head_count = queries.shape[1]

    def advance(recurrent_memory, inputs):
        query_inputs, key_inputs, value_in, beta_in, gamma_in = inputs
        decayed_state = gamma_in[:, None, None] * recurrent_memory
        initial_estimate = jnp.einsum('ypj,yp->yj', decayed_state, key_inputs, precision=highest_precision)
        recurrent_memory = decayed_state + beta_in[:, None, None] * key_inputs[:, :, None] * (value_in - initial_estimate)[:, None, :]
        return (recurrent_memory, jnp.einsum('ypj,yp->yj', recurrent_memory, query_inputs, precision=highest_precision))
    initial = jnp.zeros((head_count, HD, HD), jnp.float32)
    _, outputs = lax.scan(advance, initial, (queries, key_vecs, value_vecs, beta_vals, gamma_vals))
    return outputs

def mixer(seq_tokens, seq_docs, norm_gain, proj_weight, gating_weight, block_scale, conv_weight, decay_rate, head_gain, out_weight):
    seq_len = seq_tokens.shape[0]
    residual = seq_tokens.astype(jnp.float32)
    normed = rms_scale(residual, norm_gain).astype(jnp.bfloat16)
    flat_weight = proj_weight.reshape(D, HEADS * 4 * HD)
    total_proj = jnp.zeros((seq_len, HEADS, 4, HD), jnp.float32)
    for block_num in range(D // QB):
        rows_in = normed[:, block_num * QB:(block_num + 1) * QB]
        block_part = jnp.dot(rows_in, flat_weight[block_num * QB:(block_num + 1) * QB], preferred_element_type=jnp.float32)
        block_part = block_part.reshape(seq_len, HEADS, 4, HD) * block_scale[block_num].astype(jnp.float32)[None, :, :, None]
        total_proj = total_proj + block_part
    projected = total_proj.astype(jnp.bfloat16)
    gate_inputs = jnp.dot(normed, gating_weight.reshape(D, 2 * HEADS), preferred_element_type=jnp.float32).reshape(seq_len, 2, HEADS)
    queries, key_vecs, value_vecs, beta_vals, log_gate, gate_branch = prepare(projected, gate_inputs, seq_docs, conv_weight, decay_rate)
    same_doc = jnp.concatenate([jnp.zeros((1,), jnp.float32), (seq_docs[1:] == seq_docs[:-1]).astype(jnp.float32)], 0)
    gamma_vals = jnp.exp(log_gate) * same_doc[:, None]
    recurrent = recurrence(queries, key_vecs, value_vecs, beta_vals, gamma_vals)
    head_out = gated_output(recurrent, gate_branch, head_gain)
    attn_out = jnp.zeros((seq_len, D), jnp.float32)
    for head_num in range(HEADS):
        head_term = jnp.dot(head_out[:, head_num, :], out_weight[head_num], preferred_element_type=jnp.float32)
        head_term = lax.optimization_barrier(head_term.astype(jnp.bfloat16)).astype(jnp.float32)
        attn_out = attn_out + head_term
    return residual + attn_out

def reference(tokens, doc_ids, route_ids, norm_gain, proj_weight, gating_weight, block_scale, conv_weight, decay_rate, head_gain, out_weight, moe_gain, router_weight, expert_in, expert_out):

    def one_sequence(paired):
        return mixer(paired[0], paired[1], norm_gain, proj_weight, gating_weight, block_scale, conv_weight, decay_rate, head_gain, out_weight)
    residual = lax.map(one_sequence, (tokens, doc_ids))
    token_total = BATCH * SEQ
    flat_resid = residual.reshape(token_total, D)
    moe_in = rms_scale(flat_resid, moe_gain).astype(jnp.bfloat16)
    logits = jnp.dot(moe_in, router_weight, preferred_element_type=jnp.float32)
    route_flat = route_ids.reshape(token_total, TOP).astype(jnp.int32)
    chosen = jnp.take_along_axis(logits, route_flat, axis=1)
    raised = jnp.exp(chosen)
    route_weight = raised / lax.optimization_barrier(jnp.sum(raised, axis=1, keepdims=True))
    expert_flat = route_flat.reshape(-1)
    onehot_selection = (expert_flat[:, None] == jnp.arange(EXPERTS, dtype=jnp.int32)[None, :]).astype(jnp.int32)
    ranks = lax.optimization_barrier(jnp.sum(jnp.cumsum(onehot_selection, axis=0) * onehot_selection, axis=1)) - 1
    row_cap = BATCH * N_EXPERT * CAP
    slot_ids = (expert_flat * row_cap + ranks).astype(jnp.int32)
    owner_token = jnp.repeat(jnp.arange(token_total, dtype=jnp.int32), TOP)
    row_table = jnp.full((EXPERTS * row_cap,), token_total, jnp.int32).at[slot_ids].set(owner_token).reshape(EXPERTS, row_cap)
    weight_table = jnp.zeros((EXPERTS * row_cap,), jnp.float32).at[slot_ids].set(route_weight.reshape(-1)).reshape(EXPERTS, row_cap)
    padded = jnp.concatenate([moe_in, jnp.zeros((1, D), jnp.bfloat16)], 0)

    def one_expert(combined, inputs):
        table_row, weight_entries, gate_up_weight, down_weight = inputs
        picked_rows = padded[table_row]
        gate_up = jnp.dot(picked_rows, gate_up_weight, preferred_element_type=jnp.float32)
        hidden = (jax.nn.silu(gate_up[:, :FF]) * gate_up[:, FF:]).astype(jnp.bfloat16)
        result = jnp.dot(hidden, down_weight, preferred_element_type=jnp.float32).astype(jnp.bfloat16)
        result = lax.optimization_barrier(result).astype(jnp.float32)
        return (combined.at[table_row].add(weight_entries[:, None] * result), None)
    combined, _ = lax.scan(one_expert, jnp.zeros((token_total + 1, D), jnp.float32), (row_table, weight_table, expert_in, expert_out))
    return (flat_resid + combined[:token_total]).astype(jnp.bfloat16).reshape(BATCH, SEQ, D)
```

```python
import functools

import jax
import jax.numpy as jnp
from jax import lax
from jax.experimental import pallas as pl
from jax.experimental.pallas import tpu as pltpu
from jax.sharding import PartitionSpec as P

D = 2048
FF = 512
EXPERTS = 16

HD = 128
C = 128
PASSES = 3
f32 = jnp.float32
bf16 = jnp.bfloat16

def split(a):
    hi = a.astype(bf16)
    return hi, (a - hi.astype(f32)).astype(bf16)

def dg(a, b, dims):
    return lax.dot_general(a, b, (dims, ((), ())), preferred_element_type=f32)

NN = ((1,), (0,))
NT = ((1,), (1,))
TN = ((0,), (0,))

def mm(a, b, dims=NN, passes=3):
    if passes == 1:
        return dg(a.astype(bf16), b.astype(bf16), dims)
    ah, al = split(a); bh, bl = split(b)
    return dg(ah, bh, dims) + (dg(al, bh, dims) + dg(ah, bl, dims))

def prep_chunk(c, qkv_ref, gates_ref, docs_ref, win_ref, docc_ref, convw, rate):
    r0 = pl.multiple_of(c * C, C)
    docw = docc_ref[pl.ds(r0, C + 8), :]
    doc_col = docw[8:, :]
    parts = []
    for g in range(3):
        w = win_ref[pl.ds(r0, C + 8), g * HD:(g + 1) * HD]
        acc = w[8:, :] * convw[0:1, g * HD:(g + 1) * HD]
        for j in range(1, 4):
            keep = docw[8 - j:C + 8 - j, :] == doc_col
            acc = acc + jnp.where(keep, w[8 - j:C + 8 - j, :] * convw[j:j + 1, g * HD:(g + 1) * HD], 0.0)
        parts.append(acc * jax.nn.sigmoid(acc))
    q, k, v = parts
    q = q * (lax.rsqrt(jnp.sum(q * q, axis=1, keepdims=True) + 1e-6) * HD ** -0.5)
    k = k * lax.rsqrt(jnp.sum(k * k, axis=1, keepdims=True) + 1e-6)
    gates = gates_ref[pl.ds(r0, C), :]
    beta = jnp.broadcast_to(jax.nn.sigmoid(gates[:, 0:1]), (C, HD))
    d = gates[:, 1:2]
    sp = jnp.maximum(d, 0.0) + jnp.log1p(jnp.exp(-jnp.abs(d)))
    lg = jnp.broadcast_to(-rate * sp, (C, HD))
    row = lax.broadcasted_iota(jnp.int32, (C, C), 0)
    col = lax.broadcasted_iota(jnp.int32, (C, C), 1)
    low = (row >= col)
    tri = low.astype(bf16)
    h0 = lg.astype(bf16); r1 = lg - h0.astype(f32); h1 = r1.astype(bf16); h2 = (r1 - h1.astype(f32)).astype(bf16)
    cum = dg(tri, h0, NN) + (dg(tri, h1, NN) + dg(tri, h2, NN))
    doc_row = docs_ref[pl.ds(c, 1), :]
    keep = jnp.logical_and(low, doc_col == doc_row)
    gap = cum - cum.T
    decay = jnp.where(keep, jnp.exp(jnp.where(keep, gap, 0.0)), 0.0)
    prev = docw[7:8, :]
    start = jnp.where(doc_col == prev, jnp.exp(cum), 0.0)
    kk = mm(k, k, NT, PASSES)
    qk = mm(q, k, NT, PASSES) * decay
    L = jnp.where(row > col, beta * kk * decay, 0.0)
    eye = (row == col).astype(f32)
    T = eye - jnp.where((row >> 1) == (col >> 1), L, 0.0)
    s = 2
    while s < C:
        sh = s.bit_length() - 1
        m = jnp.logical_and((row >> (sh + 1)) == (col >> (sh + 1)), (row >> sh) != (col >> sh))
        Lm = jnp.where(m, L, 0.0)
        T = T - mm(T, mm(Lm, T, NN, PASSES), NN, PASSES)
        s *= 2
    rhs = jnp.concatenate([beta * v, beta * start * k], axis=1)
    UW = mm(T, rhs, NN, PASSES)
    kend = k * decay.T[:, C - 1:C]
    gend = start[C - 1:C, :]
    PUW = mm(qk, UW, NN, PASSES)
    KUW = mm(kend, UW, TN, PASSES)
    N = KUW[:, :HD]
    M = eye * gend - KUW[:, HD:]
    PU = PUW[:, :HD]
    Qp = start * q - PUW[:, HD:]
    return M, N, Qp, PU

def body(proj_ref, gates_ref, docs_ref, convw_ref, rate_ref, gain_ref, out_ref, win_ref, docc_ref, m_ref, n_ref, *, unroll):
    T_ = proj_ref.shape[0]
    nc = T_ // C
    win_ref[0:8, :] = jnp.zeros((8, 3 * HD), f32)
    docc_ref[0:8, :] = jnp.full((8, HD), -1.0, f32)
    convw = convw_ref[...]
    rate = rate_ref[0]
    def stage(c, _):
        r0 = pl.multiple_of(c * C, C)
        win_ref[pl.ds(pl.multiple_of(r0 + 8, 8), C), :] = proj_ref[pl.ds(r0, C), :3 * HD].astype(f32)
        docc_ref[pl.ds(pl.multiple_of(r0 + 8, 8), C), :] = jnp.broadcast_to(docs_ref[pl.ds(c, 1), :], (C, C)).T
        return 0
    lax.fori_loop(0, nc, stage, 0)
    def first(i, _):
        for u in range(unroll):
            c = i * unroll + u
            M, N, Qp, PU = prep_chunk(c, proj_ref, gates_ref, docs_ref, win_ref, docc_ref, convw, rate)
            m_ref[c, :C, :] = Qp
            m_ref[c, C:, :] = M
            n_ref[c, :C, :] = PU
            n_ref[c, C:, :] = N
        return 0
    lax.fori_loop(0, nc // unroll, first, 0)
    gain = gain_ref[...].astype(f32)
    def second(c, S):
        r0 = pl.multiple_of(c * C, C)
        both = mm(m_ref[c], S, NN, PASSES) + n_ref[c]
        o = both[:C, :]
        ms = jnp.mean(o * o, axis=1, keepdims=True)
        g = proj_ref[pl.ds(r0, C), 3 * HD:4 * HD].astype(f32)
        out_ref[pl.ds(r0, C), :] = (o * lax.rsqrt(ms + 1e-6) * gain * (g * jax.nn.sigmoid(g))).astype(bf16)
        return both[C:, :]
    lax.fori_loop(0, nc, second, jnp.zeros((HD, HD), f32))

def mixer_kernel(proj, gates, docs, convw, rate, gain, unroll=4):
    T_ = proj.shape[0]
    V = pl.BlockSpec(memory_space=pltpu.VMEM)
    return pl.pallas_call(
        functools.partial(body, unroll=unroll),
        out_shape=jax.ShapeDtypeStruct((T_, HD), bf16),
        in_specs=[V, V, V, V, pl.BlockSpec(memory_space=pltpu.SMEM), V],
        out_specs=V,
        scratch_shapes=[pltpu.VMEM((T_ + 8, 3 * HD), f32), pltpu.VMEM((T_ + 8, HD), f32),
                        pltpu.VMEM((T_ // C, 2 * C, HD), f32), pltpu.VMEM((T_ // C, 2 * C, HD), f32)],
        compiler_params=pltpu.CompilerParams(vmem_limit_bytes=48 * 1024 * 1024),
        name="delta_mixer",
    )(proj, gates, docs, convw, rate, gain)


def rms_scale(values, gain):
    mean_square = jnp.mean(values * values, axis=-1, keepdims=True)
    return values * lax.rsqrt(mean_square + 1e-06) * gain.astype(f32)


def on_device(tokens, doc_ids, route_ids, norm_gain, proj_weight, gating_weight, block_scale,
              conv_weight, decay_rate, head_gain, out_weight, moe_gain, router_weight,
              expert_in, expert_out):
    residual = tokens[0].astype(f32)
    normed = rms_scale(residual, norm_gain).astype(bf16)
    scale = jnp.repeat(block_scale[0, 0].astype(f32), HD)
    scaled = (proj_weight[:, 0, :].astype(f32) * scale[None, :]).astype(bf16)
    packed = jnp.concatenate([scaled, jnp.pad(gating_weight[:, :, 0], ((0, 0), (0, HD - 2)))], 1)
    sequence = lax.all_gather(normed, "expert", axis=0, tiled=True)
    weights = lax.all_gather(packed, "fsdp", axis=0, tiled=True)
    projected = jnp.dot(sequence, weights, preferred_element_type=f32)
    head_out = mixer_kernel(
        projected[:, :4 * HD].astype(bf16), projected[:, 4 * HD:],
        doc_ids[0].astype(f32).reshape(-1, C), conv_weight[0].astype(f32), decay_rate,
        head_gain.reshape(1, HD))
    out_full = lax.all_gather(lax.all_gather(out_weight[0], "fsdp", axis=1, tiled=True),
                              "expert", axis=0, tiled=True)
    tok = residual.shape[0]
    mine = lax.all_to_all(head_out.reshape(-1, tok, HD), "expert", split_axis=0, concat_axis=0, tiled=True)
    mine = jnp.swapaxes(mine, 0, 1).reshape(tok, D)
    mid = residual + jnp.dot(mine, out_full, preferred_element_type=f32)
    moe_in = rms_scale(mid, moe_gain).astype(bf16)
    logits = jnp.dot(moe_in, router_weight, preferred_element_type=f32)
    picked = (route_ids[0][:, :, None] == jnp.arange(EXPERTS, dtype=jnp.int32)).any(axis=1)
    raised = jnp.where(picked, jnp.exp(logits), 0.0)
    route_weight = raised / jnp.sum(raised, axis=1, keepdims=True)
    high = route_weight.astype(bf16)
    rest = (route_weight - high.astype(f32)).astype(bf16)
    sent = jnp.concatenate([moe_in, high, rest, jnp.zeros((tok, HD - 2 * EXPERTS), bf16)], 1)
    got = lax.all_gather(sent, "expert", axis=0, tiled=True)
    me = lax.axis_index("expert")
    lane = jnp.arange(HD)
    side = got[:, D:].astype(f32)
    weight = jnp.sum(jnp.where((lane == me) | (lane == me + EXPERTS), side, 0.0), axis=1, keepdims=True)
    gate_up = jnp.dot(got[:, :D], expert_in[0], preferred_element_type=f32)
    hidden = (jax.nn.silu(gate_up[:, :FF]) * gate_up[:, FF:]).astype(bf16)
    rows = (jnp.dot(hidden, expert_out[0], preferred_element_type=f32) * weight).astype(bf16)
    mixed = lax.psum_scatter(rows, "expert", scatter_dimension=0, tiled=True)
    return (mid + mixed.astype(f32)).astype(bf16)[None]


def solution(mesh):
    placed = (
        P("fsdp", "expert", None),
        P("fsdp", None),
        P("fsdp", "expert", None),
        P(),
        P("fsdp", "expert", None),
        P("fsdp", None, "expert"),
        P("fsdp", "expert", None),
        P("expert", None, None),
        P("expert"),
        P(),
        P("expert", None, "fsdp"),
        P(),
        P(),
        P("expert", None, None),
        P("expert", None, None),
    )
    return jax.shard_map(
        on_device, mesh=mesh, in_specs=placed, out_specs=P("fsdp", "expert", None), check_vma=False
    )
```

```python
import functools

import jax
import jax.numpy as jnp
from jax import lax
from jax.experimental import pallas as pl
from jax.experimental.pallas import tpu as pltpu
from jax.sharding import PartitionSpec as P

D = 2048
FF = 512
EXPERTS = 16
MESH = pl.DeviceIdType.MESH

HD = 128
C = 128
PASSES = 3
f32 = jnp.float32
bf16 = jnp.bfloat16

def split(a):
    hi = a.astype(bf16)
    return hi, (a - hi.astype(f32)).astype(bf16)

def dg(a, b, dims):
    return lax.dot_general(a, b, (dims, ((), ())), preferred_element_type=f32)

NN = ((1,), (0,))
NT = ((1,), (1,))
TN = ((0,), (0,))

def mm(a, b, dims=NN, passes=3):
    if passes == 1:
        return dg(a.astype(bf16), b.astype(bf16), dims)
    ah, al = split(a); bh, bl = split(b)
    return dg(ah, bh, dims) + (dg(al, bh, dims) + dg(ah, bl, dims))

def prep_chunk(c, qkv_ref, gates_ref, docs_ref, win_ref, docc_ref, convw, rate):
    r0 = pl.multiple_of(c * C, C)
    docw = docc_ref[pl.ds(r0, C + 8), :]
    doc_col = docw[8:, :]
    parts = []
    for g in range(3):
        w = win_ref[pl.ds(r0, C + 8), g * HD:(g + 1) * HD]
        acc = w[8:, :] * convw[0:1, g * HD:(g + 1) * HD]
        for j in range(1, 4):
            keep = docw[8 - j:C + 8 - j, :] == doc_col
            acc = acc + jnp.where(keep, w[8 - j:C + 8 - j, :] * convw[j:j + 1, g * HD:(g + 1) * HD], 0.0)
        parts.append(acc * jax.nn.sigmoid(acc))
    q, k, v = parts
    q = q * (lax.rsqrt(jnp.sum(q * q, axis=1, keepdims=True) + 1e-6) * HD ** -0.5)
    k = k * lax.rsqrt(jnp.sum(k * k, axis=1, keepdims=True) + 1e-6)
    gates = gates_ref[pl.ds(r0, C), :]
    beta = jnp.broadcast_to(jax.nn.sigmoid(gates[:, 0:1]), (C, HD))
    d = gates[:, 1:2]
    sp = jnp.maximum(d, 0.0) + jnp.log1p(jnp.exp(-jnp.abs(d)))
    lg = jnp.broadcast_to(-rate * sp, (C, HD))
    row = lax.broadcasted_iota(jnp.int32, (C, C), 0)
    col = lax.broadcasted_iota(jnp.int32, (C, C), 1)
    low = (row >= col)
    tri = low.astype(bf16)
    h0 = lg.astype(bf16); r1 = lg - h0.astype(f32); h1 = r1.astype(bf16); h2 = (r1 - h1.astype(f32)).astype(bf16)
    cum = dg(tri, h0, NN) + (dg(tri, h1, NN) + dg(tri, h2, NN))
    doc_row = docs_ref[pl.ds(c, 1), :]
    keep = jnp.logical_and(low, doc_col == doc_row)
    gap = cum - cum.T
    decay = jnp.where(keep, jnp.exp(jnp.where(keep, gap, 0.0)), 0.0)
    prev = docw[7:8, :]
    start = jnp.where(doc_col == prev, jnp.exp(cum), 0.0)
    kk = mm(k, k, NT, PASSES)
    qk = mm(q, k, NT, PASSES) * decay
    L = jnp.where(row > col, beta * kk * decay, 0.0)
    eye = (row == col).astype(f32)
    T = eye - jnp.where((row >> 1) == (col >> 1), L, 0.0)
    s = 2
    while s < C:
        sh = s.bit_length() - 1
        m = jnp.logical_and((row >> (sh + 1)) == (col >> (sh + 1)), (row >> sh) != (col >> sh))
        Lm = jnp.where(m, L, 0.0)
        T = T - mm(T, mm(Lm, T, NN, PASSES), NN, PASSES)
        s *= 2
    rhs = jnp.concatenate([beta * v, beta * start * k], axis=1)
    UW = mm(T, rhs, NN, PASSES)
    kend = k * decay.T[:, C - 1:C]
    gend = start[C - 1:C, :]
    PUW = mm(qk, UW, NN, PASSES)
    KUW = mm(kend, UW, TN, PASSES)
    N = KUW[:, :HD]
    M = eye * gend - KUW[:, HD:]
    PU = PUW[:, :HD]
    Qp = start * q - PUW[:, HD:]
    return M, N, Qp, PU

def body(proj_ref, gates_ref, docs_ref, convw_ref, rate_ref, gain_ref, out_ref, win_ref, docc_ref, m_ref, n_ref, *, unroll):
    T_ = proj_ref.shape[0]
    nc = T_ // C
    win_ref[0:8, :] = jnp.zeros((8, 3 * HD), f32)
    docc_ref[0:8, :] = jnp.full((8, HD), -1.0, f32)
    convw = convw_ref[...]
    rate = rate_ref[0]
    def stage(c, _):
        r0 = pl.multiple_of(c * C, C)
        win_ref[pl.ds(pl.multiple_of(r0 + 8, 8), C), :] = proj_ref[pl.ds(r0, C), :3 * HD].astype(f32)
        docc_ref[pl.ds(pl.multiple_of(r0 + 8, 8), C), :] = jnp.broadcast_to(docs_ref[pl.ds(c, 1), :], (C, C)).T
        return 0
    lax.fori_loop(0, nc, stage, 0)
    def first(i, _):
        for u in range(unroll):
            c = i * unroll + u
            M, N, Qp, PU = prep_chunk(c, proj_ref, gates_ref, docs_ref, win_ref, docc_ref, convw, rate)
            m_ref[c, :C, :] = Qp
            m_ref[c, C:, :] = M
            n_ref[c, :C, :] = PU
            n_ref[c, C:, :] = N
        return 0
    lax.fori_loop(0, nc // unroll, first, 0)
    gain = gain_ref[...].astype(f32)
    def second(c, S):
        r0 = pl.multiple_of(c * C, C)
        both = mm(m_ref[c], S, NN, PASSES) + n_ref[c]
        o = both[:C, :]
        ms = jnp.mean(o * o, axis=1, keepdims=True)
        g = proj_ref[pl.ds(r0, C), 3 * HD:4 * HD].astype(f32)
        out_ref[pl.ds(r0, C), :] = (o * lax.rsqrt(ms + 1e-6) * gain * (g * jax.nn.sigmoid(g))).astype(bf16)
        return both[C:, :]
    lax.fori_loop(0, nc, second, jnp.zeros((HD, HD), f32))

def mixer_kernel(proj, gates, docs, convw, rate, gain, unroll=4):
    T_ = proj.shape[0]
    V = pl.BlockSpec(memory_space=pltpu.VMEM)
    return pl.pallas_call(
        functools.partial(body, unroll=unroll),
        out_shape=jax.ShapeDtypeStruct((T_, HD), bf16),
        in_specs=[V, V, V, V, pl.BlockSpec(memory_space=pltpu.SMEM), V],
        out_specs=V,
        scratch_shapes=[pltpu.VMEM((T_ + 8, 3 * HD), f32), pltpu.VMEM((T_ + 8, HD), f32),
                        pltpu.VMEM((T_ // C, 2 * C, HD), f32), pltpu.VMEM((T_ // C, 2 * C, HD), f32)],
        compiler_params=pltpu.CompilerParams(vmem_limit_bytes=48 * 1024 * 1024),
        name="delta_mixer",
    )(proj, gates, docs, convw, rate, gain)


def rms_scale(values, gain):
    mean_square = jnp.mean(values * values, axis=-1, keepdims=True)
    return values * lax.rsqrt(mean_square + 1e-06) * gain.astype(f32)


class Place:
    def __init__(self):
        e = lax.axis_index("expert")
        self.e = e
        self.z, self.x, self.c = e // 8, (e // 2) % 4, e % 2

    def at(self, zz, dx, cc=0):
        return ((self.z + zz) % 2 * 4 + (self.x + dx) % 4) * 2 + (self.c + cc) % 2

    def pair(self, zz, dx):
        return ((self.z + zz) % 2 * 4 + (self.x + dx) % 4) * 2

    def neighbours(self):
        return [{"expert": self.at(*r)} for r in ((0, 1), (0, 3), (1, 0), (0, 0, 1))]


def greet(peers):
    barrier = pltpu.get_barrier_semaphore()
    for peer in peers:
        pl.semaphore_signal(barrier, inc=1, device_id=peer, device_id_type=MESH)
    pl.semaphore_wait(barrier, len(peers))


class Copies:
    def __init__(self, send, recv):
        self.send, self.recv, self.sent = send, recv, []

    def make(self, i, src, dst, peer):
        return pltpu.make_async_remote_copy(
            src_ref=src, dst_ref=dst, send_sem=self.send.at[i], recv_sem=self.recv.at[i],
            device_id=peer, device_id_type=MESH)

    def go(self, i, src, dst, peer):
        copy = self.make(i, src, dst, peer)
        copy.start()
        self.sent.append(copy)

    def arrive(self, i, dst, peer):
        self.make(i, dst, dst, peer).wait_recv()

    def finish(self):
        for copy in self.sent:
            copy.wait_send()


GATHER_COPIES = 30


class Gather:
    def __init__(self, full, copies, place, base=0):
        self.full, self.copies, self.place, self.base = full, copies, place, base
        self.half = full.shape[1] // 2

    def ref(self, zz, dx, h, cc=0):
        return self.full.at[self.place.at(zz, dx, cc), pl.ds(h * self.half, self.half)]

    def peer(self, *r):
        return {"expert": self.place.at(*r)}

    def go(self, n, zz, dx, h, to):
        block = self.ref(zz, dx, h)
        self.copies.go(self.base + n, block, block, self.peer(*to))

    def swap(self, zz, dx, h):
        self.go(14 + (zz * 4 + dx) * 2 + h, zz, dx, h, (0, 0, 1))

    def take(self, n, zz, dx, h):
        self.copies.arrive(self.base + n, self.ref(zz, dx, h), self.peer(0, 1))
        self.swap(zz, dx, h)

    def swapped(self, zz, dx):
        for h in range(2):
            self.copies.arrive(self.base + 14 + (zz * 4 + dx) * 2 + h, self.ref(zz, dx, h, 1), self.peer(0, 0, 1))

    def plus(self, zz, h):
        self.go(2 + zz * 2 + h, zz, 0, h, (0, 1))

    def minus(self, zz, h):
        self.go(6 + zz * 2 + h, zz, 0, h, (0, 3))

    def begin(self):
        for h in range(2):
            self.go(h, 0, 0, h, (1, 0))
            self.plus(0, h)
            self.minus(0, 1 - h)
        self.swap(0, 0, 0)
        self.swap(0, 0, 1)

    def from_x(self, zz):
        self.take(2 + zz * 2, zz, 3, 0)
        self.go(10 + zz, zz, 3, 0, (0, 1))
        self.take(6 + zz * 2 + 1, zz, 1, 1)
        self.go(12 + zz, zz, 1, 1, (0, 3))
        self.take(2 + zz * 2 + 1, zz, 3, 1)
        self.take(6 + zz * 2, zz, 1, 0)

    def from_z(self, h):
        self.take(h, 1, 0, h)
        self.plus(1, h)
        self.minus(1, h)

    def from_far(self, zz):
        self.take(10 + zz, zz, 2, 0)
        self.take(12 + zz, zz, 2, 1)


def project_kernel(tok_ref, gain_ref, pack_ref, proj_ref, gate_ref, full, w, send, recv, *, wide):
    place = Place()
    fsdp = lax.axis_index("fsdp")
    y, zl = fsdp // 4, fsdp % 4
    tok = tok_ref.shape[0]
    rows = pack_ref.shape[0]

    def line(dy, d):
        return (y + dy) % 4 * 4 + (zl + d) % 4

    full[place.e] = rms_scale(tok_ref[...].astype(f32), gain_ref[...]).astype(bf16)
    w[fsdp] = pack_ref[...]
    greet(place.neighbours() + [{"fsdp": line(*r)} for r in ((1, 0), (3, 0), (0, 1), (0, 2), (0, 3))])
    copies = Copies(send, recv)
    gather = Gather(full, copies, place)
    base = GATHER_COPIES
    half = rows // 2

    def shard(dy, d, h=None):
        slot = w.at[line(dy, (4 - d) % 4)]
        return slot if h is None else slot.at[pl.ds(h * half, half)]

    def send_shard(n, ref, peer):
        copies.go(base + n, ref, ref, {"fsdp": peer})

    def both(d):
        send_shard(3 + d, shard(0, d), line(1, 0))
        send_shard(7 + d, shard(0, d), line(3, 0))

    def along_z(d):
        copies.arrive(base + d - 1, shard(0, d), {"fsdp": line(0, d)})
        both(d)

    def along_y(d):
        copies.arrive(base + 3 + d, shard(3, d), {"fsdp": line(3, 0)})
        send_shard(11 + d, shard(3, d, 0), line(1, 0))
        copies.arrive(base + 7 + d, shard(1, d), {"fsdp": line(1, 0)})
        send_shard(15 + d, shard(1, d, 1), line(3, 0))

    def far_y(d):
        copies.arrive(base + 11 + d, shard(2, d, 0), {"fsdp": line(3, 0)})
        copies.arrive(base + 15 + d, shard(2, d, 1), {"fsdp": line(1, 0)})

    def project(zz, dx):
        gather.swapped(zz, dx)
        slot = place.pair(zz, dx)
        x = full[pl.ds(slot, 2)].reshape(2 * tok, full.shape[2])
        at = pl.ds(pl.multiple_of(slot * tok, 2 * tok), 2 * tok)
        for n in range(0, wide, 256):
            proj_ref[at, n:n + 256] = dg(x, w[:, :, n:n + 256].reshape(16 * rows, 256), NN).astype(bf16)
        gate_ref[at, :] = dg(x, w[:, :, wide:].reshape(16 * rows, HD), NN)

    for d in range(1, 4):
        send_shard(d - 1, w.at[fsdp], line(0, d))
    both(0)
    gather.begin()
    for d in range(1, 4):
        along_z(d)
    gather.from_x(0)
    along_y(0)
    gather.from_z(0)
    along_y(1)
    gather.from_z(1)
    along_y(2)
    gather.from_far(0)
    along_y(3)
    for d in range(4):
        far_y(d)
    project(0, 0)
    project(0, 3)
    gather.from_x(1)
    project(0, 1)
    project(0, 2)
    project(1, 0)
    gather.from_far(1)
    project(1, 3)
    project(1, 1)
    project(1, 2)
    copies.finish()


def project_call(tokens, gain, packed):
    tok, width = tokens.shape
    rows, cols = packed.shape
    wide = cols - HD
    V = pl.BlockSpec(memory_space=pltpu.VMEM)
    count = GATHER_COPIES + 19
    return pl.pallas_call(
        functools.partial(project_kernel, wide=wide),
        out_shape=(jax.ShapeDtypeStruct((16 * tok, wide), bf16), jax.ShapeDtypeStruct((16 * tok, HD), f32)),
        in_specs=[V] * 3,
        out_specs=(V, V),
        scratch_shapes=[pltpu.VMEM((16, tok, width), bf16), pltpu.VMEM((16, rows, cols), bf16),
                        pltpu.SemaphoreType.DMA((count,)), pltpu.SemaphoreType.DMA((count,))],
        compiler_params=pltpu.CompilerParams(collective_id=0, has_side_effects=True,
                                             vmem_limit_bytes=48 * 1024 * 1024),
        name="gather_project",
    )(tokens, gain, packed)


def add_rows(dst, sources, first, count):
    def step(i, _):
        at = pl.ds(pl.multiple_of(first + i * 16, 16), 16)
        total = dst[at, :].astype(f32)
        for source in sources:
            total = total + source[at, :].astype(f32)
        dst[at, :] = total.astype(bf16)
        return 0
    lax.fori_loop(0, count // 16, step, 0)


def expert_kernel(sent_ref, mid_ref, ein_ref, eout_ref, out_ref, full, y, kin, ap, am, bp, bm, zb,
                  win, wout, hid, send, recv, load):
    place = Place()
    tok, width = mid_ref.shape
    half = tok // 2
    ff = wout.shape[0]
    loads = [pltpu.make_async_copy(ein_ref, win, load.at[0]), pltpu.make_async_copy(eout_ref, wout, load.at[1])]
    for copy in loads:
        copy.start()
    full[place.e] = sent_ref[...]
    greet(place.neighbours())
    copies = Copies(send, recv)
    gather = Gather(full, copies, place)
    gather.begin()
    for copy in loads:
        copy.wait()
    base = GATHER_COPIES
    plus, minus = {"expert": place.at(0, 1)}, {"expert": place.at(0, 3)}
    over, twin = {"expert": place.at(1, 0)}, {"expert": place.at(0, 0, 1)}
    nf, nd = min(256, ff), min(256, width)

    def compute(zz, dx):
        gather.swapped(zz, dx)
        slot = place.pair(zz, dx)
        both = pl.ds(slot, 2)
        lane = lax.broadcasted_iota(jnp.int32, (2 * tok, HD), 1)
        side = full[both, :, width:].reshape(2 * tok, HD).astype(f32)
        hit = jnp.logical_or(lane == place.e, lane == place.e + 16)
        weight = jnp.sum(jnp.where(hit, side, 0.0), axis=1, keepdims=True)

        def inner(j, _):
            x = full[both, :, :width].reshape(2 * tok, width)
            g = dg(x, win[:, pl.ds(pl.multiple_of(j * nf, nf), nf)], NN)
            u = dg(x, win[:, pl.ds(pl.multiple_of(ff + j * nf, nf), nf)], NN)
            hid[:, pl.ds(pl.multiple_of(j * nf, nf), nf)] = (g * jax.nn.sigmoid(g) * u).astype(bf16)
            return 0
        lax.fori_loop(0, ff // nf, inner, 0)

        def outer(j, _):
            cols = pl.ds(pl.multiple_of(j * nd, nd), nd)
            out = dg(hid[...], wout[:, cols], NN) * weight
            y[both, :, cols] = out.astype(bf16).reshape(2, tok, nd)
            return 0
        lax.fori_loop(0, width // nd, outer, 0)
        n = base + zz * 4 + dx
        copies.go(n, y.at[place.at(zz, dx, 1)], kin.at[zz * 4 + dx], twin)

    def own(zz, dx):
        return y.at[place.at(zz, dx)]

    def chip_sum(zz, dx):
        copies.arrive(base + zz * 4 + dx, kin.at[zz * 4 + dx], twin)
        add_rows(own(zz, dx), [kin.at[zz * 4 + dx]], 0, tok)

    low, high = pl.ds(0, half), pl.ds(half, half)

    def far(zz):
        chip_sum(zz, 2)
        copies.go(base + 8 + zz, own(zz, 2).at[low], ap.at[zz], plus)
        copies.go(base + 10 + zz, own(zz, 2).at[high], am.at[zz], minus)

    def near(zz):
        chip_sum(zz, 1)
        copies.go(base + 12 + zz, own(zz, 1).at[high], bp.at[zz, high], plus)
        chip_sum(zz, 3)
        copies.go(base + 14 + zz, own(zz, 3).at[low], bm.at[zz, low], minus)

    def relay(zz):
        copies.arrive(base + 8 + zz, ap.at[zz], minus)
        add_rows(own(zz, 1).at[low], [ap.at[zz]], 0, half)
        copies.go(base + 16 + zz, own(zz, 1).at[low], bp.at[zz, low], plus)
        copies.arrive(base + 10 + zz, am.at[zz], plus)
        add_rows(own(zz, 3).at[high], [am.at[zz]], 0, half)
        copies.go(base + 18 + zz, own(zz, 3).at[high], bm.at[zz, high], minus)

    def settle(zz, h):
        if h == 0:
            copies.arrive(base + 14 + zz, bm.at[zz, low], plus)
            copies.arrive(base + 16 + zz, bp.at[zz, low], minus)
        else:
            copies.arrive(base + 12 + zz, bp.at[zz, high], minus)
            copies.arrive(base + 18 + zz, bm.at[zz, high], plus)

    compute(0, 0)
    gather.from_x(0)
    compute(0, 3)
    gather.from_z(0)
    compute(0, 1)
    gather.from_z(1)
    gather.from_far(0)
    compute(0, 2)
    gather.from_x(1)
    far(0)
    compute(1, 0)
    near(0)
    gather.from_far(1)
    compute(1, 3)
    relay(0)
    compute(1, 1)
    compute(1, 2)
    far(1)
    near(1)
    relay(1)
    chip_sum(1, 0)
    for h, part in ((0, low), (1, high)):
        settle(1, h)
        add_rows(own(1, 0), [bp.at[1], bm.at[1]], h * half, half)
        copies.go(base + 20 + h, own(1, 0).at[part], zb.at[part], over)
    chip_sum(0, 0)
    for h, part in ((0, low), (1, high)):
        settle(0, h)
        copies.arrive(base + 20 + h, zb.at[part], over)

        def last(i, _):
            at = pl.ds(pl.multiple_of(h * half + i * 16, 16), 16)
            total = mid_ref[at, :]
            for source in (own(0, 0), bp.at[0], bm.at[0], zb):
                total = total + source[at, :].astype(f32)
            out_ref[at, :] = total.astype(bf16)
            return 0
        lax.fori_loop(0, half // 16, last, 0)
    copies.finish()


def expert_call(sent, mid, expert_in, expert_out):
    tok, width = mid.shape
    ff = expert_out.shape[0]
    V, A = pl.BlockSpec(memory_space=pltpu.VMEM), pl.BlockSpec(memory_space=pl.ANY)
    count = GATHER_COPIES + 22
    vm = lambda *s: pltpu.VMEM(s, bf16)
    return pl.pallas_call(
        expert_kernel,
        out_shape=jax.ShapeDtypeStruct((tok, width), bf16),
        in_specs=[V, V, A, A],
        out_specs=V,
        scratch_shapes=[vm(16, tok, width + HD), vm(16, tok, width), vm(8, tok, width),
                        vm(2, tok // 2, width), vm(2, tok // 2, width), vm(2, tok, width), vm(2, tok, width),
                        vm(tok, width), vm(width, 2 * ff), vm(ff, width), vm(2 * tok, ff),
                        pltpu.SemaphoreType.DMA((count,)), pltpu.SemaphoreType.DMA((count,)),
                        pltpu.SemaphoreType.DMA((2,))],
        compiler_params=pltpu.CompilerParams(collective_id=1, has_side_effects=True,
                                             vmem_limit_bytes=52 * 1024 * 1024),
        name="expert_exchange",
    )(sent, mid, expert_in, expert_out)


def on_device(tokens, doc_ids, route_ids, norm_gain, proj_weight, gating_weight, block_scale,
              conv_weight, decay_rate, head_gain, out_weight, moe_gain, router_weight,
              expert_in, expert_out):
    residual = tokens[0].astype(f32)
    scale = jnp.repeat(block_scale[0, 0].astype(f32), HD)
    scaled = (proj_weight[:, 0, :].astype(f32) * scale[None, :]).astype(bf16)
    packed = jnp.concatenate([scaled, jnp.pad(gating_weight[:, :, 0], ((0, 0), (0, HD - 2)))], 1)
    projected, gates = project_call(tokens[0], norm_gain.reshape(1, D), packed)
    head_out = mixer_kernel(
        projected, gates,
        doc_ids[0].astype(f32).reshape(-1, C), conv_weight[0].astype(f32), decay_rate,
        head_gain.reshape(1, HD))
    out_full = lax.all_gather(lax.all_gather(out_weight[0], "fsdp", axis=1, tiled=True),
                              "expert", axis=0, tiled=True)
    tok = residual.shape[0]
    mine = lax.all_to_all(head_out.reshape(-1, tok, HD), "expert", split_axis=0, concat_axis=0, tiled=True)
    mine = jnp.swapaxes(mine, 0, 1).reshape(tok, D)
    mid = residual + jnp.dot(mine, out_full, preferred_element_type=f32)
    moe_in = rms_scale(mid, moe_gain).astype(bf16)
    logits = jnp.dot(moe_in, router_weight, preferred_element_type=f32)
    picked = (route_ids[0][:, :, None] == jnp.arange(EXPERTS, dtype=jnp.int32)).any(axis=1)
    raised = jnp.where(picked, jnp.exp(logits), 0.0)
    route_weight = raised / jnp.sum(raised, axis=1, keepdims=True)
    high = route_weight.astype(bf16)
    rest = (route_weight - high.astype(f32)).astype(bf16)
    sent = jnp.concatenate([moe_in, high, rest, jnp.zeros((tok, HD - 2 * EXPERTS), bf16)], 1)
    return expert_call(sent, mid, expert_in[0], expert_out[0])[None]


def solution(mesh):
    placed = (
        P("fsdp", "expert", None),
        P("fsdp", None),
        P("fsdp", "expert", None),
        P(),
        P("fsdp", "expert", None),
        P("fsdp", None, "expert"),
        P("fsdp", "expert", None),
        P("expert", None, None),
        P("expert"),
        P(),
        P("expert", None, "fsdp"),
        P(),
        P(),
        P("expert", None, None),
        P("expert", None, None),
    )
    return jax.shard_map(
        on_device, mesh=mesh, in_specs=placed, out_specs=P("fsdp", "expert", None), check_vma=False
    )
```

```python
import functools

import jax
import jax.numpy as jnp
from jax import lax
from jax.experimental import pallas as pl
from jax.experimental.pallas import tpu as pltpu
from jax.sharding import PartitionSpec as P

HD = 128
C = 128
EXPERTS = 16
PASSES = 3
MESH = pl.DeviceIdType.MESH
f32 = jnp.float32
bf16 = jnp.bfloat16
NN = ((1,), (0,))
NT = ((1,), (1,))
TN = ((0,), (0,))


def split(a):
    hi = a.astype(bf16)
    return hi, (a - hi.astype(f32)).astype(bf16)


def dg(a, b, dims=NN):
    return lax.dot_general(a, b, (dims, ((), ())), preferred_element_type=f32)


def mm(a, b, dims=NN, passes=PASSES):
    if passes == 1:
        return dg(a.astype(bf16), b.astype(bf16), dims)
    ah, al = split(a)
    bh, bl = split(b)
    return dg(ah, bh, dims) + (dg(al, bh, dims) + dg(ah, bl, dims))


def chunk_maps(c, gate_ref, docs_ref, win_ref, docc_ref, convw, rate):
    r0 = pl.multiple_of(c * C, C)
    docw = docc_ref[pl.ds(r0, C + 8), :]
    doc_col = docw[8:, :]
    parts = []
    for g in range(3):
        w = win_ref[pl.ds(r0, C + 8), g * HD:(g + 1) * HD]
        acc = w[8:, :] * convw[0:1, g * HD:(g + 1) * HD]
        for j in range(1, 4):
            keep = docw[8 - j:C + 8 - j, :] == doc_col
            acc = acc + jnp.where(keep, w[8 - j:C + 8 - j, :] * convw[j:j + 1, g * HD:(g + 1) * HD], 0.0)
        parts.append(acc * jax.nn.sigmoid(acc))
    q, k, v = parts
    q = q * (lax.rsqrt(jnp.sum(q * q, axis=1, keepdims=True) + 1e-6) * HD ** -0.5)
    k = k * lax.rsqrt(jnp.sum(k * k, axis=1, keepdims=True) + 1e-6)
    gates = gate_ref[pl.ds(r0, C), :]
    beta = jnp.broadcast_to(jax.nn.sigmoid(gates[:, 0:1]), (C, HD))
    d = gates[:, 1:2]
    sp = jnp.maximum(d, 0.0) + jnp.log1p(jnp.exp(-jnp.abs(d)))
    lg = jnp.broadcast_to(-rate * sp, (C, HD))
    row = lax.broadcasted_iota(jnp.int32, (C, C), 0)
    col = lax.broadcasted_iota(jnp.int32, (C, C), 1)
    low = (row >= col)
    tri = low.astype(bf16)
    h0 = lg.astype(bf16)
    r1 = lg - h0.astype(f32)
    h1 = r1.astype(bf16)
    h2 = (r1 - h1.astype(f32)).astype(bf16)
    cum = dg(tri, h0) + (dg(tri, h1) + dg(tri, h2))
    doc_row = docs_ref[pl.ds(c, 1), :]
    keep = jnp.logical_and(low, doc_col == doc_row)
    gap = cum - cum.T
    decay = jnp.where(keep, jnp.exp(jnp.where(keep, gap, 0.0)), 0.0)
    start = jnp.where(doc_col == docw[7:8, :], jnp.exp(cum), 0.0)
    kk = mm(k, k, NT)
    qk = mm(q, k, NT) * decay
    L = jnp.where(row > col, beta * kk * decay, 0.0)
    eye = (row == col).astype(f32)
    T = eye - jnp.where((row >> 1) == (col >> 1), L, 0.0)
    for sh in range(1, 7):
        m = jnp.logical_and((row >> (sh + 1)) == (col >> (sh + 1)), (row >> sh) != (col >> sh))
        T = T - mm(T, mm(jnp.where(m, L, 0.0), T))
    UW = mm(T, jnp.concatenate([beta * v, beta * start * k], axis=1))
    kend = k * decay.T[:, C - 1:C]
    PUW = mm(qk, UW)
    KUW = mm(kend, UW, TN)
    M = eye * start[C - 1:C, :] - KUW[:, HD:]
    Qp = start * q - PUW[:, HD:]
    return Qp, M, PUW[:, :HD], KUW[:, :HD]


def rms_scale(values, gain):
    mean_square = jnp.mean(values * values, axis=-1, keepdims=True)
    return values * lax.rsqrt(mean_square + 1e-06) * gain.astype(f32)


class Place:
    def __init__(self):
        e = lax.axis_index("expert")
        self.e = e
        self.z, self.x, self.c = e // 8, (e // 2) % 4, e % 2

    def at(self, zz, dx, cc=0):
        return ((self.z + zz) % 2 * 4 + (self.x + dx) % 4) * 2 + (self.c + cc) % 2

    def pair(self, zz, dx):
        return ((self.z + zz) % 2 * 4 + (self.x + dx) % 4) * 2


class Copies:
    def __init__(self, send, recv, base):
        self.send, self.recv, self.base, self.sent = send, recv, base, []

    def make(self, i, src, dst, peer):
        return pltpu.make_async_remote_copy(
            src_ref=src, dst_ref=dst, send_sem=self.send.at[self.base + i],
            recv_sem=self.recv.at[self.base + i], device_id=peer, device_id_type=MESH)

    def go(self, i, parts):
        self.make(i, *parts()).start()
        self.sent.append((i, parts))

    def arrive(self, i, dst, peer):
        self.make(i, dst, dst, peer).wait_recv()

    def finish(self):
        for i, parts in self.sent:
            self.make(i, *parts()).wait_send()


GATHER_COPIES = 30


class Gather:
    def __init__(self, full, copies, place, width):
        self.full, self.copies, self.place, self.width = full, copies, place, width
        self.half = full.shape[1] // 2

    def ref(self, zz, dx, h, cc=0):
        return self.full.at[self.place.at(zz, dx, cc), pl.ds(h * self.half, self.half), pl.ds(0, self.width)]

    def peer(self, *r):
        return {"expert": self.place.at(*r)}

    def go(self, n, zz, dx, h, to):
        def parts():
            block = self.ref(zz, dx, h)
            return block, block, self.peer(*to)
        self.copies.go(n, parts)

    def swap(self, zz, dx, h):
        self.go(14 + (zz * 4 + dx) * 2 + h, zz, dx, h, (0, 0, 1))

    def take(self, n, zz, dx, h):
        self.copies.arrive(n, self.ref(zz, dx, h), self.peer(0, 1))
        self.swap(zz, dx, h)

    def swapped(self, zz, dx):
        for h in range(2):
            self.copies.arrive(14 + (zz * 4 + dx) * 2 + h, self.ref(zz, dx, h, 1), self.peer(0, 0, 1))

    def plus(self, zz, h):
        self.go(2 + zz * 2 + h, zz, 0, h, (0, 1))

    def minus(self, zz, h):
        self.go(6 + zz * 2 + h, zz, 0, h, (0, 3))

    def begin(self):
        for h in range(2):
            self.go(h, 0, 0, h, (1, 0))
            self.plus(0, h)
            self.minus(0, 1 - h)
        self.swap(0, 0, 0)
        self.swap(0, 0, 1)

    def from_x(self, zz):
        self.take(2 + zz * 2, zz, 3, 0)
        self.go(10 + zz, zz, 3, 0, (0, 1))
        self.take(6 + zz * 2 + 1, zz, 1, 1)
        self.go(12 + zz, zz, 1, 1, (0, 3))
        self.take(2 + zz * 2 + 1, zz, 3, 1)
        self.take(6 + zz * 2, zz, 1, 0)

    def from_z(self, h):
        self.take(h, 1, 0, h)
        self.plus(1, h)
        self.minus(1, h)

    def from_far(self, zz):
        self.take(10 + zz, zz, 2, 0)
        self.take(12 + zz, zz, 2, 1)


def add_rows(dst, sources, first, count):
    def step(i, _):
        at = pl.ds(pl.multiple_of(first + i * 16, 16), 16)
        total = dst[at, :].astype(f32)
        for source in sources:
            total = total + source[at, :].astype(f32)
        dst[at, :] = total.astype(bf16)
        return 0
    lax.fori_loop(0, count // 16, step, 0)


SEM_TOKENS, SEM_SHARDS, SEM_OUT = 0, GATHER_COPIES, GATHER_COPIES + 19
SEM_HEADS = SEM_OUT + GATHER_COPIES
SEM_ROUTED = SEM_HEADS + 16
SEM_SUMS = SEM_ROUTED + GATHER_COPIES
SEM_ALL = SEM_SUMS + 22


def layer_kernel(tok_ref, docs_ref, ids_ref, gain_ref, pack_ref, conv_ref, rate_ref, hgain_ref, mgain_ref,
                 router_ref, ein_ref, eout_ref, out_ref,
                 full, w, win, branch, gate_ref, docc, maps, adds, obuf, heads, mid, y, kin, ap, am, bp, bm, zb,
                 up, down, hid, send, recv, load):
    place = Place()
    fsdp = lax.axis_index("fsdp")
    fy, fz = fsdp // 4, fsdp % 4
    tok, width = tok_ref.shape
    half = tok // 2
    rows = pack_ref.shape[0]
    ff = down.shape[0]
    chunks = 16 * tok // C

    def line(dy, d):
        return (fy + dy) % 4 * 4 + (fz + d) % 4

    barrier = pltpu.get_barrier_semaphore()
    peers = [{"expert": (place.e + i) % 16} for i in range(1, 16)]
    peers += [{"fsdp": line(*r)} for r in ((1, 0), (3, 0), (0, 1), (0, 2), (0, 3))]
    for peer in peers:
        pl.semaphore_signal(barrier, inc=1, device_id=peer, device_id_type=MESH)
    loads = [pltpu.make_async_copy(ein_ref, up, load.at[0]), pltpu.make_async_copy(eout_ref, down, load.at[1])]
    for copy in loads:
        copy.start()
    w[fsdp] = pack_ref[...]
    full[place.e, :, :width] = rms_scale(tok_ref[...].astype(f32), gain_ref[...]).astype(bf16)
    pl.semaphore_wait(barrier, len(peers))

    tokens = Copies(send, recv, SEM_TOKENS)
    shards = Copies(send, recv, SEM_SHARDS)
    gather = Gather(full, tokens, place, width)

    def shard(dy, d, h=None):
        slot = w.at[line(dy, (4 - d) % 4)]
        return slot if h is None else slot.at[pl.ds(h * (rows // 2), rows // 2)]

    def send_shard(n, at, to):
        def parts():
            ref = shard(*at)
            return ref, ref, {"fsdp": line(*to)}
        shards.go(n, parts)

    def both(d):
        send_shard(3 + d, (0, d), (1, 0))
        send_shard(7 + d, (0, d), (3, 0))

    def along_z(d):
        shards.arrive(d - 1, shard(0, d), {"fsdp": line(0, d)})
        both(d)

    def along_y(d):
        shards.arrive(3 + d, shard(3, d), {"fsdp": line(3, 0)})
        send_shard(11 + d, (3, d, 0), (1, 0))
        shards.arrive(7 + d, shard(1, d), {"fsdp": line(1, 0)})
        send_shard(15 + d, (1, d, 1), (3, 0))

    def far_y(d):
        shards.arrive(11 + d, shard(2, d, 0), {"fsdp": line(3, 0)})
        shards.arrive(15 + d, shard(2, d, 1), {"fsdp": line(1, 0)})

    for d in range(1, 4):
        send_shard(d - 1, (0, 0), (0, d))
    both(0)
    gather.begin()
    win[0:8, :] = jnp.zeros((8, 3 * HD), f32)
    docc[0:8, :] = jnp.full((8, HD), -1.0, f32)

    def spread(c, _):
        at = pl.ds(pl.multiple_of(c * C + 8, 8), C)
        docc[at, :] = jnp.broadcast_to(docs_ref[pl.ds(c, 1), :], (C, C)).T
        return 0
    lax.fori_loop(0, chunks, spread, 0)
    for d in range(1, 4):
        along_z(d)
    gather.from_x(0)
    along_y(0)
    gather.from_z(0)
    along_y(1)
    gather.from_z(1)
    along_y(2)
    gather.from_far(0)
    along_y(3)
    for d in range(4):
        far_y(d)
    for f in range(16):
        y[place.e, :, f * HD:(f + 1) * HD] = w[f, :, 5 * HD:]

    def project(zz):
        for dx in range(4):
            gather.swapped(zz, dx)

        def one(dx, _):
            slot = place.pair(zz, dx)
            x = full[pl.ds(slot, 2), :, :width].reshape(2 * tok, width)
            at = pl.ds(pl.multiple_of(slot * tok, 2 * tok), 2 * tok)
            after = pl.ds(pl.multiple_of(slot * tok + 8, 8), 2 * tok)
            r = dg(x, w[:, :, 0:2 * HD].reshape(16 * rows, 2 * HD)).astype(bf16)
            win[after, 0:2 * HD] = r.astype(f32)
            r = dg(x, w[:, :, 2 * HD:4 * HD].reshape(16 * rows, 2 * HD)).astype(bf16)
            win[after, 2 * HD:] = r[:, :HD].astype(f32)
            branch[at, :] = r[:, HD:]
            gate_ref[at, :] = dg(x, w[:, :, 4 * HD:5 * HD].reshape(16 * rows, HD))
            return 0
        lax.fori_loop(0, 4, one, 0)

    project(0)
    convw = conv_ref[...].astype(f32)
    rate = rate_ref[0]
    outs = Copies(send, recv, SEM_OUT)
    spreads = Gather(y, outs, place, width)

    def other_half():
        project(1)
        spreads.begin()

    events = {
        1: lambda: gather.from_x(1),
        2: lambda: gather.from_far(1),
        3: other_half,
        4: lambda: spreads.from_x(0),
        5: lambda: spreads.from_far(0),
        6: lambda: spreads.from_z(0),
        7: lambda: spreads.from_z(1),
    }

    def two_chunks(i, _):
        for step, event in events.items():
            pl.when(i == step)(event)
        first = (i + 5 * place.z) % 8 * 2
        for c in (first, first + 1):
            q_map, s_map, q_add, s_add = chunk_maps(c, gate_ref, docs_ref, win, docc, convw, rate)
            maps[c, :C, :] = q_map
            maps[c, C:, :] = s_map
            adds[c, :C, :] = q_add
            adds[c, C:, :] = s_add
        return 0
    lax.fori_loop(0, chunks // 2, two_chunks, 0)
    tokens.finish()
    spreads.from_x(1)

    def head_copy(c):
        return pltpu.make_async_remote_copy(
            src_ref=obuf.at[c], dst_ref=heads.at[:, pl.ds(pl.multiple_of(place.e * HD, HD), HD)],
            send_sem=send.at[SEM_HEADS + c], recv_sem=recv.at[SEM_HEADS + place.e],
            device_id={"expert": c}, device_id_type=MESH)

    hgain = hgain_ref[...].astype(f32)

    def advance(c, S):
        r0 = pl.multiple_of(c * C, C)
        two = mm(maps[c], S) + adds[c]
        o = two[:C, :]
        g = branch[pl.ds(r0, C), :].astype(f32)
        obuf[c] = (rms_scale(o, hgain) * (g * jax.nn.sigmoid(g))).astype(bf16)

        @pl.when(c != place.e)
        def _():
            head_copy(c).start()
        return two[C:, :]
    S = lax.fori_loop(0, chunks // 2, advance, jnp.zeros((HD, HD), f32))
    spreads.from_far(1)
    lax.fori_loop(chunks // 2, chunks, advance, S)
    for zz in range(2):
        for dx in range(4):
            spreads.swapped(zz, dx)
    heads[:, pl.ds(pl.multiple_of(place.e * HD, HD), HD)] = obuf[place.e]

    def head_in(h, _):
        @pl.when(h != place.e)
        def _():
            pltpu.make_async_remote_copy(
                src_ref=obuf.at[h], dst_ref=heads.at[:, pl.ds(pl.multiple_of(h * HD, HD), HD)],
                send_sem=send.at[SEM_HEADS + h], recv_sem=recv.at[SEM_HEADS + h],
                device_id={"expert": h}, device_id_type=MESH).wait_recv()
        return 0
    lax.fori_loop(0, 16, head_in, 0)
    nf, nd = min(256, ff), min(256, width)

    def out_project(j, _):
        cols = pl.ds(pl.multiple_of(j * nd, nd), nd)
        mid[:, cols] = tok_ref[:, cols].astype(f32) + dg(heads[...], y[:, :, cols].reshape(16 * HD, nd))
        return 0
    lax.fori_loop(0, width // nd, out_project, 0)
    moe_in = rms_scale(mid[...], mgain_ref[...]).astype(bf16)
    full[place.e, :, :width] = moe_in
    logits = dg(full[place.e, :, :width], router_ref[...])
    lane = lax.broadcasted_iota(jnp.int32, (tok, HD), 1)
    ids = ids_ref[...]
    picked = lane < 0
    for k in range(ids.shape[1]):
        picked = jnp.logical_or(picked, ids[:, k:k + 1] == lane % EXPERTS)
    raised = jnp.where(picked, jnp.exp(logits), 0.0)
    weights = raised / jnp.sum(jnp.where(lane < EXPERTS, raised, 0.0), axis=1, keepdims=True)
    upper = weights.astype(bf16).astype(f32)
    side = jnp.where(lane < EXPERTS, upper, jnp.where(lane < 2 * EXPERTS, weights - upper, 0.0))
    full[place.e, :, width:] = side.astype(bf16)
    outs.finish()

    routed = Copies(send, recv, SEM_ROUTED)
    sums = Copies(send, recv, SEM_SUMS)
    gather = Gather(full, routed, place, width + HD)
    gather.begin()
    for copy in loads:
        copy.wait()
    plus, minus = (lambda: {"expert": place.at(0, 1)}), (lambda: {"expert": place.at(0, 3)})
    over, twin = (lambda: {"expert": place.at(1, 0)}), (lambda: {"expert": place.at(0, 0, 1)})

    def compute(zz, dx):
        gather.swapped(zz, dx)
        pair = pl.ds(place.pair(zz, dx), 2)
        at = lax.broadcasted_iota(jnp.int32, (2 * tok, HD), 1)
        values = full[pair, :, width:].reshape(2 * tok, HD).astype(f32)
        hit = jnp.logical_or(at == place.e, at == place.e + EXPERTS)
        weight = jnp.sum(jnp.where(hit, values, 0.0), axis=1, keepdims=True)

        def inner(j, _):
            x = full[pair, :, :width].reshape(2 * tok, width)
            g = dg(x, up[:, pl.ds(pl.multiple_of(j * nf, nf), nf)])
            u = dg(x, up[:, pl.ds(pl.multiple_of(ff + j * nf, nf), nf)])
            hid[:, pl.ds(pl.multiple_of(j * nf, nf), nf)] = (g * jax.nn.sigmoid(g) * u).astype(bf16)
            return 0
        lax.fori_loop(0, ff // nf, inner, 0)

        def outer(j, _):
            cols = pl.ds(pl.multiple_of(j * nd, nd), nd)
            out = dg(hid[...], down[:, cols]) * weight
            y[pair, :, cols] = out.astype(bf16).reshape(2, tok, nd)
            return 0
        lax.fori_loop(0, width // nd, outer, 0)
        sums.go(zz * 4 + dx, lambda: (y.at[place.at(zz, dx, 1)], kin.at[zz * 4 + dx], twin()))

    def own(zz, dx):
        return y.at[place.at(zz, dx)]

    def chip_sum(zz, dx):
        sums.arrive(zz * 4 + dx, kin.at[zz * 4 + dx], twin())
        add_rows(own(zz, dx), [kin.at[zz * 4 + dx]], 0, tok)

    low, high = pl.ds(0, half), pl.ds(half, half)

    def far(zz):
        chip_sum(zz, 2)
        sums.go(8 + zz, lambda: (own(zz, 2).at[low], ap.at[zz], plus()))
        sums.go(10 + zz, lambda: (own(zz, 2).at[high], am.at[zz], minus()))

    def near(zz):
        chip_sum(zz, 1)
        sums.go(12 + zz, lambda: (own(zz, 1).at[high], bp.at[zz, high], plus()))
        chip_sum(zz, 3)
        sums.go(14 + zz, lambda: (own(zz, 3).at[low], bm.at[zz, low], minus()))

    def relay(zz):
        sums.arrive(8 + zz, ap.at[zz], minus())
        add_rows(own(zz, 1).at[low], [ap.at[zz]], 0, half)
        sums.go(16 + zz, lambda: (own(zz, 1).at[low], bp.at[zz, low], plus()))
        sums.arrive(10 + zz, am.at[zz], plus())
        add_rows(own(zz, 3).at[high], [am.at[zz]], 0, half)
        sums.go(18 + zz, lambda: (own(zz, 3).at[high], bm.at[zz, high], minus()))

    def settle(zz, h):
        if h == 0:
            sums.arrive(14 + zz, bm.at[zz, low], plus())
            sums.arrive(16 + zz, bp.at[zz, low], minus())
        else:
            sums.arrive(12 + zz, bp.at[zz, high], minus())
            sums.arrive(18 + zz, bm.at[zz, high], plus())

    compute(0, 0)
    gather.from_x(0)
    compute(0, 3)
    gather.from_z(0)
    compute(0, 1)
    gather.from_z(1)
    gather.from_far(0)
    compute(0, 2)
    gather.from_x(1)
    far(0)
    compute(1, 0)
    near(0)
    gather.from_far(1)
    compute(1, 3)
    relay(0)
    compute(1, 1)
    compute(1, 2)
    far(1)
    near(1)
    relay(1)
    chip_sum(1, 0)
    for h, part in ((0, low), (1, high)):
        settle(1, h)
        add_rows(own(1, 0), [bp.at[1], bm.at[1]], h * half, half)
        sums.go(20 + h, lambda part=part: (own(1, 0).at[part], zb.at[part], over()))
    chip_sum(0, 0)
    for h, part in ((0, low), (1, high)):
        settle(0, h)
        sums.arrive(20 + h, zb.at[part], over())

        def last(i, _):
            at = pl.ds(pl.multiple_of(h * half + i * 16, 16), 16)
            total = mid[at, :]
            for source in (own(0, 0), bp.at[0], bm.at[0], zb):
                total = total + source[at, :].astype(f32)
            out_ref[at, :] = total.astype(bf16)
            return 0
        lax.fori_loop(0, half // 16, last, 0)

    def head_out(c, _):
        @pl.when(c != place.e)
        def _():
            head_copy(c).wait_send()
        return 0
    lax.fori_loop(0, chunks, head_out, 0)
    shards.finish()
    routed.finish()
    sums.finish()


def layer_call(tokens, docs, ids, gain, packed, conv, rate, hgain, mgain, router, expert_in, expert_out):
    tok, width = tokens.shape
    rows, cols = packed.shape
    ff = expert_out.shape[0]
    seq = 16 * tok
    V, A = pl.BlockSpec(memory_space=pltpu.VMEM), pl.BlockSpec(memory_space=pl.ANY)
    S = pl.BlockSpec(memory_space=pltpu.SMEM)

    def vm(*s):
        return pltpu.VMEM(s, bf16)

    def vf(*s):
        return pltpu.VMEM(s, f32)
    sem = pltpu.SemaphoreType.DMA
    return pl.pallas_call(
        layer_kernel,
        out_shape=jax.ShapeDtypeStruct((tok, width), bf16),
        in_specs=[V, V, V, V, V, V, S, V, V, V, A, A],
        out_specs=V,
        scratch_shapes=[
            vm(16, tok, width + HD), vm(16, rows, cols), vf(seq + 8, 3 * HD), vm(seq, HD), vf(seq, HD),
            vf(seq + 8, HD), vf(seq // C, 2 * C, HD), vf(seq // C, 2 * C, HD), vm(seq // C, C, HD),
            vm(tok, 16 * HD), vf(tok, width), vm(16, tok, width), vm(8, tok, width),
            vm(2, tok // 2, width), vm(2, tok // 2, width), vm(2, tok, width), vm(2, tok, width), vm(tok, width),
            vm(width, 2 * ff), vm(ff, width), vm(2 * tok, ff), sem((SEM_ALL,)), sem((SEM_ALL,)), sem((2,))],
        compiler_params=pltpu.CompilerParams(collective_id=0, has_side_effects=True,
                                             vmem_limit_bytes=60 * 1024 * 1024),
        name="whole_layer",
    )(tokens, docs, ids, gain, packed, conv, rate, hgain, mgain, router, expert_in, expert_out)


def on_device(tokens, doc_ids, route_ids, norm_gain, proj_weight, gating_weight, block_scale,
              conv_weight, decay_rate, head_gain, out_weight, moe_gain, router_weight,
              expert_in, expert_out):
    scale = jnp.repeat(block_scale[0, 0].astype(f32), HD)
    scaled = (proj_weight[:, 0, :].astype(f32) * scale[None, :]).astype(bf16)
    packed = jnp.concatenate(
        [scaled, jnp.pad(gating_weight[:, :, 0], ((0, 0), (0, HD - 2))), out_weight[0]], 1)
    router = jnp.pad(jnp.concatenate([router_weight, router_weight], 1), ((0, 0), (0, HD - 2 * EXPERTS)))
    return layer_call(
        tokens[0], doc_ids[0].astype(f32).reshape(-1, C), route_ids[0], norm_gain.reshape(1, -1), packed,
        conv_weight[0], decay_rate, head_gain.reshape(1, -1), moe_gain.reshape(1, -1), router,
        expert_in[0], expert_out[0])[None]


def solution(mesh):
    placed = (
        P("fsdp", "expert", None),
        P("fsdp", None),
        P("fsdp", "expert", None),
        P(),
        P("fsdp", "expert", None),
        P("fsdp", None, "expert"),
        P("fsdp", "expert", None),
        P("expert", None, None),
        P("expert"),
        P(),
        P("expert", None, "fsdp"),
        P(),
        P(),
        P("expert", None, None),
        P("expert", None, None),
    )
    return jax.shard_map(
        on_device, mesh=mesh, in_specs=placed, out_specs=P("fsdp", "expert", None), check_vma=False
    )
```

```python
import functools

import jax
import jax.numpy as jnp
from jax import lax
from jax.experimental import pallas as pl
from jax.experimental.pallas import tpu as pltpu
from jax.sharding import PartitionSpec as P

HD = 128
C = 128
EXPERTS = 16
PASSES = 3
MESH = pl.DeviceIdType.MESH
f32 = jnp.float32
bf16 = jnp.bfloat16
NN = ((1,), (0,))
NT = ((1,), (1,))
TN = ((0,), (0,))


def split(a):
    hi = a.astype(bf16)
    return hi, (a - hi.astype(f32)).astype(bf16)


def dg(a, b, dims=NN):
    return lax.dot_general(a, b, (dims, ((), ())), preferred_element_type=f32)


def mm(a, b, dims=NN, passes=PASSES):
    if passes == 1:
        return dg(a.astype(bf16), b.astype(bf16), dims)
    ah, al = split(a)
    bh, bl = split(b)
    return dg(ah, bh, dims) + (dg(al, bh, dims) + dg(ah, bl, dims))


def chunk_maps(c, gate_ref, docs_ref, win_ref, docc_ref, convw, rate):
    r0 = pl.multiple_of(c * C, C)
    docw = docc_ref[pl.ds(r0, C + 8), :]
    doc_col = docw[8:, :]
    parts = []
    for g in range(3):
        w = win_ref[pl.ds(r0, C + 8), g * HD:(g + 1) * HD]
        acc = w[8:, :] * convw[0:1, g * HD:(g + 1) * HD]
        for j in range(1, 4):
            keep = docw[8 - j:C + 8 - j, :] == doc_col
            acc = acc + jnp.where(keep, w[8 - j:C + 8 - j, :] * convw[j:j + 1, g * HD:(g + 1) * HD], 0.0)
        parts.append(acc * jax.nn.sigmoid(acc))
    q, k, v = parts
    q = q * (lax.rsqrt(jnp.sum(q * q, axis=1, keepdims=True) + 1e-6) * HD ** -0.5)
    k = k * lax.rsqrt(jnp.sum(k * k, axis=1, keepdims=True) + 1e-6)
    gates = gate_ref[pl.ds(r0, C), :]
    beta = jnp.broadcast_to(jax.nn.sigmoid(gates[:, 0:1]), (C, HD))
    d = gates[:, 1:2]
    sp = jnp.maximum(d, 0.0) + jnp.log1p(jnp.exp(-jnp.abs(d)))
    lg = jnp.broadcast_to(-rate * sp, (C, HD))
    row = lax.broadcasted_iota(jnp.int32, (C, C), 0)
    col = lax.broadcasted_iota(jnp.int32, (C, C), 1)
    low = (row >= col)
    tri = low.astype(bf16)
    h0 = lg.astype(bf16)
    r1 = lg - h0.astype(f32)
    h1 = r1.astype(bf16)
    h2 = (r1 - h1.astype(f32)).astype(bf16)
    cum = dg(tri, h0) + (dg(tri, h1) + dg(tri, h2))
    doc_row = docs_ref[0:1, pl.ds(r0, C)].astype(f32)
    keep = jnp.logical_and(low, doc_col == doc_row)
    gap = cum - cum.T
    decay = jnp.where(keep, jnp.exp(jnp.where(keep, gap, 0.0)), 0.0)
    start = jnp.where(doc_col == docw[7:8, :], jnp.exp(cum), 0.0)
    kk = mm(k, k, NT)
    qk = mm(q, k, NT) * decay
    L = jnp.where(row > col, beta * kk * decay, 0.0)
    eye = (row == col).astype(f32)
    T = eye - jnp.where((row >> 1) == (col >> 1), L, 0.0)
    for sh in range(1, 7):
        m = jnp.logical_and((row >> (sh + 1)) == (col >> (sh + 1)), (row >> sh) != (col >> sh))
        T = T - mm(T, mm(jnp.where(m, L, 0.0), T))
    UW = mm(T, jnp.concatenate([beta * v, beta * start * k], axis=1))
    kend = k * decay.T[:, C - 1:C]
    PUW = mm(qk, UW)
    KUW = mm(kend, UW, TN)
    M = eye * start[C - 1:C, :] - KUW[:, HD:]
    Qp = start * q - PUW[:, HD:]
    return Qp, M, PUW[:, :HD], KUW[:, :HD]


def rms_scale(values, gain):
    mean_square = jnp.mean(values * values, axis=-1, keepdims=True)
    return values * lax.rsqrt(mean_square + 1e-06) * gain.astype(f32)


class Place:
    def __init__(self):
        e = lax.axis_index("expert")
        self.e = e
        self.z, self.x, self.c = e // 8, (e // 2) % 4, e % 2

    def at(self, zz, dx, cc=0):
        return ((self.z + zz) % 2 * 4 + (self.x + dx) % 4) * 2 + (self.c + cc) % 2

    def pair(self, zz, dx):
        return ((self.z + zz) % 2 * 4 + (self.x + dx) % 4) * 2


class Copies:
    def __init__(self, send, recv, base):
        self.send, self.recv, self.base, self.sent = send, recv, base, []

    def make(self, i, src, dst, peer):
        return pltpu.make_async_remote_copy(
            src_ref=src, dst_ref=dst, send_sem=self.send.at[self.base + i],
            recv_sem=self.recv.at[self.base + i], device_id=peer, device_id_type=MESH)

    def go(self, i, parts):
        self.make(i, *parts()).start()
        self.sent.append((i, parts))

    def arrive(self, i, dst, peer):
        self.make(i, dst, dst, peer).wait_recv()

    def finish(self):
        for i, parts in self.sent:
            self.make(i, *parts()).wait_send()


GATHER_COPIES = 36
PIECES = 4
ORDER = ((0, 0), (0, 1), (1, 0), (0, 2), (1, 1), (0, 3), (1, 2), (1, 3))


class Gather:
    def __init__(self, full, copies, place, width):
        self.full, self.copies, self.place, self.width = full, copies, place, width
        self.rows = full.shape[3] // PIECES

    def piece(self, r):
        return pl.ds(r * self.rows, self.rows)

    def ref(self, zz, dx, r):
        p = self.place
        return self.full.at[(p.z + zz) % 2, (p.x + dx) % 4, p.c, self.piece(r), pl.ds(0, self.width)]

    def column(self, zz, r, cc):
        p = self.place
        return self.full.at[(p.z + zz) % 2, :, (p.c + cc) % 2, self.piece(r), pl.ds(0, self.width)]

    def peer(self, *r):
        return {"expert": self.place.at(*r)}

    def go(self, n, zz, dx, r, to):
        def parts():
            block = self.ref(zz, dx, r)
            return block, block, self.peer(*to)
        self.copies.go(n, parts)

    def across(self, r):
        self.go(r, 0, 0, r, (1, 0))

    def out(self, zz, r):
        self.go(4 + zz * 4 + r, zz, 0, r, (0, 1))
        self.go(12 + zz * 4 + r, zz, 0, r, (0, 3))

    def begin(self):
        for r in range(2):
            self.across(r)
            self.out(0, r)

    def near(self, zz, r):
        plus = lambda: self.copies.arrive(4 + zz * 4 + r, self.ref(zz, 3, r), self.peer(0, 1))
        minus = lambda: self.copies.arrive(12 + zz * 4 + r, self.ref(zz, 1, r), self.peer(0, 1))
        if r % 2 == 0:
            plus()
            self.go(20 + zz * 4 + r, zz, 3, r, (0, 1))
            minus()
        else:
            minus()
            self.go(20 + zz * 4 + r, zz, 1, r, (0, 3))
            plus()
        if zz == 0 and r + 2 < PIECES:
            self.out(0, r + 2)

    def crossed(self, r):
        self.copies.arrive(r, self.ref(1, 0, r), self.peer(1, 0))
        self.out(1, r)
        if r + 2 < PIECES:
            self.across(r + 2)

    def advance(self, k):
        zz, r = ORDER[k]
        self.near(zz, r)
        if k + 1 < len(ORDER) and ORDER[k + 1][0] == 1:
            self.crossed(ORDER[k + 1][1])
        self.copies.arrive(20 + zz * 4 + r, self.ref(zz, 2, r), self.peer(0, 1))

        def parts():
            block = self.column(zz, r, 0)
            return block, block, self.peer(0, 0, 1)
        self.copies.go(28 + zz * 4 + r, parts)

    def swapped(self, zz, r):
        self.copies.arrive(28 + zz * 4 + r, self.column(zz, r, 1), self.peer(0, 0, 1))


class Shards:
    def __init__(self, buf, copies, line, cut):
        self.buf, self.copies, self.line, self.cut = buf, copies, line, cut

    def ref(self, dy, d, h=None):
        slot = self.buf.at[self.line(dy, (4 - d) % 4)]
        if h is None:
            return slot
        return slot.at[pl.ds(0, self.cut)] if h == 0 else slot.at[pl.ds(self.cut, self.buf.shape[1] - self.cut)]

    def peer(self, *r):
        return {"fsdp": self.line(*r)}

    def go(self, n, at, to):
        def parts():
            ref = self.ref(*at)
            return ref, ref, self.peer(*to)
        self.copies.go(n, parts)

    def both(self, d):
        self.go(3 + d, (0, d), (1, 0))
        self.go(7 + d, (0, d), (3, 0))

    def begin(self):
        for d in range(1, 4):
            self.go(d - 1, (0, 0), (0, d))
        self.both(0)

    def along_z(self, d):
        self.copies.arrive(d - 1, self.ref(0, d), self.peer(0, d))
        self.both(d)

    def along_y(self, d):
        self.copies.arrive(3 + d, self.ref(3, d), self.peer(3, 0))
        self.go(11 + d, (3, d, 0), (1, 0))
        self.copies.arrive(7 + d, self.ref(1, d), self.peer(1, 0))
        self.go(15 + d, (1, d, 1), (3, 0))

    def far_y(self, d):
        self.copies.arrive(11 + d, self.ref(2, d, 0), self.peer(3, 0))
        self.copies.arrive(15 + d, self.ref(2, d, 1), self.peer(1, 0))


def add_rows(dst, sources, count):
    def step(i, _):
        at = pl.ds(pl.multiple_of(i * 16, 16), 16)
        total = sources[0][at, :].astype(f32)
        for source in sources[1:]:
            total = total + source[at, :].astype(f32)
        dst[at, :] = total.astype(bf16)
        return 0
    lax.fori_loop(0, count // 16, step, 0)


SEM_TOKENS, SEM_SHARDS, SEM_COLS = 0, GATHER_COPIES, GATHER_COPIES + 19
SEM_OUT = SEM_COLS + 19
SEM_HEADS = SEM_OUT + GATHER_COPIES
SEM_ROUTED = SEM_HEADS + 16
SEM_SUMS = SEM_ROUTED + GATHER_COPIES
SEM_ALL = SEM_SUMS + 36


def layer_kernel(tok_ref, docs_ref, ids_ref, gains_ref, pack_ref, cols_ref, conv_ref, rate_ref, hgain_ref,
                 router_ref, ein_ref, eout_ref, out_ref,
                 full, w, gw, oc, win, branch, gate_ref, docc, maps, adds, obuf, heads, mid, y, kin, ap, bp, bm, zb,
                 up, down, hid, send, recv, load):
    place = Place()
    fsdp = lax.axis_index("fsdp")
    fy, fz = fsdp // 4, fsdp % 4
    tok, width = tok_ref.shape
    part = tok // PIECES
    ff = down.shape[0]
    chunks = 16 * tok // C
    rows = width // 16

    def line(dy, d):
        return (fy + dy) % 4 * 4 + (fz + d) % 4

    barrier = pltpu.get_barrier_semaphore()
    peers = [{"expert": (place.e + i) % 16} for i in range(1, 16)]
    peers += [{"fsdp": line(*r)} for r in ((1, 0), (3, 0), (0, 1), (0, 2), (0, 3))]
    for peer in peers:
        pl.semaphore_signal(barrier, inc=1, device_id=peer, device_id_type=MESH)
    loads = [pltpu.make_async_copy(ein_ref, up, load.at[0]), pltpu.make_async_copy(eout_ref, down, load.at[1])]
    for copy in loads:
        copy.start()
    w[fsdp] = pack_ref[...]
    oc[fsdp] = cols_ref[...]
    full[place.z, place.x, place.c, :, :width] = rms_scale(tok_ref[...].astype(f32), gains_ref[0:1, :]).astype(bf16)
    pl.semaphore_wait(barrier, len(peers))

    tokens = Copies(send, recv, SEM_TOKENS)
    weights_in = Copies(send, recv, SEM_SHARDS)
    columns_in = Copies(send, recv, SEM_COLS)
    gather = Gather(full, tokens, place, width)
    shards = Shards(w, weights_in, line, rows // 2)
    columns = Shards(oc, columns_in, line, HD // 2)
    shards.begin()
    gather.begin()
    win[0:8, :] = jnp.zeros((8, 3 * HD), f32)
    docc[0:8, :] = jnp.full((8, HD), -1.0, f32)

    def spread(c, _):
        r0 = pl.multiple_of(c * C, C)
        docs = docs_ref[0:1, pl.ds(r0, C)].astype(f32)
        docc[pl.ds(pl.multiple_of(r0 + 8, 8), C), :] = jnp.broadcast_to(docs, (C, C)).T
        return 0
    lax.fori_loop(0, chunks, spread, 0)
    gather.advance(0)
    for d in range(1, 4):
        shards.along_z(d)
    gather.advance(1)
    for d in range(4):
        shards.along_y(d)
        gather.advance(2 + d)
    for d in range(4):
        shards.far_y(d)
    columns.begin()
    for f in range(16):
        gw[:, f * rows:(f + 1) * rows] = w[f, rows:, :rows]

    def project(zz):
        for r in range(PIECES):
            gather.swapped(zz, r)

        def one(xx, _):
            zi = (place.z + zz) % 2
            slot = zi * 8 + xx * 2
            x = full[zi, xx, :, :, :width].reshape(2 * tok, width)
            at = pl.ds(pl.multiple_of(slot * tok, 2 * tok), 2 * tok)
            after = pl.ds(pl.multiple_of(slot * tok + 8, 8), 2 * tok)
            r = dg(x, w[:, :rows, 0:2 * HD].reshape(16 * rows, 2 * HD)).astype(bf16)
            win[after, 0:2 * HD] = r.astype(f32)
            r = dg(x, w[:, :rows, 2 * HD:4 * HD].reshape(16 * rows, 2 * HD)).astype(bf16)
            win[after, 2 * HD:] = r[:, :HD].astype(f32)
            branch[at, :] = r[:, HD:]
            gate_ref[at, :] = dg(x, gw[...], NT)
            return 0
        lax.fori_loop(0, 4, one, 0)

    project(0)
    convw = conv_ref[...].astype(f32)
    rate = rate_ref[0]
    outs = Copies(send, recv, SEM_OUT)
    spreads = Gather(y, outs, place, width)

    def at_0():
        gather.advance(6)
        for d in range(1, 4):
            columns.along_z(d)

    def at_1():
        gather.advance(7)
        for d in range(4):
            columns.along_y(d)

    def at_2():
        for d in range(4):
            columns.far_y(d)
        for f in range(16):
            y[place.z, place.x, place.c, :, f * HD:(f + 1) * HD] = oc[f]
        spreads.begin()

    def at_3():
        project(1)
        spreads.advance(0)

    def at_4():
        spreads.advance(1)
        spreads.advance(2)

    events = (at_0, at_1, at_2, at_3, at_4, lambda: spreads.advance(3), lambda: spreads.advance(4),
              lambda: spreads.advance(5))

    def two_chunks(i, _):
        for step, event in enumerate(events):
            pl.when(i == step)(event)
        first = (i + 5 * place.z) % 8 * 2
        for c in (first, first + 1):
            q_map, s_map, q_add, s_add = chunk_maps(c, gate_ref, docs_ref, win, docc, convw, rate)
            maps[c, :C, :] = q_map
            maps[c, C:, :] = s_map
            adds[c, :C, :] = q_add
            adds[c, C:, :] = s_add
        return 0
    lax.fori_loop(0, chunks // 2, two_chunks, 0)
    tokens.finish()

    def head_copy(c):
        return pltpu.make_async_remote_copy(
            src_ref=obuf.at[c], dst_ref=heads.at[:, pl.ds(pl.multiple_of(place.e * HD, HD), HD)],
            send_sem=send.at[SEM_HEADS + c], recv_sem=recv.at[SEM_HEADS + place.e],
            device_id={"expert": c}, device_id_type=MESH)

    hgain = hgain_ref[...].astype(f32)

    def advance(c, S):
        r0 = pl.multiple_of(c * C, C)
        two = mm(maps[c], S) + adds[c]
        o = two[:C, :]
        g = branch[pl.ds(r0, C), :].astype(f32)
        obuf[c] = (rms_scale(o, hgain) * (g * jax.nn.sigmoid(g))).astype(bf16)

        @pl.when(c != place.e)
        def _():
            head_copy(c).start()
        return two[C:, :]
    S = lax.fori_loop(0, chunks // 2, advance, jnp.zeros((HD, HD), f32))
    spreads.advance(6)
    lax.fori_loop(chunks // 2, chunks, advance, S)
    spreads.advance(7)
    for zz, r in ORDER:
        spreads.swapped(zz, r)
    heads[:, pl.ds(pl.multiple_of(place.e * HD, HD), HD)] = obuf[place.e]

    def head_in(h, _):
        @pl.when(h != place.e)
        def _():
            pltpu.make_async_remote_copy(
                src_ref=obuf.at[h], dst_ref=heads.at[:, pl.ds(pl.multiple_of(h * HD, HD), HD)],
                send_sem=send.at[SEM_HEADS + h], recv_sem=recv.at[SEM_HEADS + h],
                device_id={"expert": h}, device_id_type=MESH).wait_recv()
        return 0
    lax.fori_loop(0, 16, head_in, 0)
    nf, nd = min(256, ff), min(256, width)

    def out_project(j, _):
        cols = pl.ds(pl.multiple_of(j * nd, nd), nd)
        mid[:, cols] = tok_ref[:, cols].astype(f32) + dg(heads[...], y[:, :, :, :, cols].reshape(16 * HD, nd))
        return 0
    lax.fori_loop(0, width // nd, out_project, 0)
    moe_in = rms_scale(mid[...], gains_ref[1:2, :]).astype(bf16)
    full[place.z, place.x, place.c, :, :width] = moe_in
    logits = dg(moe_in, router_ref[...])
    lane = lax.broadcasted_iota(jnp.int32, (tok, EXPERTS), 1)
    ids = ids_ref[...]
    picked = lane < 0
    for k in range(ids.shape[1]):
        picked = jnp.logical_or(picked, ids[:, k:k + 1] == lane)
    raised = jnp.where(picked, jnp.exp(logits), 0.0)
    weights = raised / jnp.sum(raised, axis=1, keepdims=True)
    upper, lower = split(weights)
    place_row = lax.broadcasted_iota(jnp.int32, (EXPERTS, HD), 0)
    place_col = lax.broadcasted_iota(jnp.int32, (EXPERTS, HD), 1)
    side = dg(upper, (place_col == place_row).astype(bf16)) + dg(lower, (place_col == place_row + EXPERTS).astype(bf16))
    full[place.z, place.x, place.c, :, width:] = side.astype(bf16)
    outs.finish()

    routed = Copies(send, recv, SEM_ROUTED)
    sums = Copies(send, recv, SEM_SUMS)
    gather = Gather(full, routed, place, width + HD)
    gather.begin()
    for copy in loads:
        copy.wait()
    plus, minus = (lambda: {"expert": place.at(0, 1)}), (lambda: {"expert": place.at(0, 3)})
    over, twin = (lambda: {"expert": place.at(1, 0)}), (lambda: {"expert": place.at(0, 0, 1)})

    def rows_of(r):
        return pl.ds(r * part, part)

    def half(zz):
        return (place.z + zz) % 2

    def compute(zz, r):
        gather.swapped(zz, r)
        n = 8 * part
        at = lax.broadcasted_iota(jnp.int32, (n, HD), 1)
        values = full[half(zz), :, :, r * part:(r + 1) * part, width:].reshape(n, HD).astype(f32)
        hit = jnp.logical_or(at == place.e, at == place.e + EXPERTS)
        weight = jnp.sum(jnp.where(hit, values, 0.0), axis=1, keepdims=True)

        def inner(j, _):
            x = full[half(zz), :, :, r * part:(r + 1) * part, :width].reshape(n, width)
            g = dg(x, up[:, pl.ds(pl.multiple_of(j * nf, nf), nf)])
            u = dg(x, up[:, pl.ds(pl.multiple_of(ff + j * nf, nf), nf)])
            hid[:, pl.ds(pl.multiple_of(j * nf, nf), nf)] = (g * jax.nn.sigmoid(g) * u).astype(bf16)
            return 0
        lax.fori_loop(0, ff // nf, inner, 0)

        def outer(j, _):
            cols = pl.ds(pl.multiple_of(j * nd, nd), nd)
            out = dg(hid[...], down[:, cols]) * weight
            y[half(zz), :, :, r * part:(r + 1) * part, cols] = out.astype(bf16).reshape(4, 2, part, nd)
            return 0
        lax.fori_loop(0, width // nd, outer, 0)
        sums.go(zz * 4 + r, lambda: (y.at[half(zz), :, 1 - place.c, rows_of(r)],
                                     kin.at[half(zz), :, rows_of(r)], twin()))

    def own(zz, dx, r):
        return y.at[half(zz), (place.x + dx) % 4, place.c, rows_of(r)]

    def got(zz, dx, r):
        return kin.at[half(zz), (place.x + dx) % 4, rows_of(r)]

    def onward(r):
        return (plus, minus, 1, bp) if r % 2 == 0 else (minus, plus, 3, bm)

    def direct(r):
        return (minus, 3, bm) if r % 2 == 0 else (plus, 1, bp)

    def chip_sums(zz, r):
        sums.arrive(zz * 4 + r, kin.at[half(zz), :, rows_of(r)], twin())
        to, dx, into = direct(r)
        add_rows(own(zz, 2, r), [own(zz, 2, r), got(zz, 2, r)], part)
        sums.go(8 + zz * 4 + r, lambda: (own(zz, 2, r), ap.at[zz, r], onward(r)[0]()))
        add_rows(own(zz, dx, r), [own(zz, dx, r), got(zz, dx, r)], part)
        sums.go(16 + zz * 4 + r, lambda: (own(zz, dx, r), into.at[zz, rows_of(r)], to()))

    def relay(zz, r):
        to, back, dx, into = onward(r)
        sums.arrive(8 + zz * 4 + r, ap.at[zz, r], back())
        add_rows(own(zz, dx, r), [own(zz, dx, r), got(zz, dx, r), ap.at[zz, r]], part)
        sums.go(24 + zz * 4 + r, lambda: (own(zz, dx, r), into.at[zz, rows_of(r)], to()))

    def settled(zz, r):
        sums.arrive(16 + zz * 4 + r, direct(r)[2].at[zz, rows_of(r)], plus())
        sums.arrive(24 + zz * 4 + r, onward(r)[3].at[zz, rows_of(r)], plus())
        return [own(zz, 0, r), got(zz, 0, r), bp.at[zz, rows_of(r)], bm.at[zz, rows_of(r)]]

    def cross(r):
        sources = settled(1, r)
        add_rows(own(1, 0, r), sources, part)
        sums.go(32 + r, lambda: (own(1, 0, r), zb.at[rows_of(r)], over()))

    def last(r):
        sources = settled(0, r)
        sums.arrive(32 + r, zb.at[rows_of(r)], over())
        add_rows(out_ref.at[rows_of(r)], [mid.at[rows_of(r)]] + sources + [zb.at[rows_of(r)]], part)

    for k in range(len(ORDER) + 4):
        if k < len(ORDER):
            gather.advance(k)
        for lag, stage in ((1, compute), (2, chip_sums), (3, relay)):
            if 0 <= k - lag < len(ORDER):
                stage(*ORDER[k - lag])
        if k >= 4 and ORDER[k - 4][0] == 1:
            cross(ORDER[k - 4][1])
    for r in range(PIECES):
        last(r)

    def head_out(c, _):
        @pl.when(c != place.e)
        def _():
            head_copy(c).wait_send()
        return 0
    lax.fori_loop(0, chunks, head_out, 0)
    weights_in.finish()
    columns_in.finish()
    routed.finish()
    sums.finish()


def layer_call(tokens, docs, ids, gains, packed, columns, conv, rate, hgain, router, expert_in, expert_out):
    tok, width = tokens.shape
    rows, cols = packed.shape
    ff = expert_out.shape[0]
    seq = 16 * tok
    V, A = pl.BlockSpec(memory_space=pltpu.VMEM), pl.BlockSpec(memory_space=pl.ANY)
    S = pl.BlockSpec(memory_space=pltpu.SMEM)

    def vm(*s):
        return pltpu.VMEM(s, bf16)

    def vf(*s):
        return pltpu.VMEM(s, f32)
    sem = pltpu.SemaphoreType.DMA
    return pl.pallas_call(
        layer_kernel,
        out_shape=jax.ShapeDtypeStruct((tok, width), bf16),
        in_specs=[V, V, V, V, V, V, V, S, V, V, A, A],
        out_specs=V,
        scratch_shapes=[
            vm(2, 4, 2, tok, width + HD), vm(16, rows, cols), vm(16, width), vm(16, HD, HD), vf(seq + 8, 3 * HD),
            vm(seq, HD), vf(seq, 16), vf(seq + 8, HD), vf(seq // C, 2 * C, HD), vf(seq // C, 2 * C, HD),
            vm(seq // C, C, HD), vm(tok, 16 * HD), vf(tok, width), vm(2, 4, 2, tok, width), vm(2, 4, tok, width),
            vm(2, PIECES, tok // PIECES, width), vm(2, tok, width), vm(2, tok, width), vm(tok, width),
            vm(width, 2 * ff), vm(ff, width), vm(8 * tok // PIECES, ff),
            sem((SEM_ALL,)), sem((SEM_ALL,)), sem((2,))],
        compiler_params=pltpu.CompilerParams(collective_id=0, has_side_effects=True,
                                             vmem_limit_bytes=60 * 1024 * 1024),
        name="whole_layer",
    )(tokens, docs, ids, gains, packed, columns, conv, rate, hgain, router, expert_in, expert_out)


def on_device(tokens, doc_ids, route_ids, norm_gain, proj_weight, gating_weight, block_scale,
              conv_weight, decay_rate, head_gain, out_weight, moe_gain, router_weight,
              expert_in, expert_out):
    scale = jnp.repeat(block_scale[0, 0].astype(f32), HD)
    scaled = (proj_weight[:, 0, :].astype(f32) * scale[None, :]).astype(bf16)
    gating = jnp.pad(gating_weight[:, :, 0].T, ((0, 14), (0, 3 * HD)))
    packed = jnp.concatenate([scaled, gating], 0)
    return layer_call(
        tokens[0], doc_ids, route_ids[0], jnp.stack([norm_gain, moe_gain]), packed, out_weight[0],
        conv_weight[0], decay_rate, head_gain.reshape(1, -1), router_weight, expert_in[0], expert_out[0])[None]


def solution(mesh):
    placed = (
        P("fsdp", "expert", None),
        P("fsdp", None),
        P("fsdp", "expert", None),
        P(),
        P("fsdp", "expert", None),
        P("fsdp", None, "expert"),
        P("fsdp", "expert", None),
        P("expert", None, None),
        P("expert"),
        P(),
        P("expert", None, "fsdp"),
        P(),
        P(),
        P("expert", None, None),
        P("expert", None, None),
    )
    return jax.shard_map(
        on_device, mesh=mesh, in_specs=placed, out_specs=P("fsdp", "expert", None), check_vma=False
    )
```

```python
import functools

import jax
import jax.numpy as jnp
from jax import lax
from jax.experimental import pallas as pl
from jax.experimental.pallas import tpu as pltpu
from jax.sharding import PartitionSpec as P

HD = 128
C = 128
EXPERTS = 16
PASSES = 3
MESH = pl.DeviceIdType.MESH
f32 = jnp.float32
bf16 = jnp.bfloat16
NN = ((1,), (0,))
NT = ((1,), (1,))
TN = ((0,), (0,))


def split(a):
    hi = a.astype(bf16)
    return hi, (a - hi.astype(f32)).astype(bf16)


def dg(a, b, dims=NN):
    return lax.dot_general(a, b, (dims, ((), ())), preferred_element_type=f32)


def mm(a, b, dims=NN, passes=PASSES):
    if passes == 1:
        return dg(a.astype(bf16), b.astype(bf16), dims)
    ah, al = split(a)
    bh, bl = split(b)
    return dg(ah, bh, dims) + (dg(al, bh, dims) + dg(ah, bl, dims))


def chunk_maps(c, gate_ref, docs_ref, win_ref, docc_ref, convw, rate):
    r0 = pl.multiple_of(c * C, C)
    docw = docc_ref[pl.ds(r0, C + 8), :]
    doc_col = docw[8:, :]
    parts = []
    for g in range(3):
        w = win_ref[pl.ds(r0, C + 8), g * HD:(g + 1) * HD]
        acc = w[8:, :] * convw[0:1, g * HD:(g + 1) * HD]
        for j in range(1, 4):
            keep = docw[8 - j:C + 8 - j, :] == doc_col
            acc = acc + jnp.where(keep, w[8 - j:C + 8 - j, :] * convw[j:j + 1, g * HD:(g + 1) * HD], 0.0)
        parts.append(acc * jax.nn.sigmoid(acc))
    q, k, v = parts
    q = q * (lax.rsqrt(jnp.sum(q * q, axis=1, keepdims=True) + 1e-6) * HD ** -0.5)
    k = k * lax.rsqrt(jnp.sum(k * k, axis=1, keepdims=True) + 1e-6)
    gates = gate_ref[pl.ds(r0, C), :]
    beta = jnp.broadcast_to(jax.nn.sigmoid(gates[:, 0:1]), (C, HD))
    d = gates[:, 1:2]
    sp = jnp.maximum(d, 0.0) + jnp.log1p(jnp.exp(-jnp.abs(d)))
    lg = jnp.broadcast_to(-rate * sp, (C, HD))
    row = lax.broadcasted_iota(jnp.int32, (C, C), 0)
    col = lax.broadcasted_iota(jnp.int32, (C, C), 1)
    low = (row >= col)
    tri = low.astype(bf16)
    h0 = lg.astype(bf16)
    r1 = lg - h0.astype(f32)
    h1 = r1.astype(bf16)
    h2 = (r1 - h1.astype(f32)).astype(bf16)
    cum = dg(tri, h0) + (dg(tri, h1) + dg(tri, h2))
    doc_row = docs_ref[0:1, pl.ds(r0, C)].astype(f32)
    keep = jnp.logical_and(low, doc_col == doc_row)
    gap = cum - cum.T
    decay = jnp.where(keep, jnp.exp(jnp.where(keep, gap, 0.0)), 0.0)
    start = jnp.where(doc_col == docw[7:8, :], jnp.exp(cum), 0.0)
    kk = mm(k, k, NT, passes=1)
    qk = mm(q, k, NT, passes=1) * decay
    L = jnp.where(row > col, beta * kk * decay, 0.0)
    eye = (row == col).astype(f32)
    T = eye - jnp.where((row >> 1) == (col >> 1), L, 0.0)
    for sh in range(1, 7):
        m = jnp.logical_and((row >> (sh + 1)) == (col >> (sh + 1)), (row >> sh) != (col >> sh))
        T = T - mm(T, mm(jnp.where(m, L, 0.0), T, passes=1), passes=1)
    UW = mm(T, jnp.concatenate([beta * v, beta * start * k], axis=1), passes=1)
    kend = k * decay.T[:, C - 1:C]
    PUW = mm(qk, UW, passes=1)
    KUW = mm(kend, UW, TN, passes=1)
    M = eye * start[C - 1:C, :] - KUW[:, HD:]
    Qp = start * q - PUW[:, HD:]
    return Qp, M, PUW[:, :HD], KUW[:, :HD]


def rms_scale(values, gain):
    mean_square = jnp.mean(values * values, axis=-1, keepdims=True)
    return values * lax.rsqrt(mean_square + 1e-06) * gain.astype(f32)


class Place:
    def __init__(self):
        e = lax.axis_index("expert")
        self.e = e
        self.z, self.x, self.c = e // 8, (e // 2) % 4, e % 2

    def at(self, zz, dx, cc=0):
        return ((self.z + zz) % 2 * 4 + (self.x + dx) % 4) * 2 + (self.c + cc) % 2

    def pair(self, zz, dx):
        return ((self.z + zz) % 2 * 4 + (self.x + dx) % 4) * 2


class Copies:
    def __init__(self, send, recv, base):
        self.send, self.recv, self.base, self.sent = send, recv, base, []

    def make(self, i, src, dst, peer):
        return pltpu.make_async_remote_copy(
            src_ref=src, dst_ref=dst, send_sem=self.send.at[self.base + i],
            recv_sem=self.recv.at[self.base + i], device_id=peer, device_id_type=MESH)

    def go(self, i, parts):
        self.make(i, *parts()).start()
        self.sent.append((i, parts))

    def arrive(self, i, dst, peer):
        self.make(i, dst, dst, peer).wait_recv()

    def finish(self):
        for i, parts in self.sent:
            self.make(i, *parts()).wait_send()


GATHER_COPIES = 30


class Gather:
    def __init__(self, full, copies, place, width):
        self.full, self.copies, self.place, self.width = full, copies, place, width
        self.half = full.shape[1] // 2

    def ref(self, zz, dx, h, cc=0):
        return self.full.at[self.place.at(zz, dx, cc), pl.ds(h * self.half, self.half), pl.ds(0, self.width)]

    def peer(self, *r):
        return {"expert": self.place.at(*r)}

    def go(self, n, zz, dx, h, to):
        def parts():
            block = self.ref(zz, dx, h)
            return block, block, self.peer(*to)
        self.copies.go(n, parts)

    def swap(self, zz, dx, h):
        self.go(14 + (zz * 4 + dx) * 2 + h, zz, dx, h, (0, 0, 1))

    def take(self, n, zz, dx, h):
        self.copies.arrive(n, self.ref(zz, dx, h), self.peer(0, 1))
        self.swap(zz, dx, h)

    def swapped(self, zz, dx):
        for h in range(2):
            self.copies.arrive(14 + (zz * 4 + dx) * 2 + h, self.ref(zz, dx, h, 1), self.peer(0, 0, 1))

    def plus(self, zz, h):
        self.go(2 + zz * 2 + h, zz, 0, h, (0, 1))

    def minus(self, zz, h):
        self.go(6 + zz * 2 + h, zz, 0, h, (0, 3))

    def begin(self, paced=True):
        self.paced = paced
        for h in range(2):
            if h == 0 or not paced:
                self.go(h, 0, 0, h, (1, 0))
            self.plus(0, h)
            self.minus(0, 1 - h)
        self.swap(0, 0, 0)
        self.swap(0, 0, 1)

    def from_x(self, zz):
        self.take(2 + zz * 2, zz, 3, 0)
        self.go(10 + zz, zz, 3, 0, (0, 1))
        self.take(6 + zz * 2 + 1, zz, 1, 1)
        self.go(12 + zz, zz, 1, 1, (0, 3))
        self.take(2 + zz * 2 + 1, zz, 3, 1)
        self.take(6 + zz * 2, zz, 1, 0)

    def from_z(self, h):
        self.copies.arrive(h, self.ref(1, 0, h), self.peer(0, 1))
        if h == 0 and self.paced:
            self.go(1, 0, 0, 1, (1, 0))
        self.swap(1, 0, h)
        self.plus(1, h)
        self.minus(1, h)

    def from_far(self, zz):
        self.take(10 + zz, zz, 2, 0)
        self.take(12 + zz, zz, 2, 1)


def add_rows(dst, sources, first, count):
    def step(i, _):
        at = pl.ds(pl.multiple_of(first + i * 16, 16), 16)
        total = dst[at, :].astype(f32)
        for source in sources:
            total = total + source[at, :].astype(f32)
        dst[at, :] = total.astype(bf16)
        return 0
    lax.fori_loop(0, count // 16, step, 0)


SEM_TOKENS, SEM_SHARDS, SEM_OUT = 0, GATHER_COPIES, GATHER_COPIES + 19
SEM_HEADS = SEM_OUT + GATHER_COPIES
SEM_ROUTED = SEM_HEADS + 16
SEM_SUMS = SEM_ROUTED + GATHER_COPIES
SEM_ALL = SEM_SUMS + 22


def layer_kernel(tok_ref, docs_ref, ids_ref, gains_ref, pack_ref, conv_ref, rate_ref, hgain_ref,
                 router_ref, ein_ref, eout_ref, out_ref,
                 full, w, win, branch, gate_ref, docc, maps, adds, obuf, heads, mid, y, kin, ap, am, bp, bm, zb,
                 up, down, hid, send, recv, load):
    place = Place()
    fsdp = lax.axis_index("fsdp")
    fy, fz = fsdp // 4, fsdp % 4
    tok, width = tok_ref.shape
    half = tok // 2
    rows = pack_ref.shape[0]
    ff = down.shape[0]
    chunks = 16 * tok // C

    def line(dy, d):
        return (fy + dy) % 4 * 4 + (fz + d) % 4

    barrier = pltpu.get_barrier_semaphore()
    peers = [{"expert": (place.e + i) % 16} for i in range(1, 16)]
    peers += [{"fsdp": line(*r)} for r in ((1, 0), (3, 0), (0, 1), (0, 2), (0, 3))]
    for peer in peers:
        pl.semaphore_signal(barrier, inc=1, device_id=peer, device_id_type=MESH)
    loads = [pltpu.make_async_copy(ein_ref, up, load.at[0]), pltpu.make_async_copy(eout_ref, down, load.at[1])]
    for copy in loads:
        copy.start()
    w[fsdp] = pack_ref[...]
    full[place.e, :, :width] = rms_scale(tok_ref[...].astype(f32), gains_ref[0:1, :]).astype(bf16)
    pl.semaphore_wait(barrier, len(peers))

    tokens = Copies(send, recv, SEM_TOKENS)
    shards = Copies(send, recv, SEM_SHARDS)
    gather = Gather(full, tokens, place, width)

    def shard(dy, d, h=None):
        slot = w.at[line(dy, (4 - d) % 4)]
        return slot if h is None else slot.at[pl.ds(h * (rows // 2), rows // 2)]

    def send_shard(n, at, to):
        def parts():
            ref = shard(*at)
            return ref, ref, {"fsdp": line(*to)}
        shards.go(n, parts)

    def both(d):
        send_shard(3 + d, (0, d), (1, 0))
        send_shard(7 + d, (0, d), (3, 0))

    def along_z(d):
        shards.arrive(d - 1, shard(0, d), {"fsdp": line(0, d)})
        both(d)

    def along_y(d):
        shards.arrive(3 + d, shard(3, d), {"fsdp": line(3, 0)})
        send_shard(11 + d, (3, d, 0), (1, 0))
        shards.arrive(7 + d, shard(1, d), {"fsdp": line(1, 0)})
        send_shard(15 + d, (1, d, 1), (3, 0))

    def far_y(d):
        shards.arrive(11 + d, shard(2, d, 0), {"fsdp": line(3, 0)})
        shards.arrive(15 + d, shard(2, d, 1), {"fsdp": line(1, 0)})

    for d in range(1, 4):
        send_shard(d - 1, (0, 0), (0, d))
    both(0)
    gather.begin()
    win[0:8, :] = jnp.zeros((8, 3 * HD), f32)
    docc[0:8, :] = jnp.full((8, HD), -1.0, f32)

    def spread(c, _):
        at = pl.ds(pl.multiple_of(c * C + 8, 8), C)
        docs = docs_ref[0:1, pl.ds(pl.multiple_of(c * C, C), C)].astype(f32)
        docc[at, :] = jnp.broadcast_to(docs, (C, C)).T
        return 0
    lax.fori_loop(0, chunks, spread, 0)
    for d in range(1, 4):
        along_z(d)
    gather.from_x(0)
    along_y(0)
    gather.from_z(0)
    along_y(1)
    gather.from_z(1)
    along_y(2)
    gather.from_far(0)
    along_y(3)
    for d in range(4):
        far_y(d)
    for f in range(16):
        y[place.e, :, f * HD:(f + 1) * HD] = w[f, :, 5 * HD:]

    def project(zz):
        for dx in range(4):
            gather.swapped(zz, dx)

        def one(dx, _):
            slot = place.pair(zz, dx)
            x = full[pl.ds(slot, 2), :, :width].reshape(2 * tok, width)
            at = pl.ds(pl.multiple_of(slot * tok, 2 * tok), 2 * tok)
            after = pl.ds(pl.multiple_of(slot * tok + 8, 8), 2 * tok)
            r = dg(x, w[:, :, 0:2 * HD].reshape(16 * rows, 2 * HD)).astype(bf16)
            win[after, 0:2 * HD] = r.astype(f32)
            r = dg(x, w[:, :, 2 * HD:4 * HD].reshape(16 * rows, 2 * HD)).astype(bf16)
            win[after, 2 * HD:] = r[:, :HD].astype(f32)
            branch[at, :] = r[:, HD:]
            gate_ref[at, :] = dg(x, w[:, :, 4 * HD:5 * HD].reshape(16 * rows, HD))
            return 0
        lax.fori_loop(0, 4, one, 0)

    project(0)
    convw = conv_ref[...].astype(f32)
    rate = rate_ref[0]
    outs = Copies(send, recv, SEM_OUT)
    spreads = Gather(y, outs, place, width)

    def other_half():
        project(1)
        spreads.begin(paced=False)

    events = {
        1: lambda: gather.from_x(1),
        2: lambda: gather.from_far(1),
        3: other_half,
        4: lambda: spreads.from_x(0),
        5: lambda: spreads.from_far(0),
        6: lambda: spreads.from_z(0),
        7: lambda: spreads.from_z(1),
    }

    def two_chunks(i, _):
        for step, event in events.items():
            pl.when(i == step)(event)
        first = (i + 5 * place.z) % 8 * 2
        for c in (first, first + 1):
            q_map, s_map, q_add, s_add = chunk_maps(c, gate_ref, docs_ref, win, docc, convw, rate)
            maps[c, :C, :] = q_map
            maps[c, C:, :] = s_map
            adds[c, :C, :] = q_add
            adds[c, C:, :] = s_add
        return 0
    lax.fori_loop(0, chunks // 2, two_chunks, 0)
    tokens.finish()
    spreads.from_x(1)

    def head_copy(c):
        return pltpu.make_async_remote_copy(
            src_ref=obuf.at[c], dst_ref=heads.at[:, pl.ds(pl.multiple_of(place.e * HD, HD), HD)],
            send_sem=send.at[SEM_HEADS + c], recv_sem=recv.at[SEM_HEADS + place.e],
            device_id={"expert": c}, device_id_type=MESH)

    hgain = hgain_ref[...].astype(f32)

    def advance(c, S):
        r0 = pl.multiple_of(c * C, C)
        two = mm(maps[c], S) + adds[c]
        o = two[:C, :]
        g = branch[pl.ds(r0, C), :].astype(f32)
        obuf[c] = (rms_scale(o, hgain) * (g * jax.nn.sigmoid(g))).astype(bf16)

        @pl.when(c != place.e)
        def _():
            head_copy(c).start()
        return two[C:, :]
    S = lax.fori_loop(0, chunks // 2, advance, jnp.zeros((HD, HD), f32))
    spreads.from_far(1)
    lax.fori_loop(chunks // 2, chunks, advance, S)
    for zz in range(2):
        for dx in range(4):
            spreads.swapped(zz, dx)
    heads[:, pl.ds(pl.multiple_of(place.e * HD, HD), HD)] = obuf[place.e]

    def head_in(h, _):
        @pl.when(h != place.e)
        def _():
            pltpu.make_async_remote_copy(
                src_ref=obuf.at[h], dst_ref=heads.at[:, pl.ds(pl.multiple_of(h * HD, HD), HD)],
                send_sem=send.at[SEM_HEADS + h], recv_sem=recv.at[SEM_HEADS + h],
                device_id={"expert": h}, device_id_type=MESH).wait_recv()
        return 0
    lax.fori_loop(0, 16, head_in, 0)
    nf, nd = min(256, ff), min(256, width)

    def out_project(j, _):
        cols = pl.ds(pl.multiple_of(j * nd, nd), nd)
        mid[:, cols] = tok_ref[:, cols].astype(f32) + dg(heads[...], y[:, :, cols].reshape(16 * HD, nd))
        return 0
    lax.fori_loop(0, width // nd, out_project, 0)
    moe_in = rms_scale(mid[...], gains_ref[1:2, :]).astype(bf16)
    full[place.e, :, :width] = moe_in
    logits = dg(full[place.e, :, :width], router_ref[...])
    lane = lax.broadcasted_iota(jnp.int32, (tok, HD), 1)
    ids = ids_ref[...]
    picked = lane < 0
    for k in range(ids.shape[1]):
        picked = jnp.logical_or(picked, ids[:, k:k + 1] == lane % EXPERTS)
    raised = jnp.where(picked, jnp.exp(logits), 0.0)
    weights = raised / jnp.sum(jnp.where(lane < EXPERTS, raised, 0.0), axis=1, keepdims=True)
    upper = weights.astype(bf16).astype(f32)
    side = jnp.where(lane < EXPERTS, upper, jnp.where(lane < 2 * EXPERTS, weights - upper, 0.0))
    full[place.e, :, width:] = side.astype(bf16)
    outs.finish()

    routed = Copies(send, recv, SEM_ROUTED)
    sums = Copies(send, recv, SEM_SUMS)
    gather = Gather(full, routed, place, width + HD)
    gather.begin()
    for copy in loads:
        copy.wait()
    plus, minus = (lambda: {"expert": place.at(0, 1)}), (lambda: {"expert": place.at(0, 3)})
    over, twin = (lambda: {"expert": place.at(1, 0)}), (lambda: {"expert": place.at(0, 0, 1)})

    def compute(zz, dx):
        gather.swapped(zz, dx)
        pair = pl.ds(place.pair(zz, dx), 2)
        at = lax.broadcasted_iota(jnp.int32, (2 * tok, HD), 1)
        values = full[pair, :, width:].reshape(2 * tok, HD).astype(f32)
        hit = jnp.logical_or(at == place.e, at == place.e + EXPERTS)
        weight = jnp.sum(jnp.where(hit, values, 0.0), axis=1, keepdims=True)

        def inner(j, _):
            x = full[pair, :, :width].reshape(2 * tok, width)
            g = dg(x, up[:, pl.ds(pl.multiple_of(j * nf, nf), nf)])
            u = dg(x, up[:, pl.ds(pl.multiple_of(ff + j * nf, nf), nf)])
            hid[:, pl.ds(pl.multiple_of(j * nf, nf), nf)] = (g * jax.nn.sigmoid(g) * u).astype(bf16)
            return 0
        lax.fori_loop(0, ff // nf, inner, 0)

        def outer(j, _):
            cols = pl.ds(pl.multiple_of(j * nd, nd), nd)
            out = dg(hid[...], down[:, cols]) * weight
            y[pair, :, cols] = out.astype(bf16).reshape(2, tok, nd)
            return 0
        lax.fori_loop(0, width // nd, outer, 0)
        sums.go(zz * 4 + dx, lambda: (y.at[place.at(zz, dx, 1)], kin.at[zz * 4 + dx], twin()))

    def own(zz, dx):
        return y.at[place.at(zz, dx)]

    def chip_sum(zz, dx):
        sums.arrive(zz * 4 + dx, kin.at[zz * 4 + dx], twin())
        add_rows(own(zz, dx), [kin.at[zz * 4 + dx]], 0, tok)

    low, high = pl.ds(0, half), pl.ds(half, half)

    def far(zz):
        chip_sum(zz, 2)
        sums.go(8 + zz, lambda: (own(zz, 2).at[low], ap.at[zz], plus()))
        sums.go(10 + zz, lambda: (own(zz, 2).at[high], am.at[zz], minus()))

    def near(zz):
        chip_sum(zz, 1)
        sums.go(12 + zz, lambda: (own(zz, 1).at[high], bp.at[zz, high], plus()))
        chip_sum(zz, 3)
        sums.go(14 + zz, lambda: (own(zz, 3).at[low], bm.at[zz, low], minus()))

    def relay(zz):
        sums.arrive(8 + zz, ap.at[zz], minus())
        add_rows(own(zz, 1).at[low], [ap.at[zz]], 0, half)
        sums.go(16 + zz, lambda: (own(zz, 1).at[low], bp.at[zz, low], plus()))
        sums.arrive(10 + zz, am.at[zz], plus())
        add_rows(own(zz, 3).at[high], [am.at[zz]], 0, half)
        sums.go(18 + zz, lambda: (own(zz, 3).at[high], bm.at[zz, high], minus()))

    def settle(zz, h):
        if h == 0:
            sums.arrive(14 + zz, bm.at[zz, low], plus())
            sums.arrive(16 + zz, bp.at[zz, low], minus())
        else:
            sums.arrive(12 + zz, bp.at[zz, high], minus())
            sums.arrive(18 + zz, bm.at[zz, high], plus())

    compute(0, 0)
    gather.from_x(0)
    compute(0, 3)
    gather.from_z(0)
    compute(0, 1)
    gather.from_z(1)
    gather.from_far(0)
    compute(0, 2)
    gather.from_x(1)
    far(0)
    compute(1, 0)
    near(0)
    gather.from_far(1)
    compute(1, 3)
    relay(0)
    compute(1, 1)
    compute(1, 2)
    far(1)
    near(1)
    relay(1)
    chip_sum(1, 0)
    for h, part in ((0, low), (1, high)):
        settle(1, h)
        add_rows(own(1, 0), [bp.at[1], bm.at[1]], h * half, half)
        sums.go(20 + h, lambda part=part: (own(1, 0).at[part], zb.at[part], over()))
    chip_sum(0, 0)
    for h, part in ((0, low), (1, high)):
        settle(0, h)
        sums.arrive(20 + h, zb.at[part], over())

        def last(i, _):
            at = pl.ds(pl.multiple_of(h * half + i * 16, 16), 16)
            total = mid[at, :]
            for source in (own(0, 0), bp.at[0], bm.at[0], zb):
                total = total + source[at, :].astype(f32)
            out_ref[at, :] = total.astype(bf16)
            return 0
        lax.fori_loop(0, half // 16, last, 0)

    def head_out(c, _):
        @pl.when(c != place.e)
        def _():
            head_copy(c).wait_send()
        return 0
    lax.fori_loop(0, chunks, head_out, 0)
    shards.finish()
    routed.finish()
    sums.finish()


def layer_call(tokens, docs, ids, gains, packed, conv, rate, hgain, router, expert_in, expert_out):
    tok, width = tokens.shape
    rows, cols = packed.shape
    ff = expert_out.shape[0]
    seq = 16 * tok
    V, A = pl.BlockSpec(memory_space=pltpu.VMEM), pl.BlockSpec(memory_space=pl.ANY)
    S = pl.BlockSpec(memory_space=pltpu.SMEM)

    def vm(*s):
        return pltpu.VMEM(s, bf16)

    def vf(*s):
        return pltpu.VMEM(s, f32)
    sem = pltpu.SemaphoreType.DMA
    return pl.pallas_call(
        layer_kernel,
        out_shape=jax.ShapeDtypeStruct((tok, width), bf16),
        in_specs=[V, V, V, V, V, V, S, V, V, A, A],
        out_specs=V,
        scratch_shapes=[
            vm(16, tok, width + HD), vm(16, rows, cols), vf(seq + 8, 3 * HD), vm(seq, HD), vf(seq, HD),
            vf(seq + 8, HD), vf(seq // C, 2 * C, HD), vf(seq // C, 2 * C, HD), vm(seq // C, C, HD),
            vm(tok, 16 * HD), vf(tok, width), vm(16, tok, width), vm(8, tok, width),
            vm(2, tok // 2, width), vm(2, tok // 2, width), vm(2, tok, width), vm(2, tok, width), vm(tok, width),
            vm(width, 2 * ff), vm(ff, width), vm(2 * tok, ff), sem((SEM_ALL,)), sem((SEM_ALL,)), sem((2,))],
        compiler_params=pltpu.CompilerParams(collective_id=0, has_side_effects=True,
                                             vmem_limit_bytes=60 * 1024 * 1024),
        name="whole_layer",
    )(tokens, docs, ids, gains, packed, conv, rate, hgain, router, expert_in, expert_out)


def on_device(tokens, doc_ids, route_ids, norm_gain, proj_weight, gating_weight, block_scale,
              conv_weight, decay_rate, head_gain, out_weight, moe_gain, router_weight,
              expert_in, expert_out):
    scale = jnp.repeat(block_scale[0, 0].astype(f32), HD)
    scaled = (proj_weight[:, 0, :].astype(f32) * scale[None, :]).astype(bf16)
    packed = jnp.concatenate(
        [scaled, jnp.pad(gating_weight[:, :, 0], ((0, 0), (0, HD - 2))), out_weight[0]], 1)
    router = jnp.pad(jnp.concatenate([router_weight, router_weight], 1), ((0, 0), (0, HD - 2 * EXPERTS)))
    return layer_call(
        tokens[0], doc_ids, route_ids[0], jnp.stack([norm_gain, moe_gain]), packed,
        conv_weight[0], decay_rate, head_gain.reshape(1, -1), router,
        expert_in[0], expert_out[0])[None]


def solution(mesh):
    placed = (
        P("fsdp", "expert", None),
        P("fsdp", None),
        P("fsdp", "expert", None),
        P(),
        P("fsdp", "expert", None),
        P("fsdp", None, "expert"),
        P("fsdp", "expert", None),
        P("expert", None, None),
        P("expert"),
        P(),
        P("expert", None, "fsdp"),
        P(),
        P(),
        P("expert", None, None),
        P("expert", None, None),
    )
    return jax.shard_map(
        on_device, mesh=mesh, in_specs=placed, out_specs=P("fsdp", "expert", None), check_vma=False
    )
```

```python
import functools

import jax
import jax.numpy as jnp
from jax import lax
from jax.experimental import pallas as pl
from jax.experimental.pallas import tpu as pltpu
from jax.sharding import PartitionSpec as P

HD = 128
C = 128
EXPERTS = 16
PASSES = 3
MESH = pl.DeviceIdType.MESH
f32 = jnp.float32
bf16 = jnp.bfloat16
NN = ((1,), (0,))
NT = ((1,), (1,))
TN = ((0,), (0,))


def split(a):
    hi = a.astype(bf16)
    return hi, (a - hi.astype(f32)).astype(bf16)


def dg(a, b, dims=NN):
    return lax.dot_general(a, b, (dims, ((), ())), preferred_element_type=f32)


def mm(a, b, dims=NN, passes=PASSES):
    if passes == 1:
        return dg(a.astype(bf16), b.astype(bf16), dims)
    ah, al = split(a)
    bh, bl = split(b)
    return dg(ah, bh, dims) + (dg(al, bh, dims) + dg(ah, bl, dims))


def chunk_maps(c, gate_ref, docs_ref, win_ref, docc_ref, convw, rate):
    r0 = pl.multiple_of(c * C, C)
    docw = docc_ref[pl.ds(r0, C + 8), :]
    doc_col = docw[8:, :]
    parts = []
    for g in range(3):
        w = win_ref[pl.ds(r0, C + 8), g * HD:(g + 1) * HD]
        acc = w[8:, :] * convw[0:1, g * HD:(g + 1) * HD]
        for j in range(1, 4):
            keep = docw[8 - j:C + 8 - j, :] == doc_col
            acc = acc + jnp.where(keep, w[8 - j:C + 8 - j, :] * convw[j:j + 1, g * HD:(g + 1) * HD], 0.0)
        parts.append(acc * jax.nn.sigmoid(acc))
    q, k, v = parts
    q = q * (lax.rsqrt(jnp.sum(q * q, axis=1, keepdims=True) + 1e-6) * HD ** -0.5)
    k = k * lax.rsqrt(jnp.sum(k * k, axis=1, keepdims=True) + 1e-6)
    gates = gate_ref[pl.ds(r0, C), :]
    beta = jnp.broadcast_to(jax.nn.sigmoid(gates[:, 0:1]), (C, HD))
    d = gates[:, 1:2]
    sp = jnp.maximum(d, 0.0) + jnp.log1p(jnp.exp(-jnp.abs(d)))
    lg = jnp.broadcast_to(-rate * sp, (C, HD))
    row = lax.broadcasted_iota(jnp.int32, (C, C), 0)
    col = lax.broadcasted_iota(jnp.int32, (C, C), 1)
    low = (row >= col)
    tri = low.astype(bf16)
    h0 = lg.astype(bf16)
    r1 = lg - h0.astype(f32)
    h1 = r1.astype(bf16)
    h2 = (r1 - h1.astype(f32)).astype(bf16)
    cum = dg(tri, h0) + (dg(tri, h1) + dg(tri, h2))
    doc_row = docs_ref[0:1, pl.ds(r0, C)].astype(f32)
    keep = jnp.logical_and(low, doc_col == doc_row)
    gap = cum - cum.T
    decay = jnp.where(keep, jnp.exp(jnp.where(keep, gap, 0.0)), 0.0)
    start = jnp.where(doc_col == docw[7:8, :], jnp.exp(cum), 0.0)
    kk = mm(k, k, NT, passes=1)
    qk = mm(q, k, NT, passes=1) * decay
    L = jnp.where(row > col, beta * kk * decay, 0.0)
    eye = (row == col).astype(f32)
    T = eye - jnp.where((row >> 1) == (col >> 1), L, 0.0)
    for sh in range(1, 7):
        m = jnp.logical_and((row >> (sh + 1)) == (col >> (sh + 1)), (row >> sh) != (col >> sh))
        T = T - mm(T, mm(jnp.where(m, L, 0.0), T, passes=1), passes=1)
    UW = mm(T, jnp.concatenate([beta * v, beta * start * k], axis=1), passes=1)
    kend = k * decay.T[:, C - 1:C]
    PUW = mm(qk, UW, passes=1)
    KUW = mm(kend, UW, TN, passes=1)
    M = eye * start[C - 1:C, :] - KUW[:, HD:]
    Qp = start * q - PUW[:, HD:]
    return Qp, M, PUW[:, :HD], KUW[:, :HD]


def rms_scale(values, gain):
    mean_square = jnp.mean(values * values, axis=-1, keepdims=True)
    return values * lax.rsqrt(mean_square + 1e-06) * gain.astype(f32)


class Place:
    def __init__(self):
        e = lax.axis_index("expert")
        self.e = e
        self.z, self.x, self.c = e // 8, (e // 2) % 4, e % 2

    def at(self, zz, dx, cc=0):
        return ((self.z + zz) % 2 * 4 + (self.x + dx) % 4) * 2 + (self.c + cc) % 2

    def pair(self, zz, dx):
        return ((self.z + zz) % 2 * 4 + (self.x + dx) % 4) * 2


class Copies:
    def __init__(self, send, recv, base):
        self.send, self.recv, self.base, self.sent = send, recv, base, []

    def make(self, i, src, dst, peer):
        return pltpu.make_async_remote_copy(
            src_ref=src, dst_ref=dst, send_sem=self.send.at[self.base + i],
            recv_sem=self.recv.at[self.base + i], device_id=peer, device_id_type=MESH)

    def go(self, i, parts):
        self.make(i, *parts()).start()
        self.sent.append((i, parts))

    def arrive(self, i, dst, peer):
        self.make(i, dst, dst, peer).wait_recv()

    def finish(self):
        for i, parts in self.sent:
            self.make(i, *parts()).wait_send()


GATHER_COPIES = 30


class Gather:
    def __init__(self, full, copies, place, width):
        self.full, self.copies, self.place, self.width = full, copies, place, width
        self.half = full.shape[1] // 2

    def ref(self, zz, dx, h, cc=0):
        return self.full.at[self.place.at(zz, dx, cc), pl.ds(h * self.half, self.half), pl.ds(0, self.width)]

    def peer(self, *r):
        return {"expert": self.place.at(*r)}

    def go(self, n, zz, dx, h, to):
        def parts():
            block = self.ref(zz, dx, h)
            return block, block, self.peer(*to)
        self.copies.go(n, parts)

    def swap(self, zz, dx, h):
        self.go(14 + (zz * 4 + dx) * 2 + h, zz, dx, h, (0, 0, 1))

    def take(self, n, zz, dx, h):
        self.copies.arrive(n, self.ref(zz, dx, h), self.peer(0, 1))
        self.swap(zz, dx, h)

    def swapped(self, zz, dx):
        for h in range(2):
            self.copies.arrive(14 + (zz * 4 + dx) * 2 + h, self.ref(zz, dx, h, 1), self.peer(0, 0, 1))

    def plus(self, zz, h):
        self.go(2 + zz * 2 + h, zz, 0, h, (0, 1))

    def minus(self, zz, h):
        self.go(6 + zz * 2 + h, zz, 0, h, (0, 3))

    def begin(self, paced=True):
        self.paced = paced
        for h in range(2):
            if h == 0 or not paced:
                self.go(h, 0, 0, h, (1, 0))
            self.plus(0, h)
            self.minus(0, 1 - h)
        self.swap(0, 0, 0)
        self.swap(0, 0, 1)

    def from_x(self, zz):
        self.take(2 + zz * 2, zz, 3, 0)
        self.go(10 + zz, zz, 3, 0, (0, 1))
        self.take(6 + zz * 2 + 1, zz, 1, 1)
        self.go(12 + zz, zz, 1, 1, (0, 3))
        self.take(2 + zz * 2 + 1, zz, 3, 1)
        self.take(6 + zz * 2, zz, 1, 0)

    def from_z(self, h):
        self.copies.arrive(h, self.ref(1, 0, h), self.peer(0, 1))
        if h == 0 and self.paced:
            self.go(1, 0, 0, 1, (1, 0))
        self.swap(1, 0, h)
        self.plus(1, h)
        self.minus(1, h)

    def from_far(self, zz):
        self.take(10 + zz, zz, 2, 0)
        self.take(12 + zz, zz, 2, 1)


def add_rows(dst, sources, first, count):
    def step(i, _):
        at = pl.ds(pl.multiple_of(first + i * 16, 16), 16)
        total = dst[at, :].astype(f32)
        for source in sources:
            total = total + source[at, :].astype(f32)
        dst[at, :] = total.astype(bf16)
        return 0
    lax.fori_loop(0, count // 16, step, 0)


SEM_TOKENS, SEM_SHARDS, SEM_OUT = 0, GATHER_COPIES, GATHER_COPIES + 19
SEM_HEADS = SEM_OUT + GATHER_COPIES
SEM_ROUTED = SEM_HEADS + 16
SEM_SUMS = SEM_ROUTED + GATHER_COPIES
SEM_ALL = SEM_SUMS + 22


def layer_kernel(tok_ref, docs_ref, ids_ref, gains_ref, pack_ref, conv_ref, rate_ref, hgain_ref,
                 router_ref, ein_ref, eout_ref, out_ref,
                 full, w, win, branch, gate_ref, docc, maps, adds, obuf, heads, mid, y, kin, ap, am, bp, bm, zb,
                 up, down, hid, send, recv, load):
    place = Place()
    fsdp = lax.axis_index("fsdp")
    fy, fz = fsdp // 4, fsdp % 4
    tok, width = tok_ref.shape
    half = tok // 2
    rows = pack_ref.shape[0]
    ff = down.shape[0]
    chunks = 16 * tok // C

    def line(dy, d):
        return (fy + dy) % 4 * 4 + (fz + d) % 4

    barrier = pltpu.get_barrier_semaphore()
    peers = [{"expert": (place.e + i) % 16} for i in range(1, 16)]
    peers += [{"fsdp": line(*r)} for r in ((1, 0), (3, 0), (0, 1), (0, 2), (0, 3))]
    for peer in peers:
        pl.semaphore_signal(barrier, inc=1, device_id=peer, device_id_type=MESH)
    loads = [pltpu.make_async_copy(ein_ref, up, load.at[0]), pltpu.make_async_copy(eout_ref, down, load.at[1])]
    for copy in loads:
        copy.start()
    w[fsdp] = pack_ref[...]
    full[place.e, :, :width] = rms_scale(tok_ref[...].astype(f32), gains_ref[0:1, :]).astype(bf16)
    pl.semaphore_wait(barrier, len(peers))

    tokens = Copies(send, recv, SEM_TOKENS)
    shards = Copies(send, recv, SEM_SHARDS)
    gather = Gather(full, tokens, place, width)

    def shard(dy, d, h=None):
        slot = w.at[line(dy, (4 - d) % 4)]
        return slot if h is None else slot.at[pl.ds(h * (rows // 2), rows // 2)]

    def send_shard(n, at, to):
        def parts():
            ref = shard(*at)
            return ref, ref, {"fsdp": line(*to)}
        shards.go(n, parts)

    def both(d):
        send_shard(3 + d, (0, d), (1, 0))
        send_shard(7 + d, (0, d), (3, 0))

    def along_z(d):
        shards.arrive(d - 1, shard(0, d), {"fsdp": line(0, d)})
        both(d)

    def along_y(d):
        shards.arrive(3 + d, shard(3, d), {"fsdp": line(3, 0)})
        send_shard(11 + d, (3, d, 0), (1, 0))
        shards.arrive(7 + d, shard(1, d), {"fsdp": line(1, 0)})
        send_shard(15 + d, (1, d, 1), (3, 0))

    def far_y(d):
        shards.arrive(11 + d, shard(2, d, 0), {"fsdp": line(3, 0)})
        shards.arrive(15 + d, shard(2, d, 1), {"fsdp": line(1, 0)})

    for d in range(1, 4):
        send_shard(d - 1, (0, 0), (0, d))
    both(0)
    gather.begin()
    win[0:8, :] = jnp.zeros((8, 3 * HD), f32)
    docc[0:8, :] = jnp.full((8, HD), -1.0, f32)

    def spread(c, _):
        at = pl.ds(pl.multiple_of(c * C + 8, 8), C)
        docs = docs_ref[0:1, pl.ds(pl.multiple_of(c * C, C), C)].astype(f32)
        docc[at, :] = jnp.broadcast_to(docs, (C, C)).T
        return 0
    lax.fori_loop(0, chunks, spread, 0)
    for d in range(1, 4):
        along_z(d)
    gather.from_x(0)
    along_y(0)
    gather.from_z(0)
    along_y(1)
    gather.from_z(1)
    along_y(2)
    gather.from_far(0)
    along_y(3)
    for d in range(4):
        far_y(d)
    for f in range(16):
        y[place.e, :, f * HD:(f + 1) * HD] = w[f, :, 5 * HD:]

    def project(zz):
        for dx in range(4):
            gather.swapped(zz, dx)

        def one(dx, _):
            slot = place.pair(zz, dx)
            x = full[pl.ds(slot, 2), :, :width].reshape(2 * tok, width)
            at = pl.ds(pl.multiple_of(slot * tok, 2 * tok), 2 * tok)
            after = pl.ds(pl.multiple_of(slot * tok + 8, 8), 2 * tok)
            r = dg(x, w[:, :, 0:2 * HD].reshape(16 * rows, 2 * HD)).astype(bf16)
            win[after, 0:2 * HD] = r.astype(f32)
            r = dg(x, w[:, :, 2 * HD:4 * HD].reshape(16 * rows, 2 * HD)).astype(bf16)
            win[after, 2 * HD:] = r[:, :HD].astype(f32)
            branch[at, :] = r[:, HD:]
            gate_ref[at, :] = dg(x, w[:, :, 4 * HD:5 * HD].reshape(16 * rows, HD))
            return 0
        lax.fori_loop(0, 4, one, 0)

    project(0)
    convw = conv_ref[...].astype(f32)
    rate = rate_ref[0]
    outs = Copies(send, recv, SEM_OUT)
    spreads = Gather(y, outs, place, width)

    def other_half():
        project(1)
        spreads.begin(paced=False)

    events = {
        1: lambda: gather.from_x(1),
        2: lambda: gather.from_far(1),
        3: other_half,
        4: lambda: spreads.from_x(0),
        5: lambda: spreads.from_far(0),
        6: lambda: spreads.from_z(0),
        7: lambda: spreads.from_z(1),
    }

    def two_chunks(i, _):
        for step, event in events.items():
            pl.when(i == step)(event)
        first = (i + 5 * place.z) % 8 * 2
        for c in (first, first + 1):
            q_map, s_map, q_add, s_add = chunk_maps(c, gate_ref, docs_ref, win, docc, convw, rate)
            maps[c, :C, :] = q_map
            maps[c, C:, :] = s_map
            adds[c, :C, :] = q_add
            adds[c, C:, :] = s_add
        return 0
    lax.fori_loop(0, chunks // 2, two_chunks, 0)
    tokens.finish()
    spreads.from_x(1)

    def head_copy(c):
        return pltpu.make_async_remote_copy(
            src_ref=obuf.at[c], dst_ref=heads.at[:, pl.ds(pl.multiple_of(place.e * HD, HD), HD)],
            send_sem=send.at[SEM_HEADS + c], recv_sem=recv.at[SEM_HEADS + place.e],
            device_id={"expert": c}, device_id_type=MESH)

    hgain = hgain_ref[...].astype(f32)

    def advance(c, S):
        r0 = pl.multiple_of(c * C, C)
        two = mm(maps[c], S) + adds[c]
        o = two[:C, :]
        g = branch[pl.ds(r0, C), :].astype(f32)
        obuf[c] = (rms_scale(o, hgain) * (g * jax.nn.sigmoid(g))).astype(bf16)

        @pl.when(c != place.e)
        def _():
            head_copy(c).start()
        return two[C:, :]
    S = lax.fori_loop(0, chunks // 2, advance, jnp.zeros((HD, HD), f32))
    spreads.from_far(1)
    lax.fori_loop(chunks // 2, chunks, advance, S)
    for zz in range(2):
        for dx in range(4):
            spreads.swapped(zz, dx)
    heads[:, pl.ds(pl.multiple_of(place.e * HD, HD), HD)] = obuf[place.e]

    def head_in(h, _):
        @pl.when(h != place.e)
        def _():
            pltpu.make_async_remote_copy(
                src_ref=obuf.at[h], dst_ref=heads.at[:, pl.ds(pl.multiple_of(h * HD, HD), HD)],
                send_sem=send.at[SEM_HEADS + h], recv_sem=recv.at[SEM_HEADS + h],
                device_id={"expert": h}, device_id_type=MESH).wait_recv()
        return 0
    lax.fori_loop(0, 16, head_in, 0)
    nf, nd = min(256, ff), min(256, width)

    def out_project(j, _):
        cols = pl.ds(pl.multiple_of(j * nd, nd), nd)
        mid[:, cols] = tok_ref[:, cols].astype(f32) + dg(heads[...], y[:, :, cols].reshape(16 * HD, nd))
        return 0
    lax.fori_loop(0, width // nd, out_project, 0)
    moe_in = rms_scale(mid[...], gains_ref[1:2, :]).astype(bf16)
    full[place.e, :, :width] = moe_in
    logits = dg(full[place.e, :, :width], router_ref[...])
    lane = lax.broadcasted_iota(jnp.int32, (tok, HD), 1)
    ids = ids_ref[...]
    picked = lane < 0
    for k in range(ids.shape[1]):
        picked = jnp.logical_or(picked, ids[:, k:k + 1] == lane % EXPERTS)
    raised = jnp.where(picked, jnp.exp(logits), 0.0)
    weights = raised / jnp.sum(jnp.where(lane < EXPERTS, raised, 0.0), axis=1, keepdims=True)
    upper = weights.astype(bf16).astype(f32)
    side = jnp.where(lane < EXPERTS, upper, jnp.where(lane < 2 * EXPERTS, weights - upper, 0.0))
    full[place.e, :, width:] = side.astype(bf16)
    outs.finish()

    routed = Copies(send, recv, SEM_ROUTED)
    sums = Copies(send, recv, SEM_SUMS)
    gather = Gather(full, routed, place, width + HD)
    gather.begin()
    for copy in loads:
        copy.wait()
    plus, minus = (lambda: {"expert": place.at(0, 1)}), (lambda: {"expert": place.at(0, 3)})
    over, twin = (lambda: {"expert": place.at(1, 0)}), (lambda: {"expert": place.at(0, 0, 1)})

    def compute(zz, dx):
        gather.swapped(zz, dx)
        pair = pl.ds(place.pair(zz, dx), 2)
        at = lax.broadcasted_iota(jnp.int32, (2 * tok, HD), 1)
        values = full[pair, :, width:].reshape(2 * tok, HD).astype(f32)
        hit = jnp.logical_or(at == place.e, at == place.e + EXPERTS)
        weight = jnp.sum(jnp.where(hit, values, 0.0), axis=1, keepdims=True)

        def inner(j, _):
            x = full[pair, :, :width].reshape(2 * tok, width)
            g = dg(x, up[:, pl.ds(pl.multiple_of(j * nf, nf), nf)])
            u = dg(x, up[:, pl.ds(pl.multiple_of(ff + j * nf, nf), nf)])
            hid[:, pl.ds(pl.multiple_of(j * nf, nf), nf)] = (g * jax.nn.sigmoid(g) * u).astype(bf16)
            return 0
        lax.fori_loop(0, ff // nf, inner, 0)

        def outer(j, _):
            cols = pl.ds(pl.multiple_of(j * nd, nd), nd)
            out = dg(hid[...], down[:, cols]) * weight
            y[pair, :, cols] = out.astype(bf16).reshape(2, tok, nd)
            return 0
        lax.fori_loop(0, width // nd, outer, 0)
        sums.go(zz * 4 + dx, lambda: (y.at[place.at(zz, dx, 1)], kin.at[zz * 4 + dx], twin()))

    def own(zz, dx):
        return y.at[place.at(zz, dx)]

    def chip_sum(zz, dx):
        sums.arrive(zz * 4 + dx, kin.at[zz * 4 + dx], twin())
        add_rows(own(zz, dx), [kin.at[zz * 4 + dx]], 0, tok)

    low, high = pl.ds(0, half), pl.ds(half, half)

    def far(zz):
        chip_sum(zz, 2)
        sums.go(8 + zz, lambda: (own(zz, 2).at[low], ap.at[zz], plus()))
        sums.go(10 + zz, lambda: (own(zz, 2).at[high], am.at[zz], minus()))

    def near(zz):
        chip_sum(zz, 1)
        sums.go(12 + zz, lambda: (own(zz, 1).at[high], bp.at[zz, high], plus()))
        chip_sum(zz, 3)
        sums.go(14 + zz, lambda: (own(zz, 3).at[low], bm.at[zz, low], minus()))

    def relay(zz):
        sums.arrive(8 + zz, ap.at[zz], minus())
        add_rows(own(zz, 1).at[low], [ap.at[zz]], 0, half)
        sums.go(16 + zz, lambda: (own(zz, 1).at[low], bp.at[zz, low], plus()))
        sums.arrive(10 + zz, am.at[zz], plus())
        add_rows(own(zz, 3).at[high], [am.at[zz]], 0, half)
        sums.go(18 + zz, lambda: (own(zz, 3).at[high], bm.at[zz, high], minus()))

    def settle(zz, h):
        if h == 0:
            sums.arrive(14 + zz, bm.at[zz, low], plus())
            sums.arrive(16 + zz, bp.at[zz, low], minus())
        else:
            sums.arrive(12 + zz, bp.at[zz, high], minus())
            sums.arrive(18 + zz, bm.at[zz, high], plus())

    compute(0, 0)
    gather.from_x(0)
    compute(0, 3)
    gather.from_z(0)
    compute(0, 1)
    gather.from_z(1)
    gather.from_far(0)
    compute(0, 2)
    gather.from_x(1)
    compute(1, 0)
    gather.from_far(1)
    far(0)
    compute(1, 3)
    compute(1, 2)
    far(1)
    compute(1, 1)
    near(1)
    relay(1)
    chip_sum(1, 0)
    for h, part in ((0, low), (1, high)):
        settle(1, h)
        add_rows(own(1, 0), [bp.at[1], bm.at[1]], h * half, half)
        sums.go(20 + h, lambda part=part: (own(1, 0).at[part], zb.at[part], over()))
    near(0)
    relay(0)
    chip_sum(0, 0)
    for h, part in ((0, low), (1, high)):
        settle(0, h)
        sums.arrive(20 + h, zb.at[part], over())

        def last(i, _):
            at = pl.ds(pl.multiple_of(h * half + i * 16, 16), 16)
            total = mid[at, :]
            for source in (own(0, 0), bp.at[0], bm.at[0], zb):
                total = total + source[at, :].astype(f32)
            out_ref[at, :] = total.astype(bf16)
            return 0
        lax.fori_loop(0, half // 16, last, 0)

    def head_out(c, _):
        @pl.when(c != place.e)
        def _():
            head_copy(c).wait_send()
        return 0
    lax.fori_loop(0, chunks, head_out, 0)
    shards.finish()
    routed.finish()
    sums.finish()


def layer_call(tokens, docs, ids, gains, packed, conv, rate, hgain, router, expert_in, expert_out):
    tok, width = tokens.shape
    rows, cols = packed.shape
    ff = expert_out.shape[0]
    seq = 16 * tok
    V, A = pl.BlockSpec(memory_space=pltpu.VMEM), pl.BlockSpec(memory_space=pl.ANY)
    S = pl.BlockSpec(memory_space=pltpu.SMEM)

    def vm(*s):
        return pltpu.VMEM(s, bf16)

    def vf(*s):
        return pltpu.VMEM(s, f32)
    sem = pltpu.SemaphoreType.DMA
    return pl.pallas_call(
        layer_kernel,
        out_shape=jax.ShapeDtypeStruct((tok, width), bf16),
        in_specs=[V, V, V, V, V, V, S, V, V, A, A],
        out_specs=V,
        scratch_shapes=[
            vm(16, tok, width + HD), vm(16, rows, cols), vf(seq + 8, 3 * HD), vm(seq, HD), vf(seq, HD),
            vf(seq + 8, HD), vf(seq // C, 2 * C, HD), vf(seq // C, 2 * C, HD), vm(seq // C, C, HD),
            vm(tok, 16 * HD), vf(tok, width), vm(16, tok, width), vm(8, tok, width),
            vm(2, tok // 2, width), vm(2, tok // 2, width), vm(2, tok, width), vm(2, tok, width), vm(tok, width),
            vm(width, 2 * ff), vm(ff, width), vm(2 * tok, ff), sem((SEM_ALL,)), sem((SEM_ALL,)), sem((2,))],
        compiler_params=pltpu.CompilerParams(collective_id=0, has_side_effects=True,
                                             vmem_limit_bytes=60 * 1024 * 1024),
        name="whole_layer",
    )(tokens, docs, ids, gains, packed, conv, rate, hgain, router, expert_in, expert_out)


def on_device(tokens, doc_ids, route_ids, norm_gain, proj_weight, gating_weight, block_scale,
              conv_weight, decay_rate, head_gain, out_weight, moe_gain, router_weight,
              expert_in, expert_out):
    scale = jnp.repeat(block_scale[0, 0].astype(f32), HD)
    scaled = (proj_weight[:, 0, :].astype(f32) * scale[None, :]).astype(bf16)
    packed = jnp.concatenate(
        [scaled, jnp.pad(gating_weight[:, :, 0], ((0, 0), (0, HD - 2))), out_weight[0]], 1)
    router = jnp.pad(jnp.concatenate([router_weight, router_weight], 1), ((0, 0), (0, HD - 2 * EXPERTS)))
    return layer_call(
        tokens[0], doc_ids, route_ids[0], jnp.stack([norm_gain, moe_gain]), packed,
        conv_weight[0], decay_rate, head_gain.reshape(1, -1), router,
        expert_in[0], expert_out[0])[None]


def solution(mesh):
    placed = (
        P("fsdp", "expert", None),
        P("fsdp", None),
        P("fsdp", "expert", None),
        P(),
        P("fsdp", "expert", None),
        P("fsdp", None, "expert"),
        P("fsdp", "expert", None),
        P("expert", None, None),
        P("expert"),
        P(),
        P("expert", None, "fsdp"),
        P(),
        P(),
        P("expert", None, None),
        P("expert", None, None),
    )
    return jax.shard_map(
        on_device, mesh=mesh, in_specs=placed, out_specs=P("fsdp", "expert", None), check_vma=False
    )
```

```python
import functools

import jax
import jax.numpy as jnp
from jax import lax
from jax.experimental import pallas as pl
from jax.experimental.pallas import tpu as pltpu
from jax.sharding import PartitionSpec as P

HD = 128
C = 128
EXPERTS = 16
PASSES = 3
MESH = pl.DeviceIdType.MESH
f32 = jnp.float32
bf16 = jnp.bfloat16
NN = ((1,), (0,))
NT = ((1,), (1,))
TN = ((0,), (0,))


def split(a):
    hi = a.astype(bf16)
    return hi, (a - hi.astype(f32)).astype(bf16)


def dg(a, b, dims=NN):
    return lax.dot_general(a, b, (dims, ((), ())), preferred_element_type=f32)


def mm(a, b, dims=NN, passes=PASSES):
    if passes == 1:
        return dg(a.astype(bf16), b.astype(bf16), dims)
    ah, al = split(a)
    bh, bl = split(b)
    return dg(ah, bh, dims) + (dg(al, bh, dims) + dg(ah, bl, dims))


def chunk_maps(c, gate_ref, docs_ref, win_ref, docc_ref, convw, rate):
    r0 = pl.multiple_of(c * C, C)
    docw = docc_ref[pl.ds(r0, C + 8), :]
    doc_col = docw[8:, :]
    parts = []
    for g in range(3):
        w = win_ref[pl.ds(r0, C + 8), g * HD:(g + 1) * HD]
        acc = w[8:, :] * convw[0:1, g * HD:(g + 1) * HD]
        for j in range(1, 4):
            keep = docw[8 - j:C + 8 - j, :] == doc_col
            acc = acc + jnp.where(keep, w[8 - j:C + 8 - j, :] * convw[j:j + 1, g * HD:(g + 1) * HD], 0.0)
        parts.append(acc * jax.nn.sigmoid(acc))
    q, k, v = parts
    q = q * (lax.rsqrt(jnp.sum(q * q, axis=1, keepdims=True) + 1e-6) * HD ** -0.5)
    k = k * lax.rsqrt(jnp.sum(k * k, axis=1, keepdims=True) + 1e-6)
    gates = gate_ref[pl.ds(r0, C), :]
    beta = jnp.broadcast_to(jax.nn.sigmoid(gates[:, 0:1]), (C, HD))
    d = gates[:, 1:2]
    sp = jnp.maximum(d, 0.0) + jnp.log1p(jnp.exp(-jnp.abs(d)))
    lg = jnp.broadcast_to(-rate * sp, (C, HD))
    row = lax.broadcasted_iota(jnp.int32, (C, C), 0)
    col = lax.broadcasted_iota(jnp.int32, (C, C), 1)
    low = (row >= col)
    tri = low.astype(bf16)
    h0 = lg.astype(bf16)
    r1 = lg - h0.astype(f32)
    h1 = r1.astype(bf16)
    h2 = (r1 - h1.astype(f32)).astype(bf16)
    cum = dg(tri, h0) + (dg(tri, h1) + dg(tri, h2))
    doc_row = docs_ref[0:1, pl.ds(r0, C)].astype(f32)
    keep = jnp.logical_and(low, doc_col == doc_row)
    gap = cum - cum.T
    decay = jnp.where(keep, jnp.exp(jnp.where(keep, gap, 0.0)), 0.0)
    start = jnp.where(doc_col == docw[7:8, :], jnp.exp(cum), 0.0)
    kk = mm(k, k, NT, passes=1)
    qk = mm(q, k, NT, passes=1) * decay
    L = jnp.where(row > col, beta * kk * decay, 0.0)
    eye = (row == col).astype(f32)
    T = eye - jnp.where((row >> 1) == (col >> 1), L, 0.0)
    for sh in range(1, 7):
        m = jnp.logical_and((row >> (sh + 1)) == (col >> (sh + 1)), (row >> sh) != (col >> sh))
        T = T - mm(T, mm(jnp.where(m, L, 0.0), T, passes=1), passes=1)
    UW = mm(T, jnp.concatenate([beta * v, beta * start * k], axis=1), passes=1)
    kend = k * decay.T[:, C - 1:C]
    PUW = mm(qk, UW, passes=1)
    KUW = mm(kend, UW, TN, passes=1)
    M = eye * start[C - 1:C, :] - KUW[:, HD:]
    Qp = start * q - PUW[:, HD:]
    return Qp, M, PUW[:, :HD], KUW[:, :HD]


def rms_scale(values, gain):
    mean_square = jnp.mean(values * values, axis=-1, keepdims=True)
    return values * lax.rsqrt(mean_square + 1e-06) * gain.astype(f32)


class Place:
    def __init__(self):
        e = lax.axis_index("expert")
        self.e = e
        self.z, self.x, self.c = e // 8, (e // 2) % 4, e % 2

    def at(self, zz, dx, cc=0):
        return ((self.z + zz) % 2 * 4 + (self.x + dx) % 4) * 2 + (self.c + cc) % 2

    def pair(self, zz, dx):
        return ((self.z + zz) % 2 * 4 + (self.x + dx) % 4) * 2


class Copies:
    def __init__(self, send, recv, base):
        self.send, self.recv, self.base, self.sent = send, recv, base, []

    def make(self, i, src, dst, peer):
        return pltpu.make_async_remote_copy(
            src_ref=src, dst_ref=dst, send_sem=self.send.at[self.base + i],
            recv_sem=self.recv.at[self.base + i], device_id=peer, device_id_type=MESH)

    def go(self, i, parts):
        self.make(i, *parts()).start()
        self.sent.append((i, parts))

    def arrive(self, i, dst, peer):
        self.make(i, dst, dst, peer).wait_recv()

    def finish(self):
        for i, parts in self.sent:
            self.make(i, *parts()).wait_send()


GATHER_COPIES = 30


class Gather:
    def __init__(self, full, copies, place, width):
        self.full, self.copies, self.place, self.width = full, copies, place, width
        self.half = full.shape[1] // 2

    def ref(self, zz, dx, h, cc=0):
        return self.full.at[self.place.at(zz, dx, cc), pl.ds(h * self.half, self.half), pl.ds(0, self.width)]

    def peer(self, *r):
        return {"expert": self.place.at(*r)}

    def go(self, n, zz, dx, h, to):
        def parts():
            block = self.ref(zz, dx, h)
            return block, block, self.peer(*to)
        self.copies.go(n, parts)

    def swap(self, zz, dx, h):
        self.go(14 + (zz * 4 + dx) * 2 + h, zz, dx, h, (0, 0, 1))

    def take(self, n, zz, dx, h):
        self.copies.arrive(n, self.ref(zz, dx, h), self.peer(0, 1))
        self.swap(zz, dx, h)

    def swapped(self, zz, dx):
        for h in range(2):
            self.copies.arrive(14 + (zz * 4 + dx) * 2 + h, self.ref(zz, dx, h, 1), self.peer(0, 0, 1))

    def plus(self, zz, h):
        self.go(2 + zz * 2 + h, zz, 0, h, (0, 1))

    def minus(self, zz, h):
        self.go(6 + zz * 2 + h, zz, 0, h, (0, 3))

    def begin(self, paced=True):
        self.paced = paced
        for h in range(2):
            if h == 0 or not paced:
                self.go(h, 0, 0, h, (1, 0))
            self.plus(0, h)
            self.minus(0, 1 - h)
        self.swap(0, 0, 0)
        self.swap(0, 0, 1)

    def from_x(self, zz):
        self.take(2 + zz * 2, zz, 3, 0)
        self.go(10 + zz, zz, 3, 0, (0, 1))
        self.take(6 + zz * 2 + 1, zz, 1, 1)
        self.go(12 + zz, zz, 1, 1, (0, 3))
        self.take(2 + zz * 2 + 1, zz, 3, 1)
        self.take(6 + zz * 2, zz, 1, 0)

    def from_z(self, h):
        self.copies.arrive(h, self.ref(1, 0, h), self.peer(0, 1))
        if h == 0 and self.paced:
            self.go(1, 0, 0, 1, (1, 0))
        self.swap(1, 0, h)
        self.plus(1, h)
        self.minus(1, h)

    def from_far(self, zz):
        self.take(10 + zz, zz, 2, 0)
        self.take(12 + zz, zz, 2, 1)


def add_rows(dst, sources, first, count):
    def step(i, _):
        at = pl.ds(pl.multiple_of(first + i * 16, 16), 16)
        total = dst[at, :].astype(f32)
        for source in sources:
            total = total + source[at, :].astype(f32)
        dst[at, :] = total.astype(bf16)
        return 0
    lax.fori_loop(0, count // 16, step, 0)


SEM_TOKENS, SEM_SHARDS, SEM_OUT = 0, GATHER_COPIES, GATHER_COPIES + 19
SEM_HEADS = SEM_OUT + GATHER_COPIES
SEM_ROUTED = SEM_HEADS + 16
SEM_SUMS = SEM_ROUTED + GATHER_COPIES
SEM_ALL = SEM_SUMS + 22


def layer_kernel(tok_ref, docs_ref, ids_ref, gains_ref, pack_ref, conv_ref, rate_ref, hgain_ref,
                 router_ref, ein_ref, eout_ref, out_ref,
                 full, w, win, branch, gate_ref, docc, maps, adds, obuf, heads, mid, y, kin, ap, am, bp, bm, zb,
                 up, down, hid, send, recv, load):
    place = Place()
    fsdp = lax.axis_index("fsdp")
    fy, fz = fsdp // 4, fsdp % 4
    tok, width = tok_ref.shape
    half = tok // 2
    rows = pack_ref.shape[0]
    ff = down.shape[0]
    chunks = 16 * tok // C

    def line(dy, d):
        return (fy + dy) % 4 * 4 + (fz + d) % 4

    barrier = pltpu.get_barrier_semaphore()
    peers = [{"expert": (place.e + i) % 16} for i in range(1, 16)]
    peers += [{"fsdp": line(*r)} for r in ((1, 0), (3, 0), (0, 1), (0, 2), (0, 3))]
    for peer in peers:
        pl.semaphore_signal(barrier, inc=1, device_id=peer, device_id_type=MESH)
    loads = [pltpu.make_async_copy(ein_ref, up, load.at[0]), pltpu.make_async_copy(eout_ref, down, load.at[1])]
    for copy in loads:
        copy.start()
    w[fsdp] = pack_ref[...]
    full[place.e, :, :width] = rms_scale(tok_ref[...].astype(f32), gains_ref[0:1, :]).astype(bf16)
    pl.semaphore_wait(barrier, len(peers))

    tokens = Copies(send, recv, SEM_TOKENS)
    shards = Copies(send, recv, SEM_SHARDS)
    gather = Gather(full, tokens, place, width)

    def shard(dy, d, h=None):
        slot = w.at[line(dy, (4 - d) % 4)]
        return slot if h is None else slot.at[pl.ds(h * (rows // 2), rows // 2)]

    def send_shard(n, at, to):
        def parts():
            ref = shard(*at)
            return ref, ref, {"fsdp": line(*to)}
        shards.go(n, parts)

    def both(d):
        send_shard(3 + d, (0, d), (1, 0))
        send_shard(7 + d, (0, d), (3, 0))

    def along_z(d):
        shards.arrive(d - 1, shard(0, d), {"fsdp": line(0, d)})
        both(d)

    def along_y(d):
        shards.arrive(3 + d, shard(3, d), {"fsdp": line(3, 0)})
        send_shard(11 + d, (3, d, 0), (1, 0))
        shards.arrive(7 + d, shard(1, d), {"fsdp": line(1, 0)})
        send_shard(15 + d, (1, d, 1), (3, 0))

    def far_y(d):
        shards.arrive(11 + d, shard(2, d, 0), {"fsdp": line(3, 0)})
        shards.arrive(15 + d, shard(2, d, 1), {"fsdp": line(1, 0)})

    for d in range(1, 4):
        send_shard(d - 1, (0, 0), (0, d))
    both(0)
    gather.begin()
    win[0:8, :] = jnp.zeros((8, 3 * HD), f32)
    docc[0:8, :] = jnp.full((8, HD), -1.0, f32)

    def spread(c, _):
        at = pl.ds(pl.multiple_of(c * C + 8, 8), C)
        docs = docs_ref[0:1, pl.ds(pl.multiple_of(c * C, C), C)].astype(f32)
        docc[at, :] = jnp.broadcast_to(docs, (C, C)).T
        return 0
    lax.fori_loop(0, chunks, spread, 0)
    for d in range(1, 4):
        along_z(d)
    gather.from_x(0)
    along_y(0)
    gather.from_z(0)
    along_y(1)
    gather.from_z(1)
    along_y(2)
    gather.from_far(0)
    along_y(3)
    for d in range(4):
        far_y(d)
    for f in range(16):
        y[place.e, :, f * HD:(f + 1) * HD] = w[f, :, 5 * HD:]

    def project(zz):
        for dx in range(4):
            gather.swapped(zz, dx)

        def one(dx, _):
            slot = place.pair(zz, dx)
            x = full[pl.ds(slot, 2), :, :width].reshape(2 * tok, width)
            at = pl.ds(pl.multiple_of(slot * tok, 2 * tok), 2 * tok)
            after = pl.ds(pl.multiple_of(slot * tok + 8, 8), 2 * tok)
            r = dg(x, w[:, :, 0:2 * HD].reshape(16 * rows, 2 * HD)).astype(bf16)
            win[after, 0:2 * HD] = r.astype(f32)
            r = dg(x, w[:, :, 2 * HD:4 * HD].reshape(16 * rows, 2 * HD)).astype(bf16)
            win[after, 2 * HD:] = r[:, :HD].astype(f32)
            branch[at, :] = r[:, HD:]
            gate_ref[at, :] = dg(x, w[:, :, 4 * HD:5 * HD].reshape(16 * rows, HD))
            return 0
        lax.fori_loop(0, 4, one, 0)

    project(0)
    convw = conv_ref[...].astype(f32)
    rate = rate_ref[0]
    outs = Copies(send, recv, SEM_OUT)
    spreads = Gather(y, outs, place, width)

    def half_here():
        gather.from_far(1)
        spreads.begin(paced=False)

    events = {
        1: lambda: gather.from_x(1),
        2: half_here,
        3: lambda: project(1),
        4: lambda: spreads.from_x(0),
        5: lambda: spreads.from_far(0),
        6: lambda: spreads.from_z(0),
        7: lambda: spreads.from_z(1),
    }

    def two_chunks(i, _):
        for step, event in events.items():
            pl.when(i == step)(event)
        first = (i + 5 * place.z) % 8 * 2
        for c in (first, first + 1):
            q_map, s_map, q_add, s_add = chunk_maps(c, gate_ref, docs_ref, win, docc, convw, rate)
            maps[c, :C, :] = q_map
            maps[c, C:, :] = s_map
            adds[c, :C, :] = q_add
            adds[c, C:, :] = s_add
        return 0
    lax.fori_loop(0, chunks // 2, two_chunks, 0)
    tokens.finish()

    def head_copy(c):
        return pltpu.make_async_remote_copy(
            src_ref=obuf.at[c], dst_ref=heads.at[:, pl.ds(pl.multiple_of(place.e * HD, HD), HD)],
            send_sem=send.at[SEM_HEADS + c], recv_sem=recv.at[SEM_HEADS + place.e],
            device_id={"expert": c}, device_id_type=MESH)

    hgain = hgain_ref[...].astype(f32)

    def advance(c, S):
        r0 = pl.multiple_of(c * C, C)
        two = mm(maps[c], S) + adds[c]
        o = two[:C, :]
        g = branch[pl.ds(r0, C), :].astype(f32)
        obuf[c] = (rms_scale(o, hgain) * (g * jax.nn.sigmoid(g))).astype(bf16)

        @pl.when(c != place.e)
        def _():
            head_copy(c).start()
        return two[C:, :]
    S = lax.fori_loop(0, chunks // 2, advance, jnp.zeros((HD, HD), f32))
    spreads.from_x(1)
    lax.fori_loop(chunks // 2, chunks, advance, S)
    spreads.from_far(1)
    for zz in range(2):
        for dx in range(4):
            spreads.swapped(zz, dx)
    heads[:, pl.ds(pl.multiple_of(place.e * HD, HD), HD)] = obuf[place.e]

    def head_in(h, _):
        @pl.when(h != place.e)
        def _():
            pltpu.make_async_remote_copy(
                src_ref=obuf.at[h], dst_ref=heads.at[:, pl.ds(pl.multiple_of(h * HD, HD), HD)],
                send_sem=send.at[SEM_HEADS + h], recv_sem=recv.at[SEM_HEADS + h],
                device_id={"expert": h}, device_id_type=MESH).wait_recv()
        return 0
    lax.fori_loop(0, 16, head_in, 0)
    nf, nd = min(256, ff), min(256, width)

    def out_project(j, _):
        cols = pl.ds(pl.multiple_of(j * nd, nd), nd)
        mid[:, cols] = tok_ref[:, cols].astype(f32) + dg(heads[...], y[:, :, cols].reshape(16 * HD, nd))
        return 0
    lax.fori_loop(0, width // nd, out_project, 0)
    moe_in = rms_scale(mid[...], gains_ref[1:2, :]).astype(bf16)
    full[place.e, :, :width] = moe_in
    logits = dg(full[place.e, :, :width], router_ref[...])
    lane = lax.broadcasted_iota(jnp.int32, (tok, HD), 1)
    ids = ids_ref[...]
    picked = lane < 0
    for k in range(ids.shape[1]):
        picked = jnp.logical_or(picked, ids[:, k:k + 1] == lane % EXPERTS)
    raised = jnp.where(picked, jnp.exp(logits), 0.0)
    weights = raised / jnp.sum(jnp.where(lane < EXPERTS, raised, 0.0), axis=1, keepdims=True)
    upper = weights.astype(bf16).astype(f32)
    side = jnp.where(lane < EXPERTS, upper, jnp.where(lane < 2 * EXPERTS, weights - upper, 0.0))
    full[place.e, :, width:] = side.astype(bf16)
    outs.finish()

    routed = Copies(send, recv, SEM_ROUTED)
    sums = Copies(send, recv, SEM_SUMS)
    gather = Gather(full, routed, place, width + HD)
    gather.begin()
    for copy in loads:
        copy.wait()
    plus, minus = (lambda: {"expert": place.at(0, 1)}), (lambda: {"expert": place.at(0, 3)})
    over, twin = (lambda: {"expert": place.at(1, 0)}), (lambda: {"expert": place.at(0, 0, 1)})

    def compute(zz, dx):
        gather.swapped(zz, dx)
        pair = pl.ds(place.pair(zz, dx), 2)
        at = lax.broadcasted_iota(jnp.int32, (2 * tok, HD), 1)
        values = full[pair, :, width:].reshape(2 * tok, HD).astype(f32)
        hit = jnp.logical_or(at == place.e, at == place.e + EXPERTS)
        weight = jnp.sum(jnp.where(hit, values, 0.0), axis=1, keepdims=True)

        def inner(j, _):
            x = full[pair, :, :width].reshape(2 * tok, width)
            g = dg(x, up[:, pl.ds(pl.multiple_of(j * nf, nf), nf)])
            u = dg(x, up[:, pl.ds(pl.multiple_of(ff + j * nf, nf), nf)])
            hid[:, pl.ds(pl.multiple_of(j * nf, nf), nf)] = (g * jax.nn.sigmoid(g) * u).astype(bf16)
            return 0
        lax.fori_loop(0, ff // nf, inner, 0)

        def outer(j, _):
            cols = pl.ds(pl.multiple_of(j * nd, nd), nd)
            out = dg(hid[...], down[:, cols]) * weight
            y[pair, :, cols] = out.astype(bf16).reshape(2, tok, nd)
            return 0
        lax.fori_loop(0, width // nd, outer, 0)
        sums.go(zz * 4 + dx, lambda: (y.at[place.at(zz, dx, 1)], kin.at[zz * 4 + dx], twin()))

    def own(zz, dx):
        return y.at[place.at(zz, dx)]

    def chip_sum(zz, dx):
        sums.arrive(zz * 4 + dx, kin.at[zz * 4 + dx], twin())
        add_rows(own(zz, dx), [kin.at[zz * 4 + dx]], 0, tok)

    low, high = pl.ds(0, half), pl.ds(half, half)

    def far(zz):
        chip_sum(zz, 2)
        sums.go(8 + zz, lambda: (own(zz, 2).at[low], ap.at[zz], plus()))
        sums.go(10 + zz, lambda: (own(zz, 2).at[high], am.at[zz], minus()))

    def near(zz):
        chip_sum(zz, 1)
        sums.go(12 + zz, lambda: (own(zz, 1).at[high], bp.at[zz, high], plus()))
        chip_sum(zz, 3)
        sums.go(14 + zz, lambda: (own(zz, 3).at[low], bm.at[zz, low], minus()))

    def relay(zz):
        sums.arrive(8 + zz, ap.at[zz], minus())
        add_rows(own(zz, 1).at[low], [ap.at[zz]], 0, half)
        sums.go(16 + zz, lambda: (own(zz, 1).at[low], bp.at[zz, low], plus()))
        sums.arrive(10 + zz, am.at[zz], plus())
        add_rows(own(zz, 3).at[high], [am.at[zz]], 0, half)
        sums.go(18 + zz, lambda: (own(zz, 3).at[high], bm.at[zz, high], minus()))

    def settle(zz, h):
        if h == 0:
            sums.arrive(14 + zz, bm.at[zz, low], plus())
            sums.arrive(16 + zz, bp.at[zz, low], minus())
        else:
            sums.arrive(12 + zz, bp.at[zz, high], minus())
            sums.arrive(18 + zz, bm.at[zz, high], plus())

    compute(0, 0)
    gather.from_x(0)
    compute(0, 3)
    gather.from_z(0)
    compute(0, 1)
    gather.from_z(1)
    gather.from_far(0)
    compute(0, 2)
    gather.from_x(1)
    compute(1, 0)
    gather.from_far(1)
    far(0)
    compute(1, 3)
    compute(1, 2)
    far(1)
    compute(1, 1)
    near(1)
    relay(1)
    chip_sum(1, 0)
    for h, part in ((0, low), (1, high)):
        settle(1, h)
        add_rows(own(1, 0), [bp.at[1], bm.at[1]], h * half, half)
        sums.go(20 + h, lambda part=part: (own(1, 0).at[part], zb.at[part], over()))
    near(0)
    relay(0)
    chip_sum(0, 0)
    for h, part in ((0, low), (1, high)):
        settle(0, h)
        sums.arrive(20 + h, zb.at[part], over())

        def last(i, _):
            at = pl.ds(pl.multiple_of(h * half + i * 16, 16), 16)
            total = mid[at, :]
            for source in (own(0, 0), bp.at[0], bm.at[0], zb):
                total = total + source[at, :].astype(f32)
            out_ref[at, :] = total.astype(bf16)
            return 0
        lax.fori_loop(0, half // 16, last, 0)

    def head_out(c, _):
        @pl.when(c != place.e)
        def _():
            head_copy(c).wait_send()
        return 0
    lax.fori_loop(0, chunks, head_out, 0)
    shards.finish()
    routed.finish()
    sums.finish()


def layer_call(tokens, docs, ids, gains, packed, conv, rate, hgain, router, expert_in, expert_out):
    tok, width = tokens.shape
    rows, cols = packed.shape
    ff = expert_out.shape[0]
    seq = 16 * tok
    V, A = pl.BlockSpec(memory_space=pltpu.VMEM), pl.BlockSpec(memory_space=pl.ANY)
    S = pl.BlockSpec(memory_space=pltpu.SMEM)

    def vm(*s):
        return pltpu.VMEM(s, bf16)

    def vf(*s):
        return pltpu.VMEM(s, f32)
    sem = pltpu.SemaphoreType.DMA
    return pl.pallas_call(
        layer_kernel,
        out_shape=jax.ShapeDtypeStruct((tok, width), bf16),
        in_specs=[V, V, V, V, V, V, S, V, V, A, A],
        out_specs=V,
        scratch_shapes=[
            vm(16, tok, width + HD), vm(16, rows, cols), vf(seq + 8, 3 * HD), vm(seq, HD), vf(seq, HD),
            vf(seq + 8, HD), vf(seq // C, 2 * C, HD), vf(seq // C, 2 * C, HD), vm(seq // C, C, HD),
            vm(tok, 16 * HD), vf(tok, width), vm(16, tok, width), vm(8, tok, width),
            vm(2, tok // 2, width), vm(2, tok // 2, width), vm(2, tok, width), vm(2, tok, width), vm(tok, width),
            vm(width, 2 * ff), vm(ff, width), vm(2 * tok, ff), sem((SEM_ALL,)), sem((SEM_ALL,)), sem((2,))],
        compiler_params=pltpu.CompilerParams(collective_id=0, has_side_effects=True,
                                             vmem_limit_bytes=60 * 1024 * 1024),
        name="whole_layer",
    )(tokens, docs, ids, gains, packed, conv, rate, hgain, router, expert_in, expert_out)


def on_device(tokens, doc_ids, route_ids, norm_gain, proj_weight, gating_weight, block_scale,
              conv_weight, decay_rate, head_gain, out_weight, moe_gain, router_weight,
              expert_in, expert_out):
    scale = jnp.repeat(block_scale[0, 0].astype(f32), HD)
    scaled = (proj_weight[:, 0, :].astype(f32) * scale[None, :]).astype(bf16)
    packed = jnp.concatenate(
        [scaled, jnp.pad(gating_weight[:, :, 0], ((0, 0), (0, HD - 2))), out_weight[0]], 1)
    router = jnp.pad(jnp.concatenate([router_weight, router_weight], 1), ((0, 0), (0, HD - 2 * EXPERTS)))
    return layer_call(
        tokens[0], doc_ids, route_ids[0], jnp.stack([norm_gain, moe_gain]), packed,
        conv_weight[0], decay_rate, head_gain.reshape(1, -1), router,
        expert_in[0], expert_out[0])[None]


def solution(mesh):
    placed = (
        P("fsdp", "expert", None),
        P("fsdp", None),
        P("fsdp", "expert", None),
        P(),
        P("fsdp", "expert", None),
        P("fsdp", None, "expert"),
        P("fsdp", "expert", None),
        P("expert", None, None),
        P("expert"),
        P(),
        P("expert", None, "fsdp"),
        P(),
        P(),
        P("expert", None, None),
        P("expert", None, None),
    )
    return jax.shard_map(
        on_device, mesh=mesh, in_specs=placed, out_specs=P("fsdp", "expert", None), check_vma=False
    )
```

```python
import functools

import jax
import jax.numpy as jnp
from jax import lax
from jax.experimental import pallas as pl
from jax.experimental.pallas import tpu as pltpu
from jax.sharding import PartitionSpec as P

HD = 128
C = 128
EXPERTS = 16
PASSES = 3
MESH = pl.DeviceIdType.MESH
f32 = jnp.float32
bf16 = jnp.bfloat16
NN = ((1,), (0,))
NT = ((1,), (1,))
TN = ((0,), (0,))


def split(a):
    hi = a.astype(bf16)
    return hi, (a - hi.astype(f32)).astype(bf16)


def dg(a, b, dims=NN):
    return lax.dot_general(a, b, (dims, ((), ())), preferred_element_type=f32)


def mm(a, b, dims=NN, passes=PASSES):
    if passes == 1:
        return dg(a.astype(bf16), b.astype(bf16), dims)
    ah, al = split(a)
    bh, bl = split(b)
    return dg(ah, bh, dims) + (dg(al, bh, dims) + dg(ah, bl, dims))


def chunk_maps(c, gate_ref, docs_ref, win_ref, docc_ref, convw, rate):
    r0 = pl.multiple_of(c * C, C)
    docw = docc_ref[pl.ds(r0, C + 8), :]
    doc_col = docw[8:, :]
    parts = []
    for g in range(3):
        w = win_ref[pl.ds(r0, C + 8), g * HD:(g + 1) * HD]
        acc = w[8:, :] * convw[0:1, g * HD:(g + 1) * HD]
        for j in range(1, 4):
            keep = docw[8 - j:C + 8 - j, :] == doc_col
            acc = acc + jnp.where(keep, w[8 - j:C + 8 - j, :] * convw[j:j + 1, g * HD:(g + 1) * HD], 0.0)
        parts.append(acc * jax.nn.sigmoid(acc))
    q, k, v = parts
    q = q * (lax.rsqrt(jnp.sum(q * q, axis=1, keepdims=True) + 1e-6) * HD ** -0.5)
    k = k * lax.rsqrt(jnp.sum(k * k, axis=1, keepdims=True) + 1e-6)
    gates = gate_ref[pl.ds(r0, C), :]
    beta = jnp.broadcast_to(jax.nn.sigmoid(gates[:, 0:1]), (C, HD))
    d = gates[:, 1:2]
    sp = jnp.maximum(d, 0.0) + jnp.log1p(jnp.exp(-jnp.abs(d)))
    lg = jnp.broadcast_to(-rate * sp, (C, HD))
    row = lax.broadcasted_iota(jnp.int32, (C, C), 0)
    col = lax.broadcasted_iota(jnp.int32, (C, C), 1)
    low = (row >= col)
    tri = low.astype(bf16)
    h0 = lg.astype(bf16)
    r1 = lg - h0.astype(f32)
    h1 = r1.astype(bf16)
    h2 = (r1 - h1.astype(f32)).astype(bf16)
    cum = dg(tri, h0) + (dg(tri, h1) + dg(tri, h2))
    doc_row = docs_ref[0:1, pl.ds(r0, C)].astype(f32)
    keep = jnp.logical_and(low, doc_col == doc_row)
    gap = cum - cum.T
    decay = jnp.where(keep, jnp.exp(jnp.where(keep, gap, 0.0)), 0.0)
    start = jnp.where(doc_col == docw[7:8, :], jnp.exp(cum), 0.0)
    kk = mm(k, k, NT, passes=1)
    qk = mm(q, k, NT, passes=1) * decay
    L = jnp.where(row > col, beta * kk * decay, 0.0)
    eye = (row == col).astype(f32)
    T = eye - jnp.where((row >> 1) == (col >> 1), L, 0.0)
    for sh in range(1, 7):
        m = jnp.logical_and((row >> (sh + 1)) == (col >> (sh + 1)), (row >> sh) != (col >> sh))
        T = T - mm(T, mm(jnp.where(m, L, 0.0), T, passes=1), passes=1)
    UW = mm(T, jnp.concatenate([beta * v, beta * start * k], axis=1), passes=1)
    kend = k * decay.T[:, C - 1:C]
    PUW = mm(qk, UW, passes=1)
    KUW = mm(kend, UW, TN, passes=1)
    M = eye * start[C - 1:C, :] - KUW[:, HD:]
    Qp = start * q - PUW[:, HD:]
    return Qp, M, PUW[:, :HD], KUW[:, :HD]


def rms_scale(values, gain):
    mean_square = jnp.mean(values * values, axis=-1, keepdims=True)
    return values * lax.rsqrt(mean_square + 1e-06) * gain.astype(f32)


class Place:
    def __init__(self):
        e = lax.axis_index("expert")
        self.e = e
        self.z, self.x, self.c = e // 8, (e // 2) % 4, e % 2

    def at(self, zz, dx, cc=0):
        return ((self.z + zz) % 2 * 4 + (self.x + dx) % 4) * 2 + (self.c + cc) % 2

    def pair(self, zz, dx):
        return ((self.z + zz) % 2 * 4 + (self.x + dx) % 4) * 2


class Copies:
    def __init__(self, send, recv, base):
        self.send, self.recv, self.base, self.sent = send, recv, base, []

    def make(self, i, src, dst, peer):
        return pltpu.make_async_remote_copy(
            src_ref=src, dst_ref=dst, send_sem=self.send.at[self.base + i],
            recv_sem=self.recv.at[self.base + i], device_id=peer, device_id_type=MESH)

    def go(self, i, parts):
        self.make(i, *parts()).start()
        self.sent.append((i, parts))

    def arrive(self, i, dst, peer):
        self.make(i, dst, dst, peer).wait_recv()

    def finish(self):
        for i, parts in self.sent:
            self.make(i, *parts()).wait_send()


GATHER_COPIES = 30


class Gather:
    def __init__(self, full, copies, place, width):
        self.full, self.copies, self.place, self.width = full, copies, place, width
        self.half = full.shape[1] // 2

    def ref(self, zz, dx, h, cc=0):
        return self.full.at[self.place.at(zz, dx, cc), pl.ds(h * self.half, self.half), pl.ds(0, self.width)]

    def peer(self, *r):
        return {"expert": self.place.at(*r)}

    def go(self, n, zz, dx, h, to):
        def parts():
            block = self.ref(zz, dx, h)
            return block, block, self.peer(*to)
        self.copies.go(n, parts)

    def swap(self, zz, dx, h):
        self.go(14 + (zz * 4 + dx) * 2 + h, zz, dx, h, (0, 0, 1))

    def take(self, n, zz, dx, h):
        self.copies.arrive(n, self.ref(zz, dx, h), self.peer(0, 1))
        self.swap(zz, dx, h)

    def swapped(self, zz, dx):
        for h in range(2):
            self.copies.arrive(14 + (zz * 4 + dx) * 2 + h, self.ref(zz, dx, h, 1), self.peer(0, 0, 1))

    def plus(self, zz, h):
        self.go(2 + zz * 2 + h, zz, 0, h, (0, 1))

    def minus(self, zz, h):
        self.go(6 + zz * 2 + h, zz, 0, h, (0, 3))

    def begin(self, paced=True):
        self.paced = paced
        for h in range(2):
            if h == 0 or not paced:
                self.go(h, 0, 0, h, (1, 0))
            self.plus(0, h)
            self.minus(0, 1 - h)
        self.swap(0, 0, 0)
        self.swap(0, 0, 1)

    def from_x(self, zz):
        self.take(2 + zz * 2, zz, 3, 0)
        self.go(10 + zz, zz, 3, 0, (0, 1))
        self.take(6 + zz * 2 + 1, zz, 1, 1)
        self.go(12 + zz, zz, 1, 1, (0, 3))
        self.take(2 + zz * 2 + 1, zz, 3, 1)
        self.take(6 + zz * 2, zz, 1, 0)

    def from_z(self, h):
        self.copies.arrive(h, self.ref(1, 0, h), self.peer(0, 1))
        if h == 0 and self.paced:
            self.go(1, 0, 0, 1, (1, 0))
        self.swap(1, 0, h)
        self.plus(1, h)
        self.minus(1, h)

    def from_far(self, zz):
        self.take(10 + zz, zz, 2, 0)
        self.take(12 + zz, zz, 2, 1)


def add_rows(dst, sources, first, count):
    def step(i, _):
        at = pl.ds(pl.multiple_of(first + i * 16, 16), 16)
        total = dst[at, :].astype(f32)
        for source in sources:
            total = total + source[at, :].astype(f32)
        dst[at, :] = total.astype(bf16)
        return 0
    lax.fori_loop(0, count // 16, step, 0)


SEM_TOKENS, SEM_SHARDS, SEM_OUT = 0, GATHER_COPIES, GATHER_COPIES + 19
SEM_HEADS = SEM_OUT + GATHER_COPIES
SEM_ROUTED = SEM_HEADS + 16
SEM_SUMS = SEM_ROUTED + GATHER_COPIES
SEM_ALL = SEM_SUMS + 22


def layer_kernel(tok_ref, docs_ref, ids_ref, gains_ref, pack_ref, conv_ref, rate_ref, hgain_ref,
                 router_ref, ein_ref, eout_ref, out_ref,
                 full, w, win, branch, gate_ref, docc, maps, adds, obuf, heads, mid, y, kin, ap, am, bp, bm, zb,
                 up, down, hid, send, recv, load):
    place = Place()
    fsdp = lax.axis_index("fsdp")
    fy, fz = fsdp // 4, fsdp % 4
    tok, width = tok_ref.shape
    half = tok // 2
    rows = pack_ref.shape[0]
    ff = down.shape[0]
    chunks = 16 * tok // C

    def line(dy, d):
        return (fy + dy) % 4 * 4 + (fz + d) % 4

    barrier = pltpu.get_barrier_semaphore()
    peers = [{"expert": (place.e + i) % 16} for i in range(1, 16)]
    peers += [{"fsdp": line(*r)} for r in ((1, 0), (3, 0), (0, 1), (0, 2), (0, 3))]
    for peer in peers:
        pl.semaphore_signal(barrier, inc=1, device_id=peer, device_id_type=MESH)
    loads = [pltpu.make_async_copy(ein_ref, up, load.at[0]), pltpu.make_async_copy(eout_ref, down, load.at[1])]
    for copy in loads:
        copy.start()
    w[fsdp] = pack_ref[...]
    full[place.e, :, :width] = rms_scale(tok_ref[...].astype(f32), gains_ref[0:1, :]).astype(bf16)
    pl.semaphore_wait(barrier, len(peers))

    tokens = Copies(send, recv, SEM_TOKENS)
    shards = Copies(send, recv, SEM_SHARDS)
    gather = Gather(full, tokens, place, width)

    def shard(dy, d, h=None):
        slot = w.at[line(dy, (4 - d) % 4)]
        return slot if h is None else slot.at[pl.ds(h * (rows // 2), rows // 2)]

    def send_shard(n, at, to):
        def parts():
            ref = shard(*at)
            return ref, ref, {"fsdp": line(*to)}
        shards.go(n, parts)

    def both(d):
        send_shard(3 + d, (0, d), (1, 0))
        send_shard(7 + d, (0, d), (3, 0))

    def along_z(d):
        shards.arrive(d - 1, shard(0, d), {"fsdp": line(0, d)})
        both(d)

    def along_y(d):
        shards.arrive(3 + d, shard(3, d), {"fsdp": line(3, 0)})
        send_shard(11 + d, (3, d, 0), (1, 0))
        shards.arrive(7 + d, shard(1, d), {"fsdp": line(1, 0)})
        send_shard(15 + d, (1, d, 1), (3, 0))

    def far_y(d):
        shards.arrive(11 + d, shard(2, d, 0), {"fsdp": line(3, 0)})
        shards.arrive(15 + d, shard(2, d, 1), {"fsdp": line(1, 0)})

    for d in range(1, 4):
        send_shard(d - 1, (0, 0), (0, d))
    both(0)
    gather.begin()
    win[0:8, :] = jnp.zeros((8, 3 * HD), f32)
    docc[0:8, :] = jnp.full((8, HD), -1.0, f32)

    def spread(c, _):
        at = pl.ds(pl.multiple_of(c * C + 8, 8), C)
        docs = docs_ref[0:1, pl.ds(pl.multiple_of(c * C, C), C)].astype(f32)
        docc[at, :] = jnp.broadcast_to(docs, (C, C)).T
        return 0
    lax.fori_loop(0, chunks, spread, 0)
    for d in range(1, 4):
        along_z(d)
    gather.from_x(0)
    along_y(0)
    gather.from_z(0)
    along_y(1)
    gather.from_z(1)
    along_y(2)
    gather.from_far(0)
    along_y(3)
    for d in range(4):
        far_y(d)
    for f in range(16):
        y[place.e, :, f * HD:(f + 1) * HD] = w[f, :, 5 * HD:]

    def project(zz):
        for dx in range(4):
            gather.swapped(zz, dx)

        def one(dx, _):
            slot = place.pair(zz, dx)
            x = full[pl.ds(slot, 2), :, :width].reshape(2 * tok, width)
            at = pl.ds(pl.multiple_of(slot * tok, 2 * tok), 2 * tok)
            after = pl.ds(pl.multiple_of(slot * tok + 8, 8), 2 * tok)
            r = dg(x, w[:, :, 0:2 * HD].reshape(16 * rows, 2 * HD)).astype(bf16)
            win[after, 0:2 * HD] = r.astype(f32)
            r = dg(x, w[:, :, 2 * HD:4 * HD].reshape(16 * rows, 2 * HD)).astype(bf16)
            win[after, 2 * HD:] = r[:, :HD].astype(f32)
            branch[at, :] = r[:, HD:]
            gate_ref[at, :] = dg(x, w[:, :, 4 * HD:5 * HD].reshape(16 * rows, HD))
            return 0
        lax.fori_loop(0, 4, one, 0)

    project(0)
    convw = conv_ref[...].astype(f32)
    rate = rate_ref[0]
    outs = Copies(send, recv, SEM_OUT)
    spreads = Gather(y, outs, place, width)

    def half_near():
        gather.from_x(1)
        spreads.begin(paced=False)

    events = {
        1: half_near,
        2: lambda: gather.from_far(1),
        3: lambda: project(1),
        4: lambda: spreads.from_x(0),
        5: lambda: spreads.from_far(0),
        6: lambda: spreads.from_z(0),
        7: lambda: spreads.from_z(1),
    }

    def two_chunks(i, _):
        for step, event in events.items():
            pl.when(i == step)(event)
        first = (i + 5 * place.z) % 8 * 2
        for c in (first, first + 1):
            q_map, s_map, q_add, s_add = chunk_maps(c, gate_ref, docs_ref, win, docc, convw, rate)
            maps[c, :C, :] = q_map
            maps[c, C:, :] = s_map
            adds[c, :C, :] = q_add
            adds[c, C:, :] = s_add
        return 0
    lax.fori_loop(0, chunks // 2, two_chunks, 0)
    tokens.finish()

    def head_copy(c):
        return pltpu.make_async_remote_copy(
            src_ref=obuf.at[c], dst_ref=heads.at[:, pl.ds(pl.multiple_of(place.e * HD, HD), HD)],
            send_sem=send.at[SEM_HEADS + c], recv_sem=recv.at[SEM_HEADS + place.e],
            device_id={"expert": c}, device_id_type=MESH)

    hgain = hgain_ref[...].astype(f32)

    def advance(c, S):
        r0 = pl.multiple_of(c * C, C)
        two = mm(maps[c], S) + adds[c]
        o = two[:C, :]
        g = branch[pl.ds(r0, C), :].astype(f32)
        obuf[c] = (rms_scale(o, hgain) * (g * jax.nn.sigmoid(g))).astype(bf16)

        @pl.when(c != place.e)
        def _():
            head_copy(c).start()
        return two[C:, :]
    S = lax.fori_loop(0, chunks // 2, advance, jnp.zeros((HD, HD), f32))
    spreads.from_x(1)
    lax.fori_loop(chunks // 2, chunks, advance, S)
    spreads.from_far(1)
    for zz in range(2):
        for dx in range(4):
            spreads.swapped(zz, dx)
    heads[:, pl.ds(pl.multiple_of(place.e * HD, HD), HD)] = obuf[place.e]

    def head_in(h, _):
        @pl.when(h != place.e)
        def _():
            pltpu.make_async_remote_copy(
                src_ref=obuf.at[h], dst_ref=heads.at[:, pl.ds(pl.multiple_of(h * HD, HD), HD)],
                send_sem=send.at[SEM_HEADS + h], recv_sem=recv.at[SEM_HEADS + h],
                device_id={"expert": h}, device_id_type=MESH).wait_recv()
        return 0
    lax.fori_loop(0, 16, head_in, 0)
    nf, nd = min(256, ff), min(256, width)

    def out_project(j, _):
        cols = pl.ds(pl.multiple_of(j * nd, nd), nd)
        mid[:, cols] = tok_ref[:, cols].astype(f32) + dg(heads[...], y[:, :, cols].reshape(16 * HD, nd))
        return 0
    lax.fori_loop(0, width // nd, out_project, 0)
    moe_in = rms_scale(mid[...], gains_ref[1:2, :]).astype(bf16)
    full[place.e, :, :width] = moe_in
    logits = dg(full[place.e, :, :width], router_ref[...])
    lane = lax.broadcasted_iota(jnp.int32, (tok, HD), 1)
    ids = ids_ref[...]
    picked = lane < 0
    for k in range(ids.shape[1]):
        picked = jnp.logical_or(picked, ids[:, k:k + 1] == lane % EXPERTS)
    raised = jnp.where(picked, jnp.exp(logits), 0.0)
    weights = raised / jnp.sum(jnp.where(lane < EXPERTS, raised, 0.0), axis=1, keepdims=True)
    upper = weights.astype(bf16).astype(f32)
    side = jnp.where(lane < EXPERTS, upper, jnp.where(lane < 2 * EXPERTS, weights - upper, 0.0))
    full[place.e, :, width:] = side.astype(bf16)
    outs.finish()

    routed = Copies(send, recv, SEM_ROUTED)
    sums = Copies(send, recv, SEM_SUMS)
    gather = Gather(full, routed, place, width + HD)
    gather.begin()
    for copy in loads:
        copy.wait()
    plus, minus = (lambda: {"expert": place.at(0, 1)}), (lambda: {"expert": place.at(0, 3)})
    over, twin = (lambda: {"expert": place.at(1, 0)}), (lambda: {"expert": place.at(0, 0, 1)})

    def compute(zz, dx):
        gather.swapped(zz, dx)
        pair = pl.ds(place.pair(zz, dx), 2)
        at = lax.broadcasted_iota(jnp.int32, (2 * tok, HD), 1)
        values = full[pair, :, width:].reshape(2 * tok, HD).astype(f32)
        hit = jnp.logical_or(at == place.e, at == place.e + EXPERTS)
        weight = jnp.sum(jnp.where(hit, values, 0.0), axis=1, keepdims=True)

        def inner(j, _):
            x = full[pair, :, :width].reshape(2 * tok, width)
            g = dg(x, up[:, pl.ds(pl.multiple_of(j * nf, nf), nf)])
            u = dg(x, up[:, pl.ds(pl.multiple_of(ff + j * nf, nf), nf)])
            hid[:, pl.ds(pl.multiple_of(j * nf, nf), nf)] = (g * jax.nn.sigmoid(g) * u).astype(bf16)
            return 0
        lax.fori_loop(0, ff // nf, inner, 0)

        def outer(j, _):
            cols = pl.ds(pl.multiple_of(j * nd, nd), nd)
            out = dg(hid[...], down[:, cols]) * weight
            y[pair, :, cols] = out.astype(bf16).reshape(2, tok, nd)
            return 0
        lax.fori_loop(0, width // nd, outer, 0)
        sums.go(zz * 4 + dx, lambda: (y.at[place.at(zz, dx, 1)], kin.at[zz * 4 + dx], twin()))

    def own(zz, dx):
        return y.at[place.at(zz, dx)]

    def chip_sum(zz, dx):
        sums.arrive(zz * 4 + dx, kin.at[zz * 4 + dx], twin())
        add_rows(own(zz, dx), [kin.at[zz * 4 + dx]], 0, tok)

    low, high = pl.ds(0, half), pl.ds(half, half)

    def far(zz):
        chip_sum(zz, 2)
        sums.go(8 + zz, lambda: (own(zz, 2).at[low], ap.at[zz], plus()))
        sums.go(10 + zz, lambda: (own(zz, 2).at[high], am.at[zz], minus()))

    def near(zz):
        chip_sum(zz, 1)
        sums.go(12 + zz, lambda: (own(zz, 1).at[high], bp.at[zz, high], plus()))
        chip_sum(zz, 3)
        sums.go(14 + zz, lambda: (own(zz, 3).at[low], bm.at[zz, low], minus()))

    def relay(zz):
        sums.arrive(8 + zz, ap.at[zz], minus())
        add_rows(own(zz, 1).at[low], [ap.at[zz]], 0, half)
        sums.go(16 + zz, lambda: (own(zz, 1).at[low], bp.at[zz, low], plus()))
        sums.arrive(10 + zz, am.at[zz], plus())
        add_rows(own(zz, 3).at[high], [am.at[zz]], 0, half)
        sums.go(18 + zz, lambda: (own(zz, 3).at[high], bm.at[zz, high], minus()))

    def settle(zz, h):
        if h == 0:
            sums.arrive(14 + zz, bm.at[zz, low], plus())
            sums.arrive(16 + zz, bp.at[zz, low], minus())
        else:
            sums.arrive(12 + zz, bp.at[zz, high], minus())
            sums.arrive(18 + zz, bm.at[zz, high], plus())

    compute(0, 0)
    gather.from_x(0)
    compute(0, 3)
    gather.from_z(0)
    compute(0, 1)
    gather.from_z(1)
    gather.from_far(0)
    compute(0, 2)
    gather.from_x(1)
    compute(1, 0)
    gather.from_far(1)
    far(0)
    compute(1, 3)
    compute(1, 2)
    far(1)
    compute(1, 1)
    near(1)
    relay(1)
    chip_sum(1, 0)
    for h, part in ((0, low), (1, high)):
        settle(1, h)
        add_rows(own(1, 0), [bp.at[1], bm.at[1]], h * half, half)
        sums.go(20 + h, lambda part=part: (own(1, 0).at[part], zb.at[part], over()))
    near(0)
    relay(0)
    chip_sum(0, 0)
    for h, part in ((0, low), (1, high)):
        settle(0, h)
        sums.arrive(20 + h, zb.at[part], over())

        def last(i, _):
            at = pl.ds(pl.multiple_of(h * half + i * 16, 16), 16)
            total = mid[at, :]
            for source in (own(0, 0), bp.at[0], bm.at[0], zb):
                total = total + source[at, :].astype(f32)
            out_ref[at, :] = total.astype(bf16)
            return 0
        lax.fori_loop(0, half // 16, last, 0)

    def head_out(c, _):
        @pl.when(c != place.e)
        def _():
            head_copy(c).wait_send()
        return 0
    lax.fori_loop(0, chunks, head_out, 0)
    shards.finish()
    routed.finish()
    sums.finish()


def layer_call(tokens, docs, ids, gains, packed, conv, rate, hgain, router, expert_in, expert_out):
    tok, width = tokens.shape
    rows, cols = packed.shape
    ff = expert_out.shape[0]
    seq = 16 * tok
    V, A = pl.BlockSpec(memory_space=pltpu.VMEM), pl.BlockSpec(memory_space=pl.ANY)
    S = pl.BlockSpec(memory_space=pltpu.SMEM)

    def vm(*s):
        return pltpu.VMEM(s, bf16)

    def vf(*s):
        return pltpu.VMEM(s, f32)
    sem = pltpu.SemaphoreType.DMA
    return pl.pallas_call(
        layer_kernel,
        out_shape=jax.ShapeDtypeStruct((tok, width), bf16),
        in_specs=[V, V, V, V, V, V, S, V, V, A, A],
        out_specs=V,
        scratch_shapes=[
            vm(16, tok, width + HD), vm(16, rows, cols), vf(seq + 8, 3 * HD), vm(seq, HD), vf(seq, HD),
            vf(seq + 8, HD), vf(seq // C, 2 * C, HD), vf(seq // C, 2 * C, HD), vm(seq // C, C, HD),
            vm(tok, 16 * HD), vf(tok, width), vm(16, tok, width), vm(8, tok, width),
            vm(2, tok // 2, width), vm(2, tok // 2, width), vm(2, tok, width), vm(2, tok, width), vm(tok, width),
            vm(width, 2 * ff), vm(ff, width), vm(2 * tok, ff), sem((SEM_ALL,)), sem((SEM_ALL,)), sem((2,))],
        compiler_params=pltpu.CompilerParams(collective_id=0, has_side_effects=True,
                                             vmem_limit_bytes=60 * 1024 * 1024),
        name="whole_layer",
    )(tokens, docs, ids, gains, packed, conv, rate, hgain, router, expert_in, expert_out)


def on_device(tokens, doc_ids, route_ids, norm_gain, proj_weight, gating_weight, block_scale,
              conv_weight, decay_rate, head_gain, out_weight, moe_gain, router_weight,
              expert_in, expert_out):
    scale = jnp.repeat(block_scale[0, 0].astype(f32), HD)
    scaled = (proj_weight[:, 0, :].astype(f32) * scale[None, :]).astype(bf16)
    packed = jnp.concatenate(
        [scaled, jnp.pad(gating_weight[:, :, 0], ((0, 0), (0, HD - 2))), out_weight[0]], 1)
    router = jnp.pad(jnp.concatenate([router_weight, router_weight], 1), ((0, 0), (0, HD - 2 * EXPERTS)))
    return layer_call(
        tokens[0], doc_ids, route_ids[0], jnp.stack([norm_gain, moe_gain]), packed,
        conv_weight[0], decay_rate, head_gain.reshape(1, -1), router,
        expert_in[0], expert_out[0])[None]


def solution(mesh):
    placed = (
        P("fsdp", "expert", None),
        P("fsdp", None),
        P("fsdp", "expert", None),
        P(),
        P("fsdp", "expert", None),
        P("fsdp", None, "expert"),
        P("fsdp", "expert", None),
        P("expert", None, None),
        P("expert"),
        P(),
        P("expert", None, "fsdp"),
        P(),
        P(),
        P("expert", None, None),
        P("expert", None, None),
    )
    return jax.shard_map(
        on_device, mesh=mesh, in_specs=placed, out_specs=P("fsdp", "expert", None), check_vma=False
    )
```
